32 devices in a mesh: req: 16 (over z, y, x), tp: 2 (over core).
Axes of the slice: x: 2, y: 2, z: 4, core: 2. Of those that a mesh axis runs over, the one named last changes fastest.
Arguments:
- tokens: bfloat16 [3072, 1536], P('req', 'tp'), may hold values from -6 to 6
- video_lengths: int32 [5], replicated, may hold values from 1 to 1920, 3072 in all
- timestep: int32 [1], replicated, may hold values from 1 to 1000
- time_weight: float32 [256, 4608], replicated, may hold values from -0.375 to 0.375
- block_mod: float32 [3, 1536], replicated, may hold values from -3 to 3
- w_query: bfloat16 [1536, 1536], P(None, 'tp')
- w_key: bfloat16 [1536, 1536], P(None, 'tp')
- w_value: bfloat16 [1536, 1536], P(None, 'tp'), may hold values from -0.15625 to 0.15625
- w_out: bfloat16 [1536, 1536], P('tp'), may hold values from -0.15625 to 0.15625
Outputs:
- velocity: bfloat16 [3072, 1536], P('req', 'tp')
- stepped: bfloat16 [3072, 1536], P('req', 'tp')
The draws below stay inside these ranges and needn't reach their ends.
Inputs may be any that keep to these rules, and one draw needn't show every extreme that they name: `video_lengths`: the videos' lengths in packing order; they sum to 3072 and the longest has exactly 1920 tokens.
All inputs are finite; a program needn't handle non-finite values.
Results may differ from the reference program's by a relative error of at most 0.017.
Values may be sent and summed in bfloat16 or wider, within the bound.
No kernel may reach another device: no remote copies, remote signals or barrier semaphores. Data moves between devices by JAX's collectives and lax.ppermute only.
A program may use at most 256 MiB of HBM per device.

```python
import math
import jax
import jax.numpy as jnp
import numpy as np
from jax import lax

HEADS = 12
HEAD_DIM = 128
FREQ = 256
D = 1536
VIDEOS = 5
STEPS = 1000
TOKENS = 3072
MOST = 1920


def paired_weights(seed_key):
    first = jax.random.normal(jax.random.fold_in(seed_key, 11), (D, D), jnp.float32)
    second = jax.random.normal(jax.random.fold_in(seed_key, 12), (D, D), jnp.float32)
    factor = 1.7 * D ** (-0.5)
    return (first * factor, second * factor)


def draw_w_query(key, part):
    return paired_weights(key)[0].astype(jnp.bfloat16)


def draw_w_key(key, part):
    return paired_weights(key)[1].astype(jnp.bfloat16)


def block_levels(stream_key, extent, shards, smallest, largest):
    level, own = 1.0, jax.random.fold_in(stream_key, 6)
    for position, parts in shards:
        draws = jnp.exp(jax.random.uniform(jax.random.fold_in(own, position), (parts,), jnp.float32, smallest / len(shards), largest / len(shards)))
        level = level * jnp.repeat(draws, extent[position] // parts).reshape([-1 if axis == position else 1 for axis in range(len(extent))])
    return level


def split_up(number_of, total, most, slope):
    loads = [(1 << 20) // math.isqrt(standing ** slope) + 1 for standing in range(2, number_of + 1)]
    surplus, given = total - most - (number_of - 1), [1] * (number_of - 1)
    while surplus > 0:
        movable = [i for i in range(number_of - 1) if given[i] < most]
        whole, remaining = sum([loads[i] for i in movable]), surplus
        for i in movable:
            extra = min(most - given[i], max(1, remaining * loads[i] // whole), surplus)
            given[i] = given[i] + extra
            surplus = surplus - extra
    return np.array([most] + given)


def ragged(stream_key, number_of, total, bound, skew):
    if number_of == 2:
        one = jax.random.randint(stream_key, (), max(1, total - bound), min(bound, total - 1) + 1)
        return jnp.stack([one, total - one])
    sizes = jnp.asarray(split_up(number_of, total, bound, skew), jnp.int32)
    couples = (number_of - 1) // 2
    donor, taker = sizes[1:1 + 2 * couples:2], sizes[2:2 + 2 * couples:2]
    room = jnp.minimum(donor - 1, bound - taker)
    moved = jax.random.randint(jax.random.fold_in(stream_key, 1), (couples,), 0, 1 << 20) % (room + 1)
    sizes = sizes.at[1:1 + 2 * couples:2].set(donor - moved).at[2:2 + 2 * couples:2].set(taker + moved)
    return sizes[jax.random.permutation(jax.random.fold_in(stream_key, 2), number_of)]


def scatter_about(rng, extent, width, most, shards=(), kind=jnp.bfloat16):
    result = jax.random.normal(rng, extent, jnp.float32) * width
    if len(shards) > 0:
        result = block_levels(rng, extent, shards, -0.22, 0.18) * result
    return jnp.clip(result, min=-most, max=most).astype(kind)


def setup_inputs(seed: int = 0) -> dict:
    arg_keys = jax.random.split(jax.random.key(seed), 10)
    return {
        "tokens": scatter_about(arg_keys[0], (TOKENS, D), 1.0, 6.0, ((0, 16), (1, 2))),
        "video_lengths": ragged(arg_keys[1], VIDEOS, TOKENS, MOST, 2).astype(jnp.int32),
        "timestep": jax.random.randint(arg_keys[2], (1,), 1, STEPS + 1).astype(jnp.int32),
        "time_weight": scatter_about(arg_keys[3], (FREQ, 3 * D), FREQ ** -0.5, 0.375, (), jnp.float32),
        "block_mod": scatter_about(arg_keys[4], (3, D), 0.5, 3.0, (), jnp.float32),
        "w_query": draw_w_query(jax.random.fold_in(arg_keys[9], 71), 0),
        "w_key": draw_w_key(jax.random.fold_in(arg_keys[9], 71), 0),
        "w_value": scatter_about(arg_keys[7], (D, D), D ** -0.5, 0.15625, ((1, 2),)),
        "w_out": scatter_about(arg_keys[8], (D, D), D ** -0.5, 0.15625, ((0, 2),)),
    }


def noise_level(step_value):
    frac = step_value / STEPS
    return 5.0 * frac / (1.0 + 4.0 * frac)

def reference(tokens, video_lengths, timestep, time_weight, block_mod, w_query, w_key, w_value, w_out):
    time_value = timestep[0].astype(jnp.float32)
    sigma = noise_level(time_value)
    delta_sigma = noise_level(time_value - 1.0) - sigma
    half_freq = FREQ // 2
    frequency = jnp.exp(-math.log(10000.0) * jnp.arange(half_freq, dtype=jnp.float32) / half_freq)
    angle = 1000.0 * sigma * frequency
    embedding = jnp.concatenate([jnp.cos(angle), jnp.sin(angle)])
    modulation = jnp.dot(jax.nn.silu(embedding)[None, :], time_weight, precision=lax.Precision.HIGHEST, preferred_element_type=jnp.float32)[0]
    modulation = modulation.reshape(3, D) + block_mod
    shift, scale, gate = (modulation[0], modulation[1], modulation[2])
    residual = tokens.astype(jnp.float32)
    mean = lax.optimization_barrier(jnp.mean(residual, axis=1, keepdims=True))
    centred = residual - mean
    variance = lax.optimization_barrier(jnp.mean(centred * centred, axis=1, keepdims=True))
    normed = (centred * lax.rsqrt(variance + 1e-06) * (1.0 + scale) + shift).astype(jnp.bfloat16)
    query = jnp.dot(normed, w_query, preferred_element_type=jnp.float32).astype(jnp.bfloat16)
    keys = jnp.dot(normed, w_key, preferred_element_type=jnp.float32).astype(jnp.bfloat16)
    values = jnp.dot(normed, w_value, preferred_element_type=jnp.float32).astype(jnp.bfloat16)
    video_ends = jnp.cumsum(video_lengths).astype(jnp.int32)
    token_index = jnp.arange(TOKENS, dtype=jnp.int32)
    video_of = lax.optimization_barrier(jnp.sum((token_index[:, None] >= video_ends[None, :]).astype(jnp.int32), axis=1))
    same_video = video_of[:, None] == video_of[None, :]

    def split_heads(array):
        return jnp.transpose(array.reshape(TOKENS, HEADS, HEAD_DIM), (1, 0, 2))

    def one_head(packed):
        query_head, key_head, value_head = packed
        scores = jnp.dot(query_head, key_head.T, preferred_element_type=jnp.float32) / math.sqrt(HEAD_DIM)
        scores = jnp.where(same_video, scores, -1e+30)
        row_max = lax.optimization_barrier(jnp.max(scores, axis=1, keepdims=True))
        probs = jnp.where(same_video, jnp.exp(scores - row_max), 0.0)
        row_sum = lax.optimization_barrier(jnp.sum(probs, axis=1, keepdims=True))
        weighted = jnp.dot(probs.astype(jnp.bfloat16), value_head, preferred_element_type=jnp.float32)
        return (weighted / row_sum).astype(jnp.bfloat16)
    attended = lax.map(one_head, (split_heads(query), split_heads(keys), split_heads(values)))
    attended = jnp.transpose(attended, (1, 0, 2)).reshape(TOKENS, D)
    projected = jnp.dot(attended, w_out, preferred_element_type=jnp.float32)
    branch = gate * projected
    velocity = branch.astype(jnp.bfloat16)
    stepped = (residual + delta_sigma * branch).astype(jnp.bfloat16)
    return (velocity, stepped)
```

```python
import math

import jax
import jax.numpy as jnp
import numpy as np
from jax import lax
from jax.sharding import PartitionSpec as P

HEAD_DIM = 128
STEPS = 1000


def noise_level(step_value):
    frac = step_value / STEPS
    return 5.0 * frac / (1.0 + 4.0 * frac)


def head_tables(chips, tp, heads_here):
    order = [chip for chip in range(chips) if chip % 4 != 3]
    owner = np.zeros((tp, heads_here), np.int32)
    slot = np.full((tp, chips), -1, np.int32)
    for place in range(tp * heads_here):
        core, head = place % tp, place // tp
        chip = order[(place * len(order)) // (tp * heads_here)]
        owner[core, head] = chip
        slot[core, chip] = head
    return owner, slot


def make(mesh):
    chips, tp = mesh.shape["req"], mesh.shape["tp"]

    def on_device(tokens, video_lengths, timestep, time_weight, block_mod, w_query, w_key, w_value, w_out):
        rows = tokens.shape[0]
        width = time_weight.shape[1] // 3
        heads_here = w_query.shape[1] // HEAD_DIM
        owner, slot = head_tables(chips, tp, heads_here)
        me, core = lax.axis_index("req"), lax.axis_index("tp")
        full_rows = lax.all_gather(tokens, "tp", axis=1, tiled=True)
        time_value = timestep[0].astype(jnp.float32)
        sigma = noise_level(time_value)
        delta_sigma = noise_level(time_value - 1.0) - sigma
        half_freq = time_weight.shape[0] // 2
        frequency = jnp.exp(-math.log(10000.0) * jnp.arange(half_freq, dtype=jnp.float32) / half_freq)
        angle = 1000.0 * sigma * frequency
        embedding = jnp.concatenate([jnp.cos(angle), jnp.sin(angle)])
        modulation = jnp.sum(jax.nn.silu(embedding)[:, None] * time_weight, axis=0)
        modulation = modulation.reshape(3, width) + block_mod
        shift, scale, gate = (modulation[0], modulation[1], modulation[2])
        as_float = full_rows.astype(jnp.float32)
        mean = jnp.mean(as_float, axis=1, keepdims=True)
        centred = as_float - mean
        variance = jnp.mean(centred * centred, axis=1, keepdims=True)
        normed = (centred * lax.rsqrt(variance + 1e-06) * (1.0 + scale) + shift).astype(jnp.bfloat16)

        def project(weight):
            out = jnp.dot(normed, weight, preferred_element_type=jnp.float32).astype(jnp.bfloat16)
            return jnp.transpose(out.reshape(rows, heads_here, HEAD_DIM), (1, 0, 2))

        packed = jnp.stack([project(w) for w in (w_query, w_key, w_value)], axis=1)
        slots = jnp.asarray(slot)[core]
        pieces = []
        for hop in range(chips):
            head = jnp.maximum(slots[me ^ hop], 0)
            piece = lax.dynamic_index_in_dim(packed, head, 0, keepdims=False)
            if hop:
                pairs = [
                    ((chip ^ hop) * tp + c, chip * tp + c)
                    for c in range(tp) for chip in range(chips) if slot[c, chip] >= 0
                ]
                piece = lax.ppermute(piece, ("req", "tp"), pairs)
            pieces.append(piece)
        stacked = jnp.stack(pieces)
        stacked = stacked[jnp.arange(chips) ^ me]
        query, keys, values = (stacked[:, k].reshape(chips * rows, HEAD_DIM) for k in range(3))
        ends = jnp.cumsum(video_lengths)
        index = jnp.arange(chips * rows, dtype=jnp.int32)
        video = jnp.sum((index[:, None] >= ends[None, :]).astype(jnp.int32), axis=1)
        step = chips * rows // 4

        def block(args):
            q, v = args
            scores = jnp.dot(q, keys.T, preferred_element_type=jnp.float32) / math.sqrt(HEAD_DIM)
            same = v[:, None] == video[None, :]
            scores = jnp.where(same, scores, -1e30)
            top = jnp.max(scores, axis=1, keepdims=True)
            probs = jnp.where(same, jnp.exp(scores - top), 0.0)
            total = jnp.sum(probs, axis=1, keepdims=True)
            out = jnp.dot(probs.astype(jnp.bfloat16), values, preferred_element_type=jnp.float32)
            return (out / total).astype(jnp.bfloat16)

        done = lax.map(block, (query.reshape(-1, step, HEAD_DIM), video.reshape(-1, step)))
        done = done.reshape(chips, rows, HEAD_DIM)
        back = []
        for hop in range(chips):
            piece = lax.dynamic_index_in_dim(done, me ^ hop, 0, keepdims=False)
            if hop:
                pairs = [
                    (chip * tp + c, (chip ^ hop) * tp + c)
                    for c in range(tp) for chip in range(chips) if slot[c, chip] >= 0
                ]
                piece = lax.ppermute(piece, ("req", "tp"), pairs)
            back.append(piece)
        back = jnp.stack(back)
        attended = back[jnp.asarray(owner)[core] ^ me]
        attended = jnp.transpose(attended, (1, 0, 2)).reshape(rows, heads_here * HEAD_DIM)
        partial_value = jnp.dot(attended, w_out, preferred_element_type=jnp.float32).astype(jnp.bfloat16)
        share = width // tp
        mine = lax.dynamic_slice_in_dim(partial_value, core * share, share, axis=1)
        other = lax.dynamic_slice_in_dim(partial_value, (1 - core) * share, share, axis=1)
        other = lax.ppermute(other, "tp", [(0, 1), (1, 0)])
        own_sum = mine.astype(jnp.float32) + other.astype(jnp.float32)
        gate_share = lax.dynamic_slice_in_dim(gate, core * share, share)
        branch = gate_share[None, :] * own_sum
        velocity = branch.astype(jnp.bfloat16)
        stepped = (tokens.astype(jnp.float32) + delta_sigma * branch).astype(jnp.bfloat16)
        return (velocity, stepped)

    return on_device


def solution(mesh):
    return jax.shard_map(
        make(mesh),
        mesh=mesh,
        in_specs=(
            P("req", "tp"), P(), P(), P(), P(), P(None, "tp"), P(None, "tp"), P(None, "tp"), P("tp", None),
        ),
        out_specs=(P("req", "tp"), P("req", "tp")),
        check_vma=False,
    )
```

```python
import functools
import math

import jax
import jax.numpy as jnp
from jax import lax
from jax.experimental import pallas as pl
from jax.experimental.pallas import tpu as pltpu
from jax.sharding import PartitionSpec as P

HEAD_DIM = 128
STEPS = 1000
KEY_BLOCK = 512
QUERY_BLOCK = 256
NEG = -1e30
VMEM_LIMIT = 40 * 1024 * 1024


def noise_level(step_value):
    frac = step_value / STEPS
    return 5.0 * frac / (1.0 + 4.0 * frac)


def head_slots(half, heads_here):
    return [slot for slot in range(half) if slot % 4 != 3][:heads_here]


def pairs_out(chips, tp, heads_here, colour):
    half = chips // 2
    slots = head_slots(half, heads_here)
    pairs = []
    for chip in range(chips):
        for core in range(tp):
            slot = (chip % half) ^ colour
            if slot in slots:
                owner = slot + half * (1 - core)
                pairs.append((chip * tp + core, owner * tp + chip // half))
    return pairs


def any_spec():
    return pl.BlockSpec(memory_space=pl.ANY)


def vmem_spec():
    return pl.BlockSpec(memory_space=pltpu.VMEM)


def smem_spec():
    return pl.BlockSpec(memory_space=pltpu.SMEM)


def modulation_kernel(act_ref, weight_ref, block_ref, out_ref):
    row = pl.program_id(0)
    act = jnp.transpose(jnp.broadcast_to(act_ref[...], (8, act_ref.shape[1])))[:, :1]
    total = jnp.sum(act * weight_ref[...], axis=0, keepdims=True)
    out_ref[0] = total + block_ref[pl.ds(row, 1), :]


def modulate(act, time_weight, block_mod):
    freq, wide = time_weight.shape
    width = wide // 3
    return pl.pallas_call(
        modulation_kernel,
        grid=(3,),
        in_specs=[
            pl.BlockSpec((1, freq), lambda i: (0, 0)),
            pl.BlockSpec((freq, width), lambda i: (0, i)),
            pl.BlockSpec((3, width), lambda i: (0, 0)),
        ],
        out_specs=pl.BlockSpec((1, 1, width), lambda i: (i, 0, 0)),
        out_shape=jax.ShapeDtypeStruct((3, 1, width), jnp.float32),
        compiler_params=pltpu.CompilerParams(vmem_limit_bytes=VMEM_LIMIT),
        cost_estimate=pl.CostEstimate(flops=2 * freq * wide, bytes_accessed=4 * freq * wide, transcendentals=0),
    )(act, time_weight, block_mod)


def project_kernel(half, slots, own_ref, other_ref, mod_ref, wq_ref, wk_ref, wv_ref, *rest):
    outs, (full, normed, packed, sems) = rest[:half], rest[half:]
    step = pl.program_id(0)
    share = own_ref.shape[1]
    core = lax.axis_index("tp")
    place = lax.rem(lax.axis_index("req"), half)

    @pl.when(step == 0)
    def _():
        full[:, pl.ds(pl.multiple_of(core * share, 128), share)] = own_ref[...].astype(jnp.float32)
        full[:, pl.ds(pl.multiple_of((1 - core) * share, 128), share)] = other_ref[...].astype(jnp.float32)
        rows = full[...]
        centred = rows - jnp.mean(rows, axis=1, keepdims=True)
        variance = jnp.mean(centred * centred, axis=1, keepdims=True)
        normed[...] = (centred * lax.rsqrt(variance + 1e-06) * (1.0 + mod_ref[1]) + mod_ref[0]).astype(jnp.bfloat16)

    factor = math.log2(math.e) / math.sqrt(HEAD_DIM)
    heads_step = wq_ref.shape[1] // HEAD_DIM
    for part, weight in enumerate((wq_ref, wk_ref, wv_ref)):
        out = jnp.dot(normed[...], weight[...], preferred_element_type=jnp.float32)
        if part == 0:
            out = out * factor
        out = out.astype(jnp.bfloat16)
        for e in range(heads_step):
            packed[step * heads_step + e, part] = out[:, e * HEAD_DIM:(e + 1) * HEAD_DIM]

    def each_copy(head, act):
        for colour in range(half):
            @pl.when((place ^ colour) == slots[head])
            def _():
                act(pltpu.make_async_copy(packed.at[head], outs[colour], sems.at[head]))

    for group in range(len(slots) // heads_step):
        @pl.when(step == group)
        def _():
            for e in range(heads_step):
                each_copy(group * heads_step + e, lambda copy: copy.start())

    @pl.when(step == len(slots) // heads_step - 1)
    def _():
        for head in range(len(slots)):
            each_copy(head, lambda copy: copy.wait())


def project(own, other, mod, w_query, w_key, w_value, half, slots):
    rows, share = own.shape
    depth, columns = w_query.shape
    heads_step = 2 if len(slots) % 2 == 0 else 1
    wide = heads_step * HEAD_DIM
    weight = pl.BlockSpec((depth, wide), lambda i: (0, i))
    piece = jax.ShapeDtypeStruct((3, rows, HEAD_DIM), jnp.bfloat16)
    return pl.pallas_call(
        functools.partial(project_kernel, half, slots),
        grid=(columns // wide,),
        in_specs=[
            pl.BlockSpec((rows, share), lambda i: (0, 0)),
            pl.BlockSpec((rows, share), lambda i: (0, 0)),
            pl.BlockSpec(mod.shape, lambda i: (0, 0, 0)),
            weight, weight, weight,
        ],
        out_specs=[any_spec()] * half,
        out_shape=[piece] * half,
        scratch_shapes=[
            pltpu.VMEM((rows, depth), jnp.float32),
            pltpu.VMEM((rows, depth), jnp.bfloat16),
            pltpu.VMEM((len(slots), 3, rows, HEAD_DIM), jnp.bfloat16),
            pltpu.SemaphoreType.DMA((len(slots),)),
        ],
        compiler_params=pltpu.CompilerParams(vmem_limit_bytes=VMEM_LIMIT),
    )(own, other, mod, w_query, w_key, w_value)


def collect_kernel(*refs):
    pieces, out, sems = refs[:-2], refs[-2], refs[-1]
    copies = [pltpu.make_async_copy(p.at[pl.ds(1, 2)], out.at[k], sems.at[k]) for k, p in enumerate(pieces)]
    for copy in copies:
        copy.start()
    for copy in copies:
        copy.wait()


def collect(pieces):
    _, rows, wide = pieces[0].shape
    return pl.pallas_call(
        collect_kernel,
        in_specs=[any_spec()] * len(pieces),
        out_specs=any_spec(),
        out_shape=jax.ShapeDtypeStruct((len(pieces), 2, rows, wide), jnp.bfloat16),
        scratch_shapes=[pltpu.SemaphoreType.DMA((len(pieces),))],
    )(*pieces)


def attend_kernel(half, slots, lengths_ref, *refs):
    pieces, swapped = refs[:half], refs[half]
    outs = refs[half + 1:2 * half + 1]
    query, keys, values, result, top, total, sems, out_sems = refs[2 * half + 1:]
    rows = pieces[0].shape[1]
    side = lax.axis_index("tp")
    place = lax.rem(lax.axis_index("req"), half)
    active = functools.reduce(jnp.logical_or, [place == slot for slot in slots])

    def at(colour, whole):
        here = (place ^ colour) * rows
        return pl.ds(pl.multiple_of(here if whole is None else here + whole * (half * rows), 64), rows)

    @pl.when(active)
    def _():
        copies = []
        for colour in range(half):
            mine, theirs = at(colour, side), at(colour, 1 - side)
            for source, target in (
                (pieces[colour].at[0], query.at[at(colour, None)]),
                (pieces[colour].at[1], keys.at[mine]),
                (pieces[colour].at[2], values.at[mine, pl.ds(0, HEAD_DIM)]),
                (swapped.at[colour, 0], keys.at[theirs]),
                (swapped.at[colour, 1], values.at[theirs, pl.ds(0, HEAD_DIM)]),
            ):
                copies.append(pltpu.make_async_copy(source, target, sems.at[len(copies)]))
        for copy in copies:
            copy.start()
        values[:, HEAD_DIM:] = jnp.ones((values.shape[0], HEAD_DIM), jnp.bfloat16)
        for copy in copies:
            copy.wait()
        ends, end = [], jnp.int32(0)
        for video in range(lengths_ref.shape[0]):
            end = end + lengths_ref[video]
            ends.append(end)
        starts = [jnp.int32(0)] + ends[:-1]

        def query_block(block, carry):
            local = pl.multiple_of(block * QUERY_BLOCK, QUERY_BLOCK)
            first = side * (half * rows) + local
            last = first + QUERY_BLOCK - 1
            low, high = jnp.int32(0), jnp.int32(0)
            index = first + lax.broadcasted_iota(jnp.int32, (QUERY_BLOCK, 1), 0)
            row_low = jnp.zeros((QUERY_BLOCK, 1), jnp.int32)
            row_high = jnp.zeros((QUERY_BLOCK, 1), jnp.int32)
            for start, stop in zip(starts, ends):
                low = jnp.where(first >= start, start, low)
                high = jnp.where(last >= start, stop, high)
                row_low = jnp.where(index >= start, start, row_low)
                row_high = jnp.where(index >= start, stop, row_high)
            q = query[pl.ds(local, QUERY_BLOCK), :]
            top[...] = jnp.full(top.shape, NEG, jnp.float32)
            total[...] = jnp.zeros(total.shape, jnp.float32)

            def key_block(number, carry):
                begin = pl.multiple_of(number * KEY_BLOCK, KEY_BLOCK)
                score = lax.dot_general(
                    q, keys[pl.ds(begin, KEY_BLOCK), :], (((1,), (1,)), ((), ())), preferred_element_type=jnp.float32
                )
                column = begin + lax.broadcasted_iota(jnp.int32, score.shape, 1)
                score = jnp.where((column >= row_low) & (column < row_high), score, NEG)
                before = top[...]
                now = jnp.maximum(before, jnp.max(score, axis=1, keepdims=True))
                probs = jnp.exp2(score - now).astype(jnp.bfloat16)
                update = jnp.dot(probs, values[pl.ds(begin, KEY_BLOCK), :], preferred_element_type=jnp.float32)
                total[...] = total[...] * jnp.exp2(before - now) + update
                top[...] = now
                return carry

            lax.fori_loop(low // KEY_BLOCK, (high + KEY_BLOCK - 1) // KEY_BLOCK, key_block, 0)
            out = total[:, :HEAD_DIM] / total[:, HEAD_DIM:]
            result[pl.ds(local, QUERY_BLOCK), :] = out.astype(jnp.bfloat16)
            return carry

        lax.fori_loop(0, half * rows // QUERY_BLOCK, query_block, 0)
        copies = [
            pltpu.make_async_copy(result.at[at(colour, None)], outs[colour], out_sems.at[colour])
            for colour in range(half)
        ]
        for copy in copies:
            copy.start()
        for copy in copies:
            copy.wait()


def attend(lengths, pieces, swapped, half, slots):
    rows = pieces[0].shape[1]
    own = half * rows
    piece = jax.ShapeDtypeStruct((rows, HEAD_DIM), jnp.bfloat16)
    return pl.pallas_call(
        functools.partial(attend_kernel, half, slots),
        in_specs=[smem_spec()] + [any_spec()] * (half + 1),
        out_specs=[any_spec()] * half,
        out_shape=[piece] * half,
        scratch_shapes=[
            pltpu.VMEM((own, HEAD_DIM), jnp.bfloat16),
            pltpu.VMEM((2 * own, HEAD_DIM), jnp.bfloat16),
            pltpu.VMEM((2 * own, 2 * HEAD_DIM), jnp.bfloat16),
            pltpu.VMEM((own, HEAD_DIM), jnp.bfloat16),
            pltpu.VMEM((QUERY_BLOCK, 1), jnp.float32),
            pltpu.VMEM((QUERY_BLOCK, 2 * HEAD_DIM), jnp.float32),
            pltpu.SemaphoreType.DMA((5 * half,)),
            pltpu.SemaphoreType.DMA((half,)),
        ],
        compiler_params=pltpu.CompilerParams(vmem_limit_bytes=VMEM_LIMIT),
    )(lengths, *pieces, swapped)


def combine_kernel(half, slots, *refs):
    pieces, weight = refs[:half], refs[half]
    mine, theirs, attended, sems = refs[half + 1:]
    share = mine.shape[1]
    core = lax.axis_index("tp")
    place = lax.rem(lax.axis_index("req"), half)

    def each_copy(act):
        for head, slot in enumerate(slots):
            for colour in range(half):
                @pl.when((place ^ colour) == slot)
                def _():
                    target = attended.at[:, pl.ds(head * HEAD_DIM, HEAD_DIM)]
                    act(pltpu.make_async_copy(pieces[colour], target, sems.at[head]))

    each_copy(lambda copy: copy.start())
    each_copy(lambda copy: copy.wait())
    left = attended[...]
    for out, where in ((theirs, 1 - core), (mine, core)):
        columns = pl.ds(pl.multiple_of(where * share, 128), share)
        out[...] = jnp.dot(left, weight[:, columns], preferred_element_type=jnp.float32).astype(out.dtype)


def combine(pieces, w_out, half, slots):
    rows = pieces[0].shape[0]
    depth, width = w_out.shape
    return pl.pallas_call(
        functools.partial(combine_kernel, half, slots),
        in_specs=[any_spec()] * half + [vmem_spec()],
        out_specs=[vmem_spec(), vmem_spec()],
        out_shape=[
            jax.ShapeDtypeStruct((rows, width // 2), jnp.float32),
            jax.ShapeDtypeStruct((rows, width // 2), jnp.bfloat16),
        ],
        scratch_shapes=[
            pltpu.VMEM((rows, depth), jnp.bfloat16),
            pltpu.SemaphoreType.DMA((len(slots),)),
        ],
        compiler_params=pltpu.CompilerParams(vmem_limit_bytes=VMEM_LIMIT),
    )(*pieces, w_out)


def finish_kernel(timestep_ref, mine, theirs, tokens, mod_ref, velocity, stepped):
    share = tokens.shape[1]
    core = lax.axis_index("tp")
    step_value = jnp.full((1, 128), timestep_ref[0], jnp.int32).astype(jnp.float32)
    delta = (noise_level(step_value - 1.0) - noise_level(step_value))[:, :1]
    gate = mod_ref[2, :, pl.ds(pl.multiple_of(core * share, 128), share)]
    branch = gate * (mine[...] + theirs[...].astype(jnp.float32))
    velocity[...] = branch.astype(jnp.bfloat16)
    stepped[...] = (tokens[...].astype(jnp.float32) + delta * branch).astype(jnp.bfloat16)


def finish(timestep, mine, theirs, tokens, mod):
    shape = jax.ShapeDtypeStruct(tokens.shape, jnp.bfloat16)
    return pl.pallas_call(
        finish_kernel,
        in_specs=[smem_spec()] + [vmem_spec()] * 4,
        out_specs=[vmem_spec(), vmem_spec()],
        out_shape=[shape, shape],
    )(timestep, mine, theirs, tokens, mod)


def make(mesh):
    chips, tp = mesh.shape["req"], mesh.shape["tp"]
    half = chips // 2
    swap = [(0, 1), (1, 0)]

    def on_device(tokens, video_lengths, timestep, time_weight, block_mod, w_query, w_key, w_value, w_out):
        heads_here = w_query.shape[1] // HEAD_DIM
        slots = head_slots(half, heads_here)
        routes = [pairs_out(chips, tp, heads_here, colour) for colour in range(half)]
        other = lax.ppermute(tokens, "tp", swap)
        half_freq = time_weight.shape[0] // 2
        time_value = jnp.broadcast_to(timestep, (half_freq,)).astype(jnp.float32)
        sigma = noise_level(time_value)
        frequency = jnp.exp(-math.log(10000.0) * jnp.arange(half_freq, dtype=jnp.float32) / half_freq)
        angle = 1000.0 * sigma * frequency
        act = jax.nn.silu(jnp.concatenate([jnp.cos(angle), jnp.sin(angle)]))[None, :]
        mod = modulate(act, time_weight, block_mod)
        sent = project(tokens, other, mod, w_query, w_key, w_value, half, slots)
        got = [lax.ppermute(piece, ("req", "tp"), route) for piece, route in zip(sent, routes)]
        swapped = lax.ppermute(collect(got), "tp", swap)
        done = attend(video_lengths, got, swapped, half, slots)
        back = [
            lax.ppermute(piece, ("req", "tp"), [(b, a) for a, b in route]) for piece, route in zip(done, routes)
        ]
        mine, theirs = combine(back, w_out, half, slots)
        theirs = lax.ppermute(theirs, "tp", swap)
        velocity, stepped = finish(timestep, mine, theirs, tokens, mod)
        return (velocity, stepped)

    return on_device


def solution(mesh):
    return jax.shard_map(
        make(mesh),
        mesh=mesh,
        in_specs=(
            P("req", "tp"), P(), P(), P(), P(), P(None, "tp"), P(None, "tp"), P(None, "tp"), P("tp", None),
        ),
        out_specs=(P("req", "tp"), P("req", "tp")),
        check_vma=False,
    )
```

```python
import functools
import math

import jax
import jax.numpy as jnp
from jax import lax
from jax.experimental import pallas as pl
from jax.experimental.pallas import tpu as pltpu
from jax.sharding import PartitionSpec as P

HEAD_DIM = 128
STEPS = 1000
KEY_BLOCK = 512
QUERY_BLOCK = 512
NEG = -1e30
STREAM_LIMIT = 60 * 1024 * 1024
VMEM_LIMIT = 32 * 1024 * 1024


def noise_level(step_value):
    frac = step_value / STEPS
    return 5.0 * frac / (1.0 + 4.0 * frac)


def head_slots(half, heads_here):
    return [slot for slot in range(half) if slot % 4 != 3][:heads_here]


def pairs_out(chips, tp, heads_here, colour):
    half = chips // 2
    slots = head_slots(half, heads_here)
    pairs = []
    for chip in range(chips):
        for core in range(tp):
            slot = (chip % half) ^ colour
            source, target = chip * tp + core, (slot + half * core) * tp + chip // half
            if slot in slots and source != target:
                pairs.append((source, target))
    return pairs


def is_own(half):
    return lax.axis_index("req") // half == lax.axis_index("tp")


def any_spec():
    return pl.BlockSpec(memory_space=pl.ANY)


def vmem_spec():
    return pl.BlockSpec(memory_space=pltpu.VMEM)


def smem_spec():
    return pl.BlockSpec(memory_space=pltpu.SMEM)


def modulation_kernel(act_ref, weight_ref, block_ref, out_ref):
    row = pl.program_id(0)
    act = jnp.transpose(jnp.broadcast_to(act_ref[...], (8, act_ref.shape[1])))[:, :1]
    total = jnp.sum(act * weight_ref[...], axis=0, keepdims=True)
    out_ref[0] = total + block_ref[pl.ds(row, 1), :]


def modulate(act, time_weight, block_mod):
    freq, wide = time_weight.shape
    width = wide // 3
    return pl.pallas_call(
        modulation_kernel,
        grid=(3,),
        in_specs=[
            pl.BlockSpec((1, freq), lambda i: (0, 0)),
            pl.BlockSpec((freq, width), lambda i: (0, i)),
            pl.BlockSpec((3, width), lambda i: (0, 0)),
        ],
        out_specs=pl.BlockSpec((1, 1, width), lambda i: (i, 0, 0)),
        out_shape=jax.ShapeDtypeStruct((3, 1, width), jnp.float32),
        compiler_params=pltpu.CompilerParams(vmem_limit_bytes=STREAM_LIMIT),
        cost_estimate=pl.CostEstimate(flops=2 * freq * wide, bytes_accessed=4 * freq * wide, transcendentals=0),
    )(act, time_weight, block_mod)


def project_kernel(half, slots, own_ref, other_ref, mod_ref, wq_ref, wk_ref, wv_ref, *rest):
    outs, (full, normed, packed, sems) = rest[:half], rest[half:]
    step = pl.program_id(0)
    share = own_ref.shape[1]
    core = lax.axis_index("tp")
    place = lax.rem(lax.axis_index("req"), half)

    @pl.when(step == 0)
    def _():
        full[:, pl.ds(pl.multiple_of(core * share, 128), share)] = own_ref[...].astype(jnp.float32)
        full[:, pl.ds(pl.multiple_of((1 - core) * share, 128), share)] = other_ref[...].astype(jnp.float32)
        rows = full[...]
        centred = rows - jnp.mean(rows, axis=1, keepdims=True)
        variance = jnp.mean(centred * centred, axis=1, keepdims=True)
        normed[...] = (centred * lax.rsqrt(variance + 1e-06) * (1.0 + mod_ref[1]) + mod_ref[0]).astype(jnp.bfloat16)

    factor = math.log2(math.e) / math.sqrt(HEAD_DIM)
    heads_step = wq_ref.shape[1] // HEAD_DIM
    for part, weight in enumerate((wq_ref, wk_ref, wv_ref)):
        out = jnp.dot(normed[...], weight[...], preferred_element_type=jnp.float32)
        if part == 0:
            out = out * factor
        out = out.astype(jnp.bfloat16)
        for e in range(heads_step):
            packed[step * heads_step + e, part] = out[:, e * HEAD_DIM:(e + 1) * HEAD_DIM]

    def each_copy(head, act):
        for colour in range(half):
            @pl.when((place ^ colour) == slots[head])
            def _():
                act(pltpu.make_async_copy(packed.at[head], outs[colour], sems.at[head]))

    for group in range(len(slots) // heads_step):
        @pl.when(step == group)
        def _():
            for e in range(heads_step):
                each_copy(group * heads_step + e, lambda copy: copy.start())

    @pl.when(step == len(slots) // heads_step - 1)
    def _():
        for head in range(len(slots)):
            each_copy(head, lambda copy: copy.wait())


def project(own, other, mod, w_query, w_key, w_value, half, slots):
    rows, share = own.shape
    depth, columns = w_query.shape
    heads_step = 2 if len(slots) % 2 == 0 else 1
    wide = heads_step * HEAD_DIM
    weight = pl.BlockSpec((depth, wide), lambda i: (0, i))
    piece = jax.ShapeDtypeStruct((3, rows, HEAD_DIM), jnp.bfloat16)
    return pl.pallas_call(
        functools.partial(project_kernel, half, slots),
        grid=(columns // wide,),
        in_specs=[
            pl.BlockSpec((rows, share), lambda i: (0, 0)),
            pl.BlockSpec((rows, share), lambda i: (0, 0)),
            pl.BlockSpec(mod.shape, lambda i: (0, 0, 0)),
            weight, weight, weight,
        ],
        out_specs=[any_spec()] * half,
        out_shape=[piece] * half,
        scratch_shapes=[
            pltpu.VMEM((rows, depth), jnp.float32),
            pltpu.VMEM((rows, depth), jnp.bfloat16),
            pltpu.VMEM((len(slots), 3, rows, HEAD_DIM), jnp.bfloat16),
            pltpu.SemaphoreType.DMA((len(slots),)),
        ],
        compiler_params=pltpu.CompilerParams(vmem_limit_bytes=STREAM_LIMIT),
    )(own, other, mod, w_query, w_key, w_value)


def collect_kernel(half, sent_ref, *refs):
    pieces, out, sems = refs[:half], refs[half], refs[half + 1]
    own = is_own(half)

    def each_copy(act):
        for colour, piece in enumerate(pieces):
            copy = pltpu.make_async_copy(piece.at[pl.ds(1, 2)], out.at[colour], sems.at[colour])
            if colour:
                act(copy)
            else:
                pl.when(jnp.logical_not(own))(functools.partial(act, copy))
                local = pltpu.make_async_copy(sent_ref.at[pl.ds(1, 2)], out.at[colour], sems.at[colour])
                pl.when(own)(functools.partial(act, local))

    each_copy(lambda copy: copy.start())
    each_copy(lambda copy: copy.wait())


def collect(sent, pieces, half):
    _, rows, wide = sent.shape
    return pl.pallas_call(
        functools.partial(collect_kernel, half),
        in_specs=[any_spec()] * (half + 1),
        out_specs=any_spec(),
        out_shape=jax.ShapeDtypeStruct((half, 2, rows, wide), jnp.bfloat16),
        scratch_shapes=[pltpu.SemaphoreType.DMA((half,))],
        compiler_params=pltpu.CompilerParams(vmem_limit_bytes=VMEM_LIMIT),
    )(sent, *pieces)


def attend_kernel(half, slots, lengths_ref, sent_ref, *refs):
    pieces, swapped = refs[:half], refs[half]
    outs = refs[half + 1:2 * half + 1]
    query, keys, values, result, top, total, sems, out_sems = refs[2 * half + 1:]
    rows = pieces[0].shape[1]
    side = lax.axis_index("tp")
    place = lax.rem(lax.axis_index("req"), half)
    own = is_own(half)
    active = functools.reduce(jnp.logical_or, [place == slot for slot in slots])
    front = pl.ds(0, HEAD_DIM)

    def at(colour, which):
        return pl.ds(pl.multiple_of((place ^ colour) * rows + which * (half * rows), 64), rows)

    def each_copy(act):
        for colour in range(half):
            def load(piece, colour=colour):
                for part, target in enumerate((
                    query.at[at(colour, 0), front],
                    keys.at[at(colour, side), front],
                    values.at[at(colour, side), front],
                )):
                    act(pltpu.make_async_copy(piece.at[part], target, sems.at[5 * colour + part]))

            if colour:
                load(pieces[colour])
            else:
                pl.when(jnp.logical_not(own))(functools.partial(load, pieces[0]))
                pl.when(own)(functools.partial(load, sent_ref))
            for part, target in enumerate((keys, values)):
                target = target.at[at(colour, 1 - side), front]
                act(pltpu.make_async_copy(swapped.at[colour, part], target, sems.at[5 * colour + 3 + part]))

    @pl.when(active)
    def _():
        each_copy(lambda copy: copy.start())
        ends, end = [], jnp.int32(0)
        for video in range(lengths_ref.shape[0]):
            end = end + lengths_ref[video]
            ends.append(end)
        starts = [jnp.int32(0)] + ends[:-1]
        lane = lax.broadcasted_iota(jnp.int32, (1, HEAD_DIM), 1)
        lane_start = jnp.zeros((1, HEAD_DIM), jnp.int32)
        lane_stop = jnp.zeros((1, HEAD_DIM), jnp.int32)
        for video, (start, stop) in enumerate(zip(starts, ends)):
            lane_start = jnp.where(lane == video, start, lane_start)
            lane_stop = jnp.where(lane == video, stop, lane_stop)

        def inside(first, count):
            index = first + lax.broadcasted_iota(jnp.int32, (count, HEAD_DIM), 0)
            return (index >= lane_start) & (index < lane_stop)

        def fill_query(block, carry):
            local = pl.multiple_of(block * QUERY_BLOCK, QUERY_BLOCK)
            member = inside(side * (half * rows) + local, QUERY_BLOCK)
            query[pl.ds(local, QUERY_BLOCK), HEAD_DIM:] = jnp.where(member, 1.0, 0.0).astype(jnp.bfloat16)
            return carry

        def fill_keys(block, carry):
            begin = pl.multiple_of(block * KEY_BLOCK, KEY_BLOCK)
            keys[pl.ds(begin, KEY_BLOCK), HEAD_DIM:] = jnp.where(
                inside(begin, KEY_BLOCK) | (lane >= lengths_ref.shape[0]), 0.0, NEG
            ).astype(jnp.bfloat16)
            values[pl.ds(begin, KEY_BLOCK), HEAD_DIM:] = jnp.ones((KEY_BLOCK, HEAD_DIM), jnp.bfloat16)
            return carry

        lax.fori_loop(0, half * rows // QUERY_BLOCK, fill_query, 0)
        lax.fori_loop(0, 2 * half * rows // KEY_BLOCK, fill_keys, 0)
        each_copy(lambda copy: copy.wait())

        def query_block(block, carry):
            local = pl.multiple_of(block * QUERY_BLOCK, QUERY_BLOCK)
            first = side * (half * rows) + local
            last = first + QUERY_BLOCK - 1
            low, high = jnp.int32(0), jnp.int32(0)
            for start, stop in zip(starts, ends):
                low = jnp.where(first >= start, start, low)
                high = jnp.where(last >= start, stop, high)
            q = query[pl.ds(local, QUERY_BLOCK), :]
            top[...] = jnp.full(top.shape, 2 * NEG, jnp.float32)
            total[...] = jnp.zeros(total.shape, jnp.float32)

            def key_block(number, carry):
                begin = pl.multiple_of(number * KEY_BLOCK, KEY_BLOCK)
                score = lax.dot_general(
                    q, keys[pl.ds(begin, KEY_BLOCK), :], (((1,), (1,)), ((), ())), preferred_element_type=jnp.float32
                )
                tiles = [score[:, k:k + HEAD_DIM] for k in range(0, KEY_BLOCK, HEAD_DIM)]
                most = jnp.max(functools.reduce(jnp.maximum, tiles), axis=1, keepdims=True)
                before = top[...]
                now = jnp.maximum(before, most)
                probs = jnp.concatenate([jnp.exp2(tile - now).astype(jnp.bfloat16) for tile in tiles], axis=1)
                update = jnp.dot(probs, values[pl.ds(begin, KEY_BLOCK), :], preferred_element_type=jnp.float32)
                shrink = jnp.exp2(before - now)
                total[:, :HEAD_DIM] = total[:, :HEAD_DIM] * shrink + update[:, :HEAD_DIM]
                total[:, HEAD_DIM:] = total[:, HEAD_DIM:] * shrink + update[:, HEAD_DIM:]
                top[...] = now
                return carry

            lax.fori_loop(low // KEY_BLOCK, (high + KEY_BLOCK - 1) // KEY_BLOCK, key_block, 0)
            out = total[:, :HEAD_DIM] / total[:, HEAD_DIM:]
            result[pl.ds(local, QUERY_BLOCK), :] = out.astype(jnp.bfloat16)
            return carry

        lax.fori_loop(0, half * rows // QUERY_BLOCK, query_block, 0)
        copies = [
            pltpu.make_async_copy(result.at[at(colour, 0)], outs[colour], out_sems.at[colour])
            for colour in range(half)
        ]
        for copy in copies:
            copy.start()
        for copy in copies:
            copy.wait()


def attend(lengths, sent, pieces, swapped, half, slots):
    rows = sent.shape[1]
    own = half * rows
    piece = jax.ShapeDtypeStruct((rows, HEAD_DIM), jnp.bfloat16)
    return pl.pallas_call(
        functools.partial(attend_kernel, half, slots),
        in_specs=[smem_spec()] + [any_spec()] * (half + 2),
        out_specs=[any_spec()] * half,
        out_shape=[piece] * half,
        scratch_shapes=[
            pltpu.VMEM((own, 2 * HEAD_DIM), jnp.bfloat16),
            pltpu.VMEM((2 * own, 2 * HEAD_DIM), jnp.bfloat16),
            pltpu.VMEM((2 * own, 2 * HEAD_DIM), jnp.bfloat16),
            pltpu.VMEM((own, HEAD_DIM), jnp.bfloat16),
            pltpu.VMEM((QUERY_BLOCK, HEAD_DIM), jnp.float32),
            pltpu.VMEM((QUERY_BLOCK, 2 * HEAD_DIM), jnp.float32),
            pltpu.SemaphoreType.DMA((5 * half,)),
            pltpu.SemaphoreType.DMA((half,)),
        ],
        compiler_params=pltpu.CompilerParams(vmem_limit_bytes=VMEM_LIMIT),
    )(lengths, sent, *pieces, swapped)


def combine_kernel(half, slots, done_ref, *refs):
    pieces, weight = refs[:half], refs[half]
    own = is_own(half)
    mine, theirs, attended, sems = refs[half + 1:]
    share = mine.shape[1]
    core = lax.axis_index("tp")
    place = lax.rem(lax.axis_index("req"), half)

    def each_copy(act):
        for head, slot in enumerate(slots):
            for colour in range(half):
                @pl.when((place ^ colour) == slot)
                def _():
                    target = attended.at[:, pl.ds(head * HEAD_DIM, HEAD_DIM)]
                    copy = pltpu.make_async_copy(pieces[colour], target, sems.at[head])
                    if colour:
                        act(copy)
                    else:
                        pl.when(jnp.logical_not(own))(functools.partial(act, copy))
                        local = pltpu.make_async_copy(done_ref, target, sems.at[head])
                        pl.when(own)(functools.partial(act, local))

    each_copy(lambda copy: copy.start())
    each_copy(lambda copy: copy.wait())
    left = attended[...]
    for out, where in ((theirs, 1 - core), (mine, core)):
        columns = pl.ds(pl.multiple_of(where * share, 128), share)
        out[...] = jnp.dot(left, weight[:, columns], preferred_element_type=jnp.float32).astype(out.dtype)


def combine(done, pieces, w_out, half, slots):
    rows = done.shape[0]
    depth, width = w_out.shape
    return pl.pallas_call(
        functools.partial(combine_kernel, half, slots),
        in_specs=[any_spec()] * (half + 1) + [vmem_spec()],
        out_specs=[vmem_spec(), vmem_spec()],
        out_shape=[
            jax.ShapeDtypeStruct((rows, width // 2), jnp.float32),
            jax.ShapeDtypeStruct((rows, width // 2), jnp.bfloat16),
        ],
        scratch_shapes=[
            pltpu.VMEM((rows, depth), jnp.bfloat16),
            pltpu.SemaphoreType.DMA((len(slots),)),
        ],
        compiler_params=pltpu.CompilerParams(vmem_limit_bytes=VMEM_LIMIT),
    )(done, *pieces, w_out)


def finish_kernel(timestep_ref, mine, theirs, tokens, mod_ref, velocity, stepped):
    share = tokens.shape[1]
    core = lax.axis_index("tp")
    step_value = jnp.full((1, 128), timestep_ref[0], jnp.int32).astype(jnp.float32)
    delta = (noise_level(step_value - 1.0) - noise_level(step_value))[:, :1]
    gate = mod_ref[2, :, pl.ds(pl.multiple_of(core * share, 128), share)]
    branch = gate * (mine[...] + theirs[...].astype(jnp.float32))
    velocity[...] = branch.astype(jnp.bfloat16)
    stepped[...] = (tokens[...].astype(jnp.float32) + delta * branch).astype(jnp.bfloat16)


def finish(timestep, mine, theirs, tokens, mod):
    shape = jax.ShapeDtypeStruct(tokens.shape, jnp.bfloat16)
    return pl.pallas_call(
        finish_kernel,
        in_specs=[smem_spec()] + [vmem_spec()] * 4,
        out_specs=[vmem_spec(), vmem_spec()],
        out_shape=[shape, shape],
        compiler_params=pltpu.CompilerParams(vmem_limit_bytes=VMEM_LIMIT),
    )(timestep, mine, theirs, tokens, mod)


def make(mesh):
    chips, tp = mesh.shape["req"], mesh.shape["tp"]
    half = chips // 2
    swap = [(0, 1), (1, 0)]

    def on_device(tokens, video_lengths, timestep, time_weight, block_mod, w_query, w_key, w_value, w_out):
        heads_here = w_query.shape[1] // HEAD_DIM
        slots = head_slots(half, heads_here)
        routes = [pairs_out(chips, tp, heads_here, colour) for colour in range(half)]
        other = lax.ppermute(tokens, "tp", swap)
        half_freq = time_weight.shape[0] // 2
        time_value = jnp.broadcast_to(timestep, (half_freq,)).astype(jnp.float32)
        sigma = noise_level(time_value)
        frequency = jnp.exp(-math.log(10000.0) * jnp.arange(half_freq, dtype=jnp.float32) / half_freq)
        angle = 1000.0 * sigma * frequency
        act = jax.nn.silu(jnp.concatenate([jnp.cos(angle), jnp.sin(angle)]))[None, :]
        mod = modulate(act, time_weight, block_mod)
        sent = project(tokens, other, mod, w_query, w_key, w_value, half, slots)
        got = [lax.ppermute(piece, ("req", "tp"), route) for piece, route in zip(sent, routes)]
        swapped = lax.ppermute(collect(sent[0], got, half), "tp", swap)
        done = attend(video_lengths, sent[0], got, swapped, half, slots)
        back = [
            lax.ppermute(piece, ("req", "tp"), [(b, a) for a, b in route]) for piece, route in zip(done, routes)
        ]
        mine, theirs = combine(done[0], back, w_out, half, slots)
        theirs = lax.ppermute(theirs, "tp", swap)
        velocity, stepped = finish(timestep, mine, theirs, tokens, mod)
        return (velocity, stepped)

    return on_device


def solution(mesh):
    return jax.shard_map(
        make(mesh),
        mesh=mesh,
        in_specs=(
            P("req", "tp"), P(), P(), P(), P(), P(None, "tp"), P(None, "tp"), P(None, "tp"), P("tp", None),
        ),
        out_specs=(P("req", "tp"), P("req", "tp")),
        check_vma=False,
    )
```

```python
import functools
import math

import jax
import jax.numpy as jnp
from jax import lax
from jax.experimental import pallas as pl
from jax.experimental.pallas import tpu as pltpu
from jax.sharding import PartitionSpec as P

HEAD_DIM = 128
STEPS = 1000
KEY_CHIPS = 4
QUERY_CHIPS = 4
NEG = -1e30
STREAM_LIMIT = 56 * 1024 * 1024
VMEM_LIMIT = 32 * 1024 * 1024


def noise_level(step_value):
    frac = step_value / STEPS
    return 5.0 * frac / (1.0 + 4.0 * frac)


def owners(chips, tp, heads_here):
    order = [chip for chip in range(chips) if chip % 4 != 3]
    return [[order[head * tp + core] for head in range(heads_here)] for core in range(tp)]


def owner_of(table, core, head):
    return jnp.where(core == 0, table[0][head], table[1][head])


def any_spec():
    return pl.BlockSpec(memory_space=pl.ANY)


def vmem_spec():
    return pl.BlockSpec(memory_space=pltpu.VMEM)


def smem_spec():
    return pl.BlockSpec(memory_space=pltpu.SMEM)


def modulation_kernel(act_ref, weight_ref, block_ref, out_ref, weight, sems):
    freq, width = weight.shape[0], block_ref.shape[1]
    parts = sems.shape[0]
    rows = freq // parts
    copies = []
    for part in range(parts):
        here = pl.ds(part * rows, rows)
        copies.append(pltpu.make_async_copy(weight_ref.at[here], weight.at[here], sems.at[part]))
        copies[-1].start()
    act = jnp.transpose(jnp.broadcast_to(act_ref[...], (8, freq)))[:, :1]
    for part in range(parts):
        copies[part].wait()
        here = slice(part * rows, (part + 1) * rows)
        for k in range(3):
            columns = slice(k * width, (k + 1) * width)
            term = jnp.sum(act[here] * weight[here, columns], axis=0, keepdims=True)
            out_ref[k] = term + (out_ref[k] if part else block_ref[k:k + 1, :])


def modulate(act, time_weight, block_mod):
    freq, wide = time_weight.shape
    width = wide // 3
    return pl.pallas_call(
        modulation_kernel,
        in_specs=[vmem_spec(), any_spec(), vmem_spec()],
        out_specs=vmem_spec(),
        out_shape=jax.ShapeDtypeStruct((3, 1, width), jnp.float32),
        scratch_shapes=[pltpu.VMEM((freq, wide), jnp.float32), pltpu.SemaphoreType.DMA((8,))],
        compiler_params=pltpu.CompilerParams(vmem_limit_bytes=STREAM_LIMIT),
        cost_estimate=pl.CostEstimate(flops=2 * freq * wide, bytes_accessed=4 * freq * wide, transcendentals=0),
    )(act, time_weight, block_mod)


def project_kernel(table, own_ref, other_ref, mod_ref, wq_ref, wk_ref, wv_ref, *rest):
    near_ref, far_ref, weights, full, normed, packed, sems, out_sems = rest
    depth, columns = wq_ref.shape
    rows, share = own_ref.shape
    wide = 2 * HEAD_DIM
    part_rows = rows // 2
    core = lax.axis_index("tp")
    loads = {}
    for group in range(columns // wide):
        for part, ref in enumerate((wq_ref, wk_ref, wv_ref)):
            here = pl.ds(group * wide, wide)
            loads[group, part] = pltpu.make_async_copy(
                ref.at[:, here], weights.at[part, :, here], sems.at[3 * group + part]
            )
            loads[group, part].start()
    full[:, pl.ds(pl.multiple_of(core * share, 128), share)] = own_ref[...].astype(jnp.float32)
    full[:, pl.ds(pl.multiple_of((1 - core) * share, 128), share)] = other_ref[...].astype(jnp.float32)
    whole = full[...]
    centred = whole - jnp.mean(whole, axis=1, keepdims=True)
    variance = jnp.mean(centred * centred, axis=1, keepdims=True)
    normed[...] = (centred * lax.rsqrt(variance + 1e-06) * (1.0 + mod_ref[1]) + mod_ref[0]).astype(jnp.bfloat16)
    factor = math.log2(math.e) / math.sqrt(HEAD_DIM)
    near, far = (pl.ds(pl.multiple_of(side * part_rows, 32), part_rows) for side in (core, 1 - core))
    copies = []
    for group in range(columns // wide):
        for part in range(3):
            loads[group, part].wait()
            out = jnp.dot(
                normed[...], weights[part, :, group * wide:(group + 1) * wide], preferred_element_type=jnp.float32
            )
            if part == 0:
                out = out * factor
            for e in range(2):
                packed[2 * group + e, part] = out[:, e * HEAD_DIM:(e + 1) * HEAD_DIM].astype(jnp.bfloat16)
        for head in (2 * group, 2 * group + 1):
            for source, target in (
                (near, near_ref.at[owner_of(table, core, head)]), (far, far_ref.at[head]),
            ):
                copies.append(
                    pltpu.make_async_copy(packed.at[head, :, source], target, out_sems.at[len(copies)])
                )
                copies[-1].start()
    for copy in copies:
        copy.wait()


def project(own, other, mod, w_query, w_key, w_value, chips, table):
    rows, share = own.shape
    depth, columns = w_query.shape
    heads_here = columns // HEAD_DIM
    return pl.pallas_call(
        functools.partial(project_kernel, table),
        in_specs=[vmem_spec()] * 3 + [any_spec()] * 3,
        out_specs=[any_spec()] * 2,
        out_shape=[
            jax.ShapeDtypeStruct((chips, 3, rows // 2, HEAD_DIM), jnp.bfloat16),
            jax.ShapeDtypeStruct((heads_here, 3, rows // 2, HEAD_DIM), jnp.bfloat16),
        ],
        scratch_shapes=[
            pltpu.VMEM((3, depth, columns), jnp.bfloat16),
            pltpu.VMEM((rows, depth), jnp.float32),
            pltpu.VMEM((rows, depth), jnp.bfloat16),
            pltpu.VMEM((heads_here, 3, rows, HEAD_DIM), jnp.bfloat16),
            pltpu.SemaphoreType.DMA((3 * heads_here // 2,)),
            pltpu.SemaphoreType.DMA((2 * heads_here,)),
        ],
        compiler_params=pltpu.CompilerParams(vmem_limit_bytes=STREAM_LIMIT),
    )(own, other, mod, w_query, w_key, w_value)


def merge_kernel(table, near_ref, far_ref, out_ref, sems):
    core = lax.axis_index("tp")
    copies = [
        pltpu.make_async_copy(far_ref.at[head], out_ref.at[owner_of(table, 1 - core, head)], sems.at[head])
        for head in range(far_ref.shape[0])
    ]
    for copy in copies:
        copy.start()
    for copy in copies:
        copy.wait()


def merge(near, far, table):
    return pl.pallas_call(
        functools.partial(merge_kernel, table),
        in_specs=[any_spec()] * 2,
        out_specs=any_spec(),
        out_shape=jax.ShapeDtypeStruct(near.shape, near.dtype),
        scratch_shapes=[pltpu.SemaphoreType.DMA((far.shape[0],))],
        input_output_aliases={0: 0},
        compiler_params=pltpu.CompilerParams(vmem_limit_bytes=VMEM_LIMIT),
    )(near, far)


def attend_kernel(table, lengths_ref, near_ref, far_ref, out_ref, query, keys, values, result, top, total, sems):
    chips, part_rows = query.shape[:2]
    side = lax.axis_index("tp")
    chip = lax.axis_index("req")
    active = functools.reduce(jnp.logical_or, [chip == owner for owner in table[0] + table[1]])
    front = pl.ds(0, HEAD_DIM)
    videos = lengths_ref.shape[0]

    @pl.when(active)
    def _():
        copies = []
        for source, target in (
            (near_ref.at[:, 0], query.at[:, :, front]),
            (near_ref.at[:, 1], keys.at[:, side, :, front]),
            (near_ref.at[:, 2], values.at[:, side, :, front]),
            (far_ref.at[:, 1], keys.at[:, 1 - side, :, front]),
            (far_ref.at[:, 2], values.at[:, 1 - side, :, front]),
        ):
            copies.append(pltpu.make_async_copy(source, target, sems.at[len(copies)]))
            copies[-1].start()
        ends, end = [], jnp.int32(0)
        for video in range(videos):
            end = end + lengths_ref[video]
            ends.append(end)
        starts = [jnp.int32(0)] + ends[:-1]
        lane = lax.broadcasted_iota(jnp.int32, (1, HEAD_DIM), 1)
        lane_start = jnp.zeros((1, HEAD_DIM), jnp.int32)
        lane_stop = jnp.zeros((1, HEAD_DIM), jnp.int32)
        for video, (start, stop) in enumerate(zip(starts, ends)):
            lane_start = jnp.where(lane == video, start, lane_start)
            lane_stop = jnp.where(lane == video, stop, lane_stop)
        place = lax.broadcasted_iota(jnp.int32, (part_rows, HEAD_DIM), 0)

        def fill(number, carry):
            for part in range(2):
                index = (2 * number + part) * part_rows + place
                member = (index >= lane_start) & (index < lane_stop)
                keys[number, part, :, HEAD_DIM:] = jnp.where(member | (lane >= videos), 0.0, NEG).astype(jnp.bfloat16)
                values[number, part, :, HEAD_DIM:] = jnp.ones((part_rows, HEAD_DIM), jnp.bfloat16)
            index = (2 * number + side) * part_rows + place
            member = (index >= lane_start) & (index < lane_stop)
            query[number, :, HEAD_DIM:] = jnp.where(member, 1.0, 0.0).astype(jnp.bfloat16)
            return carry

        lax.fori_loop(0, chips, fill, 0)
        for copy in copies:
            copy.wait()
        block_rows = QUERY_CHIPS * part_rows
        key_rows = 2 * KEY_CHIPS * part_rows

        def query_block(block, carry):
            first = (2 * QUERY_CHIPS * block + side) * part_rows
            last = first + 2 * (QUERY_CHIPS - 1) * part_rows + part_rows - 1
            low, high = jnp.int32(0), jnp.int32(0)
            for start, stop in zip(starts, ends):
                low = jnp.where(first >= start, start, low)
                high = jnp.where(last >= start, stop, high)
            q = query[pl.ds(block * QUERY_CHIPS, QUERY_CHIPS)].reshape(block_rows, 2 * HEAD_DIM)
            top[...] = jnp.full(top.shape, 2 * NEG, jnp.float32)
            total[...] = jnp.zeros(total.shape, jnp.float32)

            def key_block(number, carry):
                here = pl.ds(number * KEY_CHIPS, KEY_CHIPS)
                k = keys[here].reshape(key_rows, 2 * HEAD_DIM)
                score = lax.dot_general(q, k, (((1,), (1,)), ((), ())), preferred_element_type=jnp.float32)
                tiles = [score[:, j:j + HEAD_DIM] for j in range(0, key_rows, HEAD_DIM)]
                most = jnp.max(functools.reduce(jnp.maximum, tiles), axis=1, keepdims=True)
                before = top[...]
                now = jnp.maximum(before, most)
                probs = jnp.concatenate([jnp.exp2(tile - now).astype(jnp.bfloat16) for tile in tiles], axis=1)
                v = values[here].reshape(key_rows, 2 * HEAD_DIM)
                update = jnp.dot(probs, v, preferred_element_type=jnp.float32)
                shrink = jnp.exp2(before - now)
                total[:, :HEAD_DIM] = total[:, :HEAD_DIM] * shrink + update[:, :HEAD_DIM]
                total[:, HEAD_DIM:] = total[:, HEAD_DIM:] * shrink + update[:, HEAD_DIM:]
                top[...] = now
                return carry

            lax.fori_loop(low // key_rows, (high + key_rows - 1) // key_rows, key_block, 0)
            out = (total[:, :HEAD_DIM] / total[:, HEAD_DIM:]).astype(jnp.bfloat16)
            result[pl.ds(block * QUERY_CHIPS, QUERY_CHIPS)] = out.reshape(QUERY_CHIPS, part_rows, HEAD_DIM)
            return carry

        lax.fori_loop(0, chips // QUERY_CHIPS, query_block, 0)
        copy = pltpu.make_async_copy(result, out_ref, sems.at[0])
        copy.start()
        copy.wait()


def attend(lengths, near, far, table):
    chips, _, part_rows, _ = near.shape
    block_rows = QUERY_CHIPS * part_rows
    return pl.pallas_call(
        functools.partial(attend_kernel, table),
        in_specs=[smem_spec()] + [any_spec()] * 2,
        out_specs=any_spec(),
        out_shape=jax.ShapeDtypeStruct((chips, part_rows, HEAD_DIM), jnp.bfloat16),
        scratch_shapes=[
            pltpu.VMEM((chips, part_rows, 2 * HEAD_DIM), jnp.bfloat16),
            pltpu.VMEM((chips, 2, part_rows, 2 * HEAD_DIM), jnp.bfloat16),
            pltpu.VMEM((chips, 2, part_rows, 2 * HEAD_DIM), jnp.bfloat16),
            pltpu.VMEM((chips, part_rows, HEAD_DIM), jnp.bfloat16),
            pltpu.VMEM((block_rows, HEAD_DIM), jnp.float32),
            pltpu.VMEM((block_rows, 2 * HEAD_DIM), jnp.float32),
            pltpu.SemaphoreType.DMA((5,)),
        ],
        compiler_params=pltpu.CompilerParams(vmem_limit_bytes=VMEM_LIMIT),
    )(lengths, near, far)


def combine_kernel(table, near_ref, far_ref, weight, mine, theirs, attended, sems):
    share = mine.shape[1]
    part_rows = near_ref.shape[1]
    core = lax.axis_index("tp")
    copies = []
    for head in range(len(table[0])):
        columns = pl.ds(head * HEAD_DIM, HEAD_DIM)
        owner = owner_of(table, core, head)
        for source, side in ((near_ref, core), (far_ref, 1 - core)):
            target = attended.at[pl.ds(pl.multiple_of(side * part_rows, 32), part_rows), columns]
            copies.append(pltpu.make_async_copy(source.at[owner], target, sems.at[len(copies)]))
            copies[-1].start()
    for copy in copies:
        copy.wait()
    left = attended[...]
    for out, where in ((theirs, 1 - core), (mine, core)):
        columns = pl.ds(pl.multiple_of(where * share, 128), share)
        out[...] = jnp.dot(left, weight[:, columns], preferred_element_type=jnp.float32).astype(out.dtype)


def combine(near, far, w_out, table):
    rows = 2 * near.shape[1]
    depth, width = w_out.shape
    return pl.pallas_call(
        functools.partial(combine_kernel, table),
        in_specs=[any_spec()] * 2 + [vmem_spec()],
        out_specs=[vmem_spec(), vmem_spec()],
        out_shape=[
            jax.ShapeDtypeStruct((rows, width // 2), jnp.float32),
            jax.ShapeDtypeStruct((rows, width // 2), jnp.bfloat16),
        ],
        scratch_shapes=[
            pltpu.VMEM((rows, depth), jnp.bfloat16),
            pltpu.SemaphoreType.DMA((2 * len(table[0]),)),
        ],
        compiler_params=pltpu.CompilerParams(vmem_limit_bytes=VMEM_LIMIT),
    )(near, far, w_out)


def finish_kernel(timestep_ref, mine, theirs, tokens, mod_ref, velocity, stepped):
    share = tokens.shape[1]
    core = lax.axis_index("tp")
    step_value = jnp.full((1, 128), timestep_ref[0], jnp.int32).astype(jnp.float32)
    delta = (noise_level(step_value - 1.0) - noise_level(step_value))[:, :1]
    gate = mod_ref[2, :, pl.ds(pl.multiple_of(core * share, 128), share)]
    branch = gate * (mine[...] + theirs[...].astype(jnp.float32))
    velocity[...] = branch.astype(jnp.bfloat16)
    stepped[...] = (tokens[...].astype(jnp.float32) + delta * branch).astype(jnp.bfloat16)


def finish(timestep, mine, theirs, tokens, mod):
    shape = jax.ShapeDtypeStruct(tokens.shape, jnp.bfloat16)
    return pl.pallas_call(
        finish_kernel,
        in_specs=[smem_spec()] + [vmem_spec()] * 4,
        out_specs=[vmem_spec(), vmem_spec()],
        out_shape=[shape, shape],
        compiler_params=pltpu.CompilerParams(vmem_limit_bytes=VMEM_LIMIT),
    )(timestep, mine, theirs, tokens, mod)


def make(mesh):
    chips, tp = mesh.shape["req"], mesh.shape["tp"]
    swap = [(0, 1), (1, 0)]

    def on_device(tokens, video_lengths, timestep, time_weight, block_mod, w_query, w_key, w_value, w_out):
        heads_here = w_query.shape[1] // HEAD_DIM
        table = owners(chips, tp, heads_here)
        other = lax.ppermute(tokens, "tp", swap)
        half_freq = time_weight.shape[0] // 2
        time_value = jnp.broadcast_to(timestep, (half_freq,)).astype(jnp.float32)
        sigma = noise_level(time_value)
        frequency = jnp.exp(-math.log(10000.0) * jnp.arange(half_freq, dtype=jnp.float32) / half_freq)
        angle = 1000.0 * sigma * frequency
        act = jax.nn.silu(jnp.concatenate([jnp.cos(angle), jnp.sin(angle)]))[None, :]
        mod = modulate(act, time_weight, block_mod)
        near, far = project(tokens, other, mod, w_query, w_key, w_value, chips, table)
        near = merge(near, lax.ppermute(far, "tp", swap), table)
        near = lax.all_to_all(near, "req", 0, 0, tiled=True)
        done = attend(video_lengths, near, lax.ppermute(near, "tp", swap), table)
        done = lax.all_to_all(done, "req", 0, 0, tiled=True)
        mine, theirs = combine(done, lax.ppermute(done, "tp", swap), w_out, table)
        theirs = lax.ppermute(theirs, "tp", swap)
        velocity, stepped = finish(timestep, mine, theirs, tokens, mod)
        return (velocity, stepped)

    return on_device


def solution(mesh):
    return jax.shard_map(
        make(mesh),
        mesh=mesh,
        in_specs=(
            P("req", "tp"), P(), P(), P(), P(), P(None, "tp"), P(None, "tp"), P(None, "tp"), P("tp", None),
        ),
        out_specs=(P("req", "tp"), P("req", "tp")),
        check_vma=False,
    )
```

```python
import functools
import math

import jax
import jax.numpy as jnp
from jax import lax
from jax.experimental import pallas as pl
from jax.experimental.pallas import tpu as pltpu
from jax.sharding import PartitionSpec as P

HEAD_DIM = 128
STEPS = 1000
KEY_CHIPS = 16
QUERY_CHIPS = 4
NEG = -1e30
STREAM_LIMIT = 51 * 1024 * 1024
VMEM_LIMIT = 32 * 1024 * 1024


def noise_level(step_value):
    frac = step_value / STEPS
    return 5.0 * frac / (1.0 + 4.0 * frac)


def owners(chips, tp, heads_here):
    order = [chip for chip in range(chips) if chip % 4 != 3]
    return [[order[head * tp + core] for head in range(heads_here)] for core in range(tp)]


def owner_of(table, core, head):
    return jnp.where(core == 0, table[0][head], table[1][head])


def any_spec():
    return pl.BlockSpec(memory_space=pl.ANY)


def vmem_spec():
    return pl.BlockSpec(memory_space=pltpu.VMEM)


def smem_spec():
    return pl.BlockSpec(memory_space=pltpu.SMEM)


def project_kernel(table, act_ref, block_ref, own_ref, other_ref, time_ref, wq_ref, wk_ref, wv_ref, *rest):
    near_ref, far_ref, gate_ref, times, weights, full, normed, packed, sems, out_sems = rest
    depth, columns = wq_ref.shape
    rows, share = own_ref.shape
    freq = times.shape[0]
    part_rows = rows // 2
    core = lax.axis_index("tp")
    mine = pl.multiple_of(core * share, 128)
    loads = []

    def load(source, target):
        loads.append(pltpu.make_async_copy(source, target, sems.at[len(loads)]))
        loads[-1].start()

    for part in range(2):
        here = pl.ds(part * (freq // 2), freq // 2)
        load(time_ref.at[here, pl.ds(0, 2 * depth)], times.at[here, pl.ds(0, 2 * depth)])
    for part, ref in enumerate((wq_ref, wk_ref, wv_ref)):
        for cut in range(2):
            here = pl.ds(cut * (depth // 2), depth // 2)
            load(ref.at[here], weights.at[part, here])
    load(
        time_ref.at[:, pl.ds(pl.multiple_of(2 * depth + core * share, 128), share)],
        times.at[:, pl.ds(2 * depth, share)],
    )
    full[:, pl.ds(mine, share)] = own_ref[...].astype(jnp.float32)
    full[:, pl.ds(pl.multiple_of((1 - core) * share, 128), share)] = other_ref[...].astype(jnp.float32)
    whole = full[...]
    centred = whole - jnp.mean(whole, axis=1, keepdims=True)
    variance = jnp.mean(centred * centred, axis=1, keepdims=True)
    full[...] = centred * lax.rsqrt(variance + 1e-06)
    act = jnp.transpose(jnp.broadcast_to(act_ref[...], (8, freq)))[:, :1]
    act = jnp.broadcast_to(act, (freq, HEAD_DIM))

    def modulation(column):
        return jnp.sum(act * times[:, column:column + HEAD_DIM], axis=0, keepdims=True)

    loads[0].wait()
    loads[1].wait()
    for column in range(0, depth, HEAD_DIM):
        here = slice(column, column + HEAD_DIM)
        shift = modulation(column) + block_ref[0:1, here]
        scale = modulation(depth + column) + block_ref[1:2, here]
        normed[:, here] = (full[:, here] * (1.0 + scale) + shift).astype(jnp.bfloat16)
    factor = math.log2(math.e) / math.sqrt(HEAD_DIM)
    for part in range(3):
        loads[2 + 2 * part].wait()
        loads[3 + 2 * part].wait()
        for column in range(0, columns, 2 * HEAD_DIM):
            out = jnp.dot(
                normed[...], weights[part, :, column:column + 2 * HEAD_DIM], preferred_element_type=jnp.float32
            )
            if part == 0:
                out = out * factor
            for e in range(2):
                piece = out[:, e * HEAD_DIM:(e + 1) * HEAD_DIM].astype(jnp.bfloat16)
                packed[column // HEAD_DIM + e, part] = piece
    near, far = (pl.ds(pl.multiple_of(side * part_rows, 32), part_rows) for side in (core, 1 - core))
    copies = []
    for head in range(columns // HEAD_DIM):
        for source, target in ((far, far_ref.at[head]), (near, near_ref.at[owner_of(table, core, head)])):
            copies.append(pltpu.make_async_copy(packed.at[head, :, source], target, out_sems.at[len(copies)]))
            copies[-1].start()
    loads[8].wait()
    for column in range(0, share, HEAD_DIM):
        here = pl.ds(pl.multiple_of(mine + column, 128), HEAD_DIM)
        gate_ref[:, column:column + HEAD_DIM] = modulation(2 * depth + column) + block_ref[2:3, here]
    for copy in copies:
        copy.wait()


def project(act, block_mod, own, other, time_weight, w_query, w_key, w_value, chips, table):
    rows, share = own.shape
    depth, columns = w_query.shape
    freq = time_weight.shape[0]
    heads_here = columns // HEAD_DIM
    return pl.pallas_call(
        functools.partial(project_kernel, table),
        in_specs=[vmem_spec()] * 4 + [any_spec()] * 4,
        out_specs=[any_spec()] * 2 + [vmem_spec()],
        out_shape=[
            jax.ShapeDtypeStruct((chips, 3, rows // 2, HEAD_DIM), jnp.bfloat16),
            jax.ShapeDtypeStruct((heads_here, 3, rows // 2, HEAD_DIM), jnp.bfloat16),
            jax.ShapeDtypeStruct((1, share), jnp.float32),
        ],
        scratch_shapes=[
            pltpu.VMEM((freq, 2 * depth + share), jnp.float32),
            pltpu.VMEM((3, depth, columns), jnp.bfloat16),
            pltpu.VMEM((rows, depth), jnp.float32),
            pltpu.VMEM((rows, depth), jnp.bfloat16),
            pltpu.VMEM((heads_here, 3, rows, HEAD_DIM), jnp.bfloat16),
            pltpu.SemaphoreType.DMA((9,)),
            pltpu.SemaphoreType.DMA((2 * heads_here,)),
        ],
        compiler_params=pltpu.CompilerParams(vmem_limit_bytes=STREAM_LIMIT),
    )(act, block_mod, own, other, time_weight, w_query, w_key, w_value)


def merge_kernel(table, near_ref, far_ref, out_ref, sems):
    core = lax.axis_index("tp")
    copies = [
        pltpu.make_async_copy(far_ref.at[head], out_ref.at[owner_of(table, 1 - core, head)], sems.at[head])
        for head in range(far_ref.shape[0])
    ]
    for copy in copies:
        copy.start()
    for copy in copies:
        copy.wait()


def merge(near, far, table):
    return pl.pallas_call(
        functools.partial(merge_kernel, table),
        in_specs=[any_spec()] * 2,
        out_specs=any_spec(),
        out_shape=jax.ShapeDtypeStruct(near.shape, near.dtype),
        scratch_shapes=[pltpu.SemaphoreType.DMA((far.shape[0],))],
        input_output_aliases={0: 0},
        compiler_params=pltpu.CompilerParams(vmem_limit_bytes=VMEM_LIMIT),
    )(near, far)


def attend_kernel(table, lengths_ref, near_ref, far_ref, out_ref, query, keys, values, result, top, total, sems):
    chips, part_rows = query.shape[:2]
    side = lax.axis_index("tp")
    chip = lax.axis_index("req")
    active = functools.reduce(jnp.logical_or, [chip == owner for owner in table[0] + table[1]])
    front = pl.ds(0, HEAD_DIM)
    videos = lengths_ref.shape[0]

    @pl.when(active)
    def _():
        copies = []
        for source, target in (
            (near_ref.at[:, 0], query.at[:, :, front]),
            (near_ref.at[:, 1], keys.at[:, side, :, front]),
            (near_ref.at[:, 2], values.at[:, side, :, front]),
            (far_ref.at[:, 1], keys.at[:, 1 - side, :, front]),
            (far_ref.at[:, 2], values.at[:, 1 - side, :, front]),
        ):
            copies.append(pltpu.make_async_copy(source, target, sems.at[len(copies)]))
            copies[-1].start()
        ends, end = [], jnp.int32(0)
        for video in range(videos):
            end = end + lengths_ref[video]
            ends.append(end)
        starts = [jnp.int32(0)] + ends[:-1]
        lane = lax.broadcasted_iota(jnp.int32, (1, HEAD_DIM), 1)
        lane_start = jnp.zeros((1, HEAD_DIM), jnp.int32)
        lane_stop = jnp.zeros((1, HEAD_DIM), jnp.int32)
        for video, (start, stop) in enumerate(zip(starts, ends)):
            lane_start = jnp.where(lane == video, start, lane_start)
            lane_stop = jnp.where(lane == video, stop, lane_stop)
        place = lax.broadcasted_iota(jnp.int32, (part_rows, HEAD_DIM), 0)

        def fill(number, carry):
            for part in range(2):
                index = (2 * number + part) * part_rows + place
                member = (index >= lane_start) & (index < lane_stop)
                keys[number, part, :, HEAD_DIM:] = jnp.where(member | (lane >= videos), 0.0, NEG).astype(jnp.bfloat16)
                values[number, part, :, HEAD_DIM:] = jnp.ones((part_rows, HEAD_DIM), jnp.bfloat16)
            index = (2 * number + side) * part_rows + place
            member = (index >= lane_start) & (index < lane_stop)
            query[number, :, HEAD_DIM:] = jnp.where(member, 1.0, 0.0).astype(jnp.bfloat16)
            return carry

        lax.fori_loop(0, chips, fill, 0)
        for copy in copies:
            copy.wait()
        block_rows = QUERY_CHIPS * part_rows
        key_rows = 2 * KEY_CHIPS * part_rows
        groups = chips // KEY_CHIPS

        def query_block(block, carry):
            first = (2 * QUERY_CHIPS * block + side) * part_rows
            last = first + 2 * (QUERY_CHIPS - 1) * part_rows + part_rows - 1
            low, high = jnp.int32(0), jnp.int32(0)
            for start, stop in zip(starts, ends):
                low = jnp.where(first >= start, start, low)
                high = jnp.where(last >= start, stop, high)
            q = query[pl.ds(block * QUERY_CHIPS, QUERY_CHIPS)].reshape(block_rows, 2 * HEAD_DIM)

            def scores(number):
                k = keys[pl.ds(number * KEY_CHIPS, KEY_CHIPS)].reshape(key_rows, 2 * HEAD_DIM)
                score = lax.dot_general(q, k, (((1,), (1,)), ((), ())), preferred_element_type=jnp.float32)
                tiles = [score[:, j:j + HEAD_DIM] for j in range(0, key_rows, HEAD_DIM)]
                most = jnp.max(functools.reduce(jnp.maximum, tiles), axis=1, keepdims=True)
                return tiles, jnp.broadcast_to(most, (block_rows, HEAD_DIM))

            def weigh(number, tiles, now):
                probs = jnp.concatenate([jnp.exp2(tile - now).astype(jnp.bfloat16) for tile in tiles], axis=1)
                v = values[pl.ds(number * KEY_CHIPS, KEY_CHIPS)].reshape(key_rows, 2 * HEAD_DIM)
                return jnp.dot(probs, v, preferred_element_type=jnp.float32)

            if groups == 1:
                tiles, now = scores(0)
                update = weigh(0, tiles, now)
                out = update[:, :HEAD_DIM] / update[:, HEAD_DIM:]
            else:
                top[...] = jnp.full(top.shape, 2 * NEG, jnp.float32)
                total[...] = jnp.zeros(total.shape, jnp.float32)

                def key_block(number, carry):
                    tiles, most = scores(number)
                    before = top[...]
                    now = jnp.maximum(before, most)
                    update = weigh(number, tiles, now)
                    shrink = jnp.exp2(before - now)
                    total[:, :HEAD_DIM] = total[:, :HEAD_DIM] * shrink + update[:, :HEAD_DIM]
                    total[:, HEAD_DIM:] = total[:, HEAD_DIM:] * shrink + update[:, HEAD_DIM:]
                    top[...] = now
                    return carry

                lax.fori_loop(low // key_rows, (high + key_rows - 1) // key_rows, key_block, 0)
                out = total[:, :HEAD_DIM] / total[:, HEAD_DIM:]
            result[pl.ds(block * QUERY_CHIPS, QUERY_CHIPS)] = out.astype(jnp.bfloat16).reshape(
                QUERY_CHIPS, part_rows, HEAD_DIM
            )
            return carry

        lax.fori_loop(0, chips // QUERY_CHIPS, query_block, 0)
        copy = pltpu.make_async_copy(result, out_ref, sems.at[0])
        copy.start()
        copy.wait()


def attend(lengths, near, far, table):
    chips, _, part_rows, _ = near.shape
    block_rows = QUERY_CHIPS * part_rows
    return pl.pallas_call(
        functools.partial(attend_kernel, table),
        in_specs=[smem_spec()] + [any_spec()] * 2,
        out_specs=any_spec(),
        out_shape=jax.ShapeDtypeStruct((chips, part_rows, HEAD_DIM), jnp.bfloat16),
        scratch_shapes=[
            pltpu.VMEM((chips, part_rows, 2 * HEAD_DIM), jnp.bfloat16),
            pltpu.VMEM((chips, 2, part_rows, 2 * HEAD_DIM), jnp.bfloat16),
            pltpu.VMEM((chips, 2, part_rows, 2 * HEAD_DIM), jnp.bfloat16),
            pltpu.VMEM((chips, part_rows, HEAD_DIM), jnp.bfloat16),
            pltpu.VMEM((block_rows, HEAD_DIM), jnp.float32),
            pltpu.VMEM((block_rows, 2 * HEAD_DIM), jnp.float32),
            pltpu.SemaphoreType.DMA((5,)),
        ],
        compiler_params=pltpu.CompilerParams(vmem_limit_bytes=VMEM_LIMIT),
    )(lengths, near, far)


def combine_kernel(table, near_ref, far_ref, weight, mine, theirs, attended, sems):
    share = mine.shape[1]
    part_rows = near_ref.shape[1]
    core = lax.axis_index("tp")
    copies = []
    for head in range(len(table[0])):
        columns = pl.ds(head * HEAD_DIM, HEAD_DIM)
        owner = owner_of(table, core, head)
        for source, side in ((near_ref, core), (far_ref, 1 - core)):
            target = attended.at[pl.ds(pl.multiple_of(side * part_rows, 32), part_rows), columns]
            copies.append(pltpu.make_async_copy(source.at[owner], target, sems.at[len(copies)]))
            copies[-1].start()
    for copy in copies:
        copy.wait()
    left = attended[...]
    for out, where in ((theirs, 1 - core), (mine, core)):
        columns = pl.ds(pl.multiple_of(where * share, 128), share)
        out[...] = jnp.dot(left, weight[:, columns], preferred_element_type=jnp.float32).astype(out.dtype)


def combine(near, far, w_out, table):
    rows = 2 * near.shape[1]
    depth, width = w_out.shape
    return pl.pallas_call(
        functools.partial(combine_kernel, table),
        in_specs=[any_spec()] * 2 + [vmem_spec()],
        out_specs=[vmem_spec(), vmem_spec()],
        out_shape=[
            jax.ShapeDtypeStruct((rows, width // 2), jnp.float32),
            jax.ShapeDtypeStruct((rows, width // 2), jnp.bfloat16),
        ],
        scratch_shapes=[
            pltpu.VMEM((rows, depth), jnp.bfloat16),
            pltpu.SemaphoreType.DMA((2 * len(table[0]),)),
        ],
        compiler_params=pltpu.CompilerParams(vmem_limit_bytes=VMEM_LIMIT),
    )(near, far, w_out)


def finish_kernel(timestep_ref, mine, theirs, tokens, gate_ref, velocity, stepped):
    step_value = jnp.full((1, 128), timestep_ref[0], jnp.int32).astype(jnp.float32)
    delta = (noise_level(step_value - 1.0) - noise_level(step_value))[:, :1]
    branch = gate_ref[...] * (mine[...] + theirs[...].astype(jnp.float32))
    velocity[...] = branch.astype(jnp.bfloat16)
    stepped[...] = (tokens[...].astype(jnp.float32) + delta * branch).astype(jnp.bfloat16)


def finish(timestep, mine, theirs, tokens, gate):
    shape = jax.ShapeDtypeStruct(tokens.shape, jnp.bfloat16)
    return pl.pallas_call(
        finish_kernel,
        in_specs=[smem_spec()] + [vmem_spec()] * 4,
        out_specs=[vmem_spec(), vmem_spec()],
        out_shape=[shape, shape],
        compiler_params=pltpu.CompilerParams(vmem_limit_bytes=VMEM_LIMIT),
    )(timestep, mine, theirs, tokens, gate)


def make(mesh):
    chips, tp = mesh.shape["req"], mesh.shape["tp"]
    swap = [(0, 1), (1, 0)]

    def on_device(tokens, video_lengths, timestep, time_weight, block_mod, w_query, w_key, w_value, w_out):
        heads_here = w_query.shape[1] // HEAD_DIM
        table = owners(chips, tp, heads_here)
        other = lax.ppermute(tokens, "tp", swap)
        half_freq = time_weight.shape[0] // 2
        time_value = jnp.broadcast_to(timestep, (half_freq,)).astype(jnp.float32)
        sigma = noise_level(time_value)
        frequency = jnp.exp(-math.log(10000.0) * jnp.arange(half_freq, dtype=jnp.float32) / half_freq)
        angle = 1000.0 * sigma * frequency
        act = jax.nn.silu(jnp.concatenate([jnp.cos(angle), jnp.sin(angle)]))[None, :]
        near, far, gate = project(act, block_mod, tokens, other, time_weight, w_query, w_key, w_value, chips, table)
        near = merge(near, lax.ppermute(far, "tp", swap), table)
        near = lax.all_to_all(near, "req", 0, 0, tiled=True)
        done = attend(video_lengths, near, lax.ppermute(near, "tp", swap), table)
        done = lax.all_to_all(done, "req", 0, 0, tiled=True)
        mine, theirs = combine(done, lax.ppermute(done, "tp", swap), w_out, table)
        theirs = lax.ppermute(theirs, "tp", swap)
        velocity, stepped = finish(timestep, mine, theirs, tokens, gate)
        return (velocity, stepped)

    return on_device


def solution(mesh):
    return jax.shard_map(
        make(mesh),
        mesh=mesh,
        in_specs=(
            P("req", "tp"), P(), P(), P(), P(), P(None, "tp"), P(None, "tp"), P(None, "tp"), P("tp", None),
        ),
        out_specs=(P("req", "tp"), P("req", "tp")),
        check_vma=False,
    )
```

```python
import functools
import math

import jax
import jax.numpy as jnp
from jax import lax
from jax.experimental import pallas as pl
from jax.experimental.pallas import tpu as pltpu
from jax.sharding import PartitionSpec as P

HEAD_DIM = 128
STEPS = 1000
QUERY_BLOCK = 384
KEY_GROUP = 3072
WINDOWS = (1024, 2048)
NEG = -1e30
STREAM_LIMIT = 51 * 1024 * 1024
VMEM_LIMIT = 32 * 1024 * 1024


def noise_level(step_value):
    frac = step_value / STEPS
    return 5.0 * frac / (1.0 + 4.0 * frac)


def pairs_out(chips, heads, colour):
    half = chips // 2
    pairs = []
    for chip in range(chips):
        side, slot, x = chip // half, chip % half // 2, chip % 2
        for core in range(2):
            source, target = chip * 2 + core, (core * half + (slot ^ colour) * 2 + x) * 2 + side
            if (slot ^ colour) < heads and source != target:
                pairs.append((source, target))
    return pairs


def place_of(colours):
    chip = lax.axis_index("req")
    slot = lax.rem(chip // 2, colours)
    return slot, lax.rem(chip, 2), chip // (2 * colours) == lax.axis_index("tp")


def any_spec():
    return pl.BlockSpec(memory_space=pl.ANY)


def vmem_spec():
    return pl.BlockSpec(memory_space=pltpu.VMEM)


def smem_spec():
    return pl.BlockSpec(memory_space=pltpu.SMEM)


def standardise(full, own_ref, other_ref):
    share = own_ref.shape[1]
    core = lax.axis_index("tp")
    full[:, pl.ds(pl.multiple_of(core * share, 128), share)] = own_ref[...].astype(jnp.float32)
    full[:, pl.ds(pl.multiple_of((1 - core) * share, 128), share)] = other_ref[...].astype(jnp.float32)
    whole = full[...]
    centred = whole - jnp.mean(whole, axis=1, keepdims=True)
    variance = jnp.mean(centred * centred, axis=1, keepdims=True)
    return centred * lax.rsqrt(variance + 1e-06)


def project_part(packed, normed, weight, part):
    out = jnp.dot(normed[...], weight, preferred_element_type=jnp.float32)
    if part == 0:
        out = out * (math.log2(math.e) / math.sqrt(HEAD_DIM))
    for head in range(out.shape[1] // HEAD_DIM):
        packed[head, part] = out[:, head * HEAD_DIM:(head + 1) * HEAD_DIM].astype(jnp.bfloat16)


def load_weights(load, refs, weights):
    depth, columns = weights.shape[1:]
    x = lax.rem(lax.axis_index("req"), 2)
    for part, ref in enumerate(refs):
        for cut in range(2):
            here = pl.ds(cut * (depth // 2), depth // 2)
            load(ref.at[here, pl.ds(pl.multiple_of(x * columns, 128), columns)], weights.at[part, here])


def project_kernel(act_ref, block_ref, own_ref, other_ref, time_ref, wq_ref, wk_ref, wv_ref, *rest):
    packed, mod_ref, gate_ref, weights, times, full, normed, sems = rest
    depth = full.shape[1]
    share = own_ref.shape[1]
    freq = times.shape[0]
    core = lax.axis_index("tp")
    loads = []

    def load(source, target):
        loads.append(pltpu.make_async_copy(source, target, sems.at[len(loads)]))
        loads[-1].start()

    for part in range(2):
        here = pl.ds(part * (freq // 2), freq // 2)
        load(time_ref.at[here, pl.ds(0, 2 * depth)], times.at[here, pl.ds(0, 2 * depth)])
    load_weights(load, (wq_ref, wk_ref, wv_ref), weights)
    load(
        time_ref.at[:, pl.ds(pl.multiple_of(2 * depth + core * share, 128), share)],
        times.at[:, pl.ds(2 * depth, share)],
    )
    full[...] = standardise(full, own_ref, other_ref)
    act = jnp.transpose(jnp.broadcast_to(act_ref[...], (8, freq)))[:, :1]
    act = jnp.broadcast_to(act, (freq, HEAD_DIM))

    def modulation(column):
        return jnp.sum(act * times[:, column:column + HEAD_DIM], axis=0, keepdims=True)

    loads[0].wait()
    loads[1].wait()
    for column in range(0, depth, HEAD_DIM):
        here = slice(column, column + HEAD_DIM)
        shift = modulation(column) + block_ref[0:1, here]
        scale = modulation(depth + column) + block_ref[1:2, here]
        mod_ref[0:1, here] = shift
        mod_ref[1:2, here] = scale
        normed[:, here] = (full[:, here] * (1.0 + scale) + shift).astype(jnp.bfloat16)
    for part in range(3):
        loads[2 + 2 * part].wait()
        loads[3 + 2 * part].wait()
        project_part(packed, normed, weights[part], part)
    loads[8].wait()
    for column in range(0, share, HEAD_DIM):
        here = pl.ds(pl.multiple_of(core * share + column, 128), HEAD_DIM)
        gate_ref[:, column:column + HEAD_DIM] = modulation(2 * depth + column) + block_ref[2:3, here]


def project(act, block_mod, own, other, time_weight, w_query, w_key, w_value):
    rows, share = own.shape
    depth, columns = w_query.shape
    columns = columns // 2
    freq = time_weight.shape[0]
    heads = columns // HEAD_DIM
    return pl.pallas_call(
        project_kernel,
        in_specs=[vmem_spec()] * 4 + [any_spec()] * 4,
        out_specs=[vmem_spec()] * 3,
        out_shape=[
            jax.ShapeDtypeStruct((heads, 3, rows, HEAD_DIM), jnp.bfloat16),
            jax.ShapeDtypeStruct((2, depth), jnp.float32),
            jax.ShapeDtypeStruct((1, share), jnp.float32),
        ],
        scratch_shapes=[
            pltpu.VMEM((3, depth, columns), jnp.bfloat16),
            pltpu.VMEM((freq, 2 * depth + share), jnp.float32),
            pltpu.VMEM((rows, depth), jnp.float32),
            pltpu.VMEM((rows, depth), jnp.bfloat16),
            pltpu.SemaphoreType.DMA((9,)),
        ],
        compiler_params=pltpu.CompilerParams(vmem_limit_bytes=STREAM_LIMIT),
        cost_estimate=pl.CostEstimate(flops=6 * rows * depth * columns, bytes_accessed=8 * 2**20, transcendentals=0),
    )(act, block_mod, own, other, time_weight, w_query, w_key, w_value)


def share_kernel(colours, near_ref, far_ref, mod_ref, mine, wq_ref, wk_ref, wv_ref, *rest):
    outs, (weights, full, normed, packed, load_sems, sems) = rest[:colours], rest[colours:]
    heads, _, rows, _ = mine.shape
    loads = []

    def load(source, target):
        loads.append(pltpu.make_async_copy(source, target, load_sems.at[len(loads)]))
        loads[-1].start()

    load_weights(load, (wq_ref, wk_ref, wv_ref), weights)
    slot, x, _ = place_of(colours)

    def each_copy(source, position, offset, act):
        for head in range(heads):
            for colour in range(colours):
                @pl.when((slot ^ colour) == head)
                def _():
                    here = pl.ds(pl.multiple_of(position * rows, 64), rows)
                    act(pltpu.make_async_copy(source.at[head], outs[colour].at[:, here], sems.at[offset + head]))

    each_copy(mine, x, 0, lambda copy: copy.start())
    scaled = standardise(full, near_ref, far_ref)
    normed[...] = (scaled * (1.0 + mod_ref[1:2, :]) + mod_ref[0:1, :]).astype(jnp.bfloat16)
    for part in range(3):
        loads[2 * part].wait()
        loads[2 * part + 1].wait()
        project_part(packed, normed, weights[part], part)
    each_copy(packed, 1 - x, heads, lambda copy: copy.start())
    each_copy(mine, x, 0, lambda copy: copy.wait())
    each_copy(packed, 1 - x, heads, lambda copy: copy.wait())


def project_shared(near, far, mod, mine, w_query, w_key, w_value, colours):
    heads, _, rows, _ = mine.shape
    depth = mod.shape[1]
    return pl.pallas_call(
        functools.partial(share_kernel, colours),
        in_specs=[vmem_spec()] * 3 + [any_spec()] * 4,
        out_specs=[any_spec()] * colours,
        out_shape=[jax.ShapeDtypeStruct((3, 2 * rows, HEAD_DIM), jnp.bfloat16)] * colours,
        scratch_shapes=[
            pltpu.VMEM((3, depth, heads * HEAD_DIM), jnp.bfloat16),
            pltpu.VMEM((rows, depth), jnp.float32),
            pltpu.VMEM((rows, depth), jnp.bfloat16),
            pltpu.VMEM(mine.shape, jnp.bfloat16),
            pltpu.SemaphoreType.DMA((6,)),
            pltpu.SemaphoreType.DMA((2 * heads,)),
        ],
        compiler_params=pltpu.CompilerParams(vmem_limit_bytes=STREAM_LIMIT),
    )(near, far, mod, mine, w_query, w_key, w_value)


def collect_kernel(colours, sent_ref, *refs):
    pieces, out, sems = refs[:colours], refs[colours], refs[colours + 1]
    own = place_of(colours)[2]

    def each_copy(act):
        for colour, piece in enumerate(pieces):
            copy = pltpu.make_async_copy(piece.at[pl.ds(1, 2)], out.at[colour], sems.at[colour])
            if colour:
                act(copy)
            else:
                pl.when(jnp.logical_not(own))(functools.partial(act, copy))
                local = pltpu.make_async_copy(sent_ref.at[pl.ds(1, 2)], out.at[colour], sems.at[colour])
                pl.when(own)(functools.partial(act, local))

    each_copy(lambda copy: copy.start())
    each_copy(lambda copy: copy.wait())


def collect(sent, pieces):
    _, rows, wide = sent.shape
    colours = len(pieces)
    return pl.pallas_call(
        functools.partial(collect_kernel, colours),
        in_specs=[any_spec()] * (colours + 1),
        out_specs=any_spec(),
        out_shape=jax.ShapeDtypeStruct((colours, 2, rows, wide), jnp.bfloat16),
        scratch_shapes=[pltpu.SemaphoreType.DMA((colours,))],
        compiler_params=pltpu.CompilerParams(vmem_limit_bytes=VMEM_LIMIT),
    )(sent, *pieces)


def attend_kernel(colours, heads, lengths_ref, sent_ref, *refs):
    pieces, swapped = refs[:colours], refs[colours]
    outs = refs[colours + 1:2 * colours + 1]
    query, keys, values, result, top, total, sems, out_sems = refs[2 * colours + 1:]
    rows = sent_ref.shape[1]
    own_rows, all_rows = query.shape[0], keys.shape[0]
    side = lax.axis_index("tp")
    slot, _, own = place_of(colours)
    front = pl.ds(0, HEAD_DIM)
    videos = lengths_ref.shape[0]

    def at(colour, which):
        return pl.ds(pl.multiple_of((slot ^ colour) * rows + which * own_rows, 128), rows)

    def each_copy(act):
        for colour in range(colours):
            def load(piece, colour=colour):
                for part, target in enumerate((
                    query.at[at(colour, 0), front],
                    keys.at[at(colour, side), front],
                    values.at[at(colour, side), front],
                )):
                    act(pltpu.make_async_copy(piece.at[part], target, sems.at[5 * colour + part]))

            if colour:
                load(pieces[colour])
            else:
                pl.when(jnp.logical_not(own))(functools.partial(load, pieces[0]))
                pl.when(own)(functools.partial(load, sent_ref))
            for part, target in enumerate((keys, values)):
                target = target.at[at(colour, 1 - side), front]
                act(pltpu.make_async_copy(swapped.at[colour, part], target, sems.at[5 * colour + 3 + part]))

    @pl.when(slot < heads)
    def _():
        each_copy(lambda copy: copy.start())
        ends, end = [], jnp.int32(0)
        for video in range(videos):
            end = end + lengths_ref[video]
            ends.append(end)
        starts = [jnp.int32(0)] + ends[:-1]
        lane = lax.broadcasted_iota(jnp.int32, (1, HEAD_DIM), 1)
        lane_start = jnp.zeros((1, HEAD_DIM), jnp.int32)
        lane_stop = jnp.zeros((1, HEAD_DIM), jnp.int32)
        for video, (start, stop) in enumerate(zip(starts, ends)):
            lane_start = jnp.where(lane == video, start, lane_start)
            lane_stop = jnp.where(lane == video, stop, lane_stop)
        place = lax.broadcasted_iota(jnp.int32, (HEAD_DIM, HEAD_DIM), 0)

        def inside(first):
            index = first + place
            return (index >= lane_start) & (index < lane_stop)

        def fill_query(block, carry):
            local = pl.multiple_of(block * HEAD_DIM, HEAD_DIM)
            member = inside(side * own_rows + local)
            query[pl.ds(local, HEAD_DIM), HEAD_DIM:] = jnp.where(member, 1.0, 0.0).astype(jnp.bfloat16)
            return carry

        def fill_keys(block, carry):
            begin = pl.multiple_of(block * HEAD_DIM, HEAD_DIM)
            keys[pl.ds(begin, HEAD_DIM), HEAD_DIM:] = jnp.where(
                inside(begin) | (lane >= videos), 0.0, NEG
            ).astype(jnp.bfloat16)
            values[pl.ds(begin, HEAD_DIM), HEAD_DIM:] = jnp.ones((HEAD_DIM, HEAD_DIM), jnp.bfloat16)
            return carry

        lax.fori_loop(0, own_rows // HEAD_DIM, fill_query, 0)
        lax.fori_loop(0, all_rows // HEAD_DIM, fill_keys, 0)
        each_copy(lambda copy: copy.wait())

        def query_block(block, carry):
            local = pl.multiple_of(block * QUERY_BLOCK, QUERY_BLOCK)
            first = side * own_rows + local
            last = first + QUERY_BLOCK - 1
            low, high = jnp.int32(0), jnp.int32(0)
            for start, stop in zip(starts, ends):
                low = jnp.where(first >= start, start, low)
                high = jnp.where(last >= start, stop, high)
            low = low // HEAD_DIM * HEAD_DIM

            def scores(begin, count):
                score = lax.dot_general(
                    query[pl.ds(local, QUERY_BLOCK), :], keys[pl.ds(begin, count), :], (((1,), (1,)), ((), ())),
                    preferred_element_type=jnp.float32,
                )
                tiles = [score[:, j:j + HEAD_DIM] for j in range(0, count, HEAD_DIM)]
                most = jnp.max(functools.reduce(jnp.maximum, tiles), axis=1, keepdims=True)
                return tiles, jnp.broadcast_to(most, (QUERY_BLOCK, HEAD_DIM))

            def weigh(begin, count, tiles, now):
                probs = jnp.concatenate([jnp.exp2(tile - now).astype(jnp.bfloat16) for tile in tiles], axis=1)
                return jnp.dot(probs, values[pl.ds(begin, count), :], preferred_element_type=jnp.float32)

            def store(update):
                out = update[:, :HEAD_DIM] / update[:, HEAD_DIM:]
                result[pl.ds(local, QUERY_BLOCK), :] = out.astype(jnp.bfloat16)

            def window(count):
                begin = pl.multiple_of(jnp.minimum(low, all_rows - count), HEAD_DIM)
                tiles, now = scores(begin, count)
                store(weigh(begin, count, tiles, now))

            def long():
                top[...] = jnp.full(top.shape, 2 * NEG, jnp.float32)
                total[...] = jnp.zeros(total.shape, jnp.float32)

                def key_block(number, carry):
                    begin = pl.multiple_of(number * KEY_GROUP, KEY_GROUP)
                    tiles, most = scores(begin, KEY_GROUP)
                    before = top[...]
                    now = jnp.maximum(before, most)
                    update = weigh(begin, KEY_GROUP, tiles, now)
                    shrink = jnp.exp2(before - now)
                    total[:, :HEAD_DIM] = total[:, :HEAD_DIM] * shrink + update[:, :HEAD_DIM]
                    total[:, HEAD_DIM:] = total[:, HEAD_DIM:] * shrink + update[:, HEAD_DIM:]
                    top[...] = now
                    return carry

                lax.fori_loop(low // KEY_GROUP, (high + KEY_GROUP - 1) // KEY_GROUP, key_block, 0)
                store(total)

            need = high - low
            small, middle = WINDOWS
            pl.when(need <= small)(lambda: window(small))
            pl.when((need > small) & (need <= middle))(lambda: window(middle))
            if all_rows == KEY_GROUP:
                pl.when(need > middle)(lambda: window(KEY_GROUP))
            else:
                pl.when(need > middle)(long)
            return carry

        lax.fori_loop(0, own_rows // QUERY_BLOCK, query_block, 0)
        copies = [
            pltpu.make_async_copy(result.at[at(colour, 0)], outs[colour], out_sems.at[colour])
            for colour in range(colours)
        ]
        for copy in copies:
            copy.start()
        for copy in copies:
            copy.wait()


def attend(lengths, sent, pieces, swapped, heads):
    rows = sent.shape[1]
    colours = len(pieces)
    own = colours * rows
    return pl.pallas_call(
        functools.partial(attend_kernel, colours, heads),
        in_specs=[smem_spec()] + [any_spec()] * (colours + 2),
        out_specs=[any_spec()] * colours,
        out_shape=[jax.ShapeDtypeStruct((rows, HEAD_DIM), jnp.bfloat16)] * colours,
        scratch_shapes=[
            pltpu.VMEM((own, 2 * HEAD_DIM), jnp.bfloat16),
            pltpu.VMEM((2 * own, 2 * HEAD_DIM), jnp.bfloat16),
            pltpu.VMEM((2 * own, 2 * HEAD_DIM), jnp.bfloat16),
            pltpu.VMEM((own, HEAD_DIM), jnp.bfloat16),
            pltpu.VMEM((QUERY_BLOCK, HEAD_DIM), jnp.float32),
            pltpu.VMEM((QUERY_BLOCK, 2 * HEAD_DIM), jnp.float32),
            pltpu.SemaphoreType.DMA((5 * colours,)),
            pltpu.SemaphoreType.DMA((colours,)),
        ],
        compiler_params=pltpu.CompilerParams(vmem_limit_bytes=VMEM_LIMIT),
    )(lengths, sent, *pieces, swapped)


def part_kernel(colours, done_ref, *refs):
    pieces, (keep, give, sems) = refs[:colours], refs[colours:]
    heads, rows, _ = keep.shape
    slot, x, own = place_of(colours)

    def each_copy(act):
        for head in range(heads):
            for number, (target, position) in enumerate(((give, 1 - x), (keep, x))):
                here = pl.ds(pl.multiple_of(position * rows, 64), rows)

                def move(piece, head=head, number=number, target=target, here=here):
                    act(pltpu.make_async_copy(piece.at[here], target.at[head], sems.at[2 * head + number]))

                for colour in range(colours):
                    right = (slot ^ colour) == head
                    if colour:
                        pl.when(right)(functools.partial(move, pieces[colour]))
                    else:
                        pl.when(right & jnp.logical_not(own))(functools.partial(move, pieces[0]))
                        pl.when(right & own)(functools.partial(move, done_ref))

    each_copy(lambda copy: copy.start())
    each_copy(lambda copy: copy.wait())


def part(done, pieces, heads):
    rows = done.shape[0] // 2
    shape = jax.ShapeDtypeStruct((heads, rows, HEAD_DIM), jnp.bfloat16)
    return pl.pallas_call(
        functools.partial(part_kernel, len(pieces)),
        in_specs=[any_spec()] * (len(pieces) + 1),
        out_specs=[any_spec()] * 2,
        out_shape=[shape, shape],
        scratch_shapes=[pltpu.SemaphoreType.DMA((2 * heads,))],
        compiler_params=pltpu.CompilerParams(vmem_limit_bytes=VMEM_LIMIT),
    )(done, *pieces)


def combine_kernel(keep_ref, got_ref, weight, mine, theirs, attended, sems):
    share = mine.shape[1]
    heads = keep_ref.shape[0]
    core = lax.axis_index("tp")
    x = lax.rem(lax.axis_index("req"), 2)
    copies = []
    for head in range(heads):
        for source, which in ((keep_ref, x), (got_ref, 1 - x)):
            columns = pl.ds(pl.multiple_of((which * heads + head) * HEAD_DIM, HEAD_DIM), HEAD_DIM)
            copies.append(pltpu.make_async_copy(source.at[head], attended.at[:, columns], sems.at[len(copies)]))
            copies[-1].start()
    for copy in copies:
        copy.wait()
    left = attended[...]
    for out, where in ((theirs, 1 - core), (mine, core)):
        columns = pl.ds(pl.multiple_of(where * share, 128), share)
        out[...] = jnp.dot(left, weight[:, columns], preferred_element_type=jnp.float32).astype(out.dtype)


def combine(keep, got, w_out):
    heads, rows, _ = keep.shape
    depth, width = w_out.shape
    return pl.pallas_call(
        combine_kernel,
        in_specs=[any_spec()] * 2 + [vmem_spec()],
        out_specs=[vmem_spec(), vmem_spec()],
        out_shape=[
            jax.ShapeDtypeStruct((rows, width // 2), jnp.float32),
            jax.ShapeDtypeStruct((rows, width // 2), jnp.bfloat16),
        ],
        scratch_shapes=[
            pltpu.VMEM((rows, depth), jnp.bfloat16),
            pltpu.SemaphoreType.DMA((2 * heads,)),
        ],
        compiler_params=pltpu.CompilerParams(vmem_limit_bytes=VMEM_LIMIT),
    )(keep, got, w_out)


def finish_kernel(timestep_ref, mine, theirs, tokens, gate_ref, velocity, stepped):
    step_value = jnp.full((1, 128), timestep_ref[0], jnp.int32).astype(jnp.float32)
    delta = (noise_level(step_value - 1.0) - noise_level(step_value))[:, :1]
    branch = gate_ref[...] * (mine[...] + theirs[...].astype(jnp.float32))
    velocity[...] = branch.astype(jnp.bfloat16)
    stepped[...] = (tokens[...].astype(jnp.float32) + delta * branch).astype(jnp.bfloat16)


def finish(timestep, mine, theirs, tokens, gate):
    shape = jax.ShapeDtypeStruct(tokens.shape, jnp.bfloat16)
    return pl.pallas_call(
        finish_kernel,
        in_specs=[smem_spec()] + [vmem_spec()] * 4,
        out_specs=[vmem_spec(), vmem_spec()],
        out_shape=[shape, shape],
        compiler_params=pltpu.CompilerParams(vmem_limit_bytes=VMEM_LIMIT),
    )(timestep, mine, theirs, tokens, gate)


def make(mesh):
    chips = mesh.shape["req"]
    colours = chips // 4
    swap = [(0, 1), (1, 0)]
    cross = [(chip, chip ^ 1) for chip in range(chips)]

    def on_device(tokens, video_lengths, timestep, time_weight, block_mod, w_query, w_key, w_value, w_out):
        heads = w_query.shape[1] // HEAD_DIM // 2
        routes = [pairs_out(chips, heads, colour) for colour in range(colours)]
        near = lax.ppermute(tokens, "req", cross)
        other = lax.ppermute(tokens, "tp", swap)
        half_freq = time_weight.shape[0] // 2
        time_value = jnp.broadcast_to(timestep, (half_freq,)).astype(jnp.float32)
        sigma = noise_level(time_value)
        frequency = jnp.exp(-math.log(10000.0) * jnp.arange(half_freq, dtype=jnp.float32) / half_freq)
        angle = 1000.0 * sigma * frequency
        act = jax.nn.silu(jnp.concatenate([jnp.cos(angle), jnp.sin(angle)]))[None, :]
        mine, mod, gate = project(act, block_mod, tokens, other, time_weight, w_query, w_key, w_value)
        near, mine, mod, gate = lax.optimization_barrier((near, mine, mod, gate))
        far = lax.ppermute(near, "tp", swap)
        sent = project_shared(near, far, mod, mine, w_query, w_key, w_value, colours)
        got = [lax.ppermute(piece, ("req", "tp"), route) for piece, route in zip(sent, routes)]
        swapped = lax.ppermute(collect(sent[0], got), "tp", swap)
        done = attend(video_lengths, sent[0], got, swapped, heads)
        back = [
            lax.ppermute(piece, ("req", "tp"), [(b, a) for a, b in route]) for piece, route in zip(done, routes)
        ]
        keep, give = part(done[0], back, heads)
        mine, theirs = combine(keep, lax.ppermute(give, "req", cross), w_out)
        theirs = lax.ppermute(theirs, "tp", swap)
        velocity, stepped = finish(timestep, mine, theirs, tokens, gate)
        return (velocity, stepped)

    return on_device


def solution(mesh):
    return jax.shard_map(
        make(mesh),
        mesh=mesh,
        in_specs=(
            P("req", "tp"), P(), P(), P(), P(), P(None, "tp"), P(None, "tp"), P(None, "tp"), P("tp", None),
        ),
        out_specs=(P("req", "tp"), P("req", "tp")),
        check_vma=False,
    )
```

```python
import functools
import math

import jax
import jax.numpy as jnp
from jax import lax
from jax.experimental import pallas as pl
from jax.experimental.pallas import tpu as pltpu
from jax.sharding import PartitionSpec as P

HEAD_DIM = 128
STEPS = 1000
QUERY_BLOCK = 384
KEY_GROUP = 3072
WINDOWS = (1024, 2048)
NEG = -1e30
STREAM_LIMIT = 51 * 1024 * 1024
VMEM_LIMIT = 32 * 1024 * 1024


def noise_level(step_value):
    frac = step_value / STEPS
    return 5.0 * frac / (1.0 + 4.0 * frac)


def pairs_out(chips, heads, colour):
    colours = chips // 4
    pairs = []
    for chip in range(chips):
        side, bit, slot = chip // (2 * colours), chip // colours % 2, chip % colours
        for core in range(2):
            owner = (2 * side + core) * colours + (slot ^ colour)
            source, target = chip * 2 + core, owner * 2 + bit
            if (slot ^ colour) < heads and source != target:
                pairs.append((source, target))
    return pairs


def place_of(colours):
    chip = lax.axis_index("req")
    return (
        lax.rem(chip, colours),
        chip // (2 * colours),
        lax.rem(chip // colours, 2) == lax.axis_index("tp"),
    )


def any_spec():
    return pl.BlockSpec(memory_space=pl.ANY)


def vmem_spec():
    return pl.BlockSpec(memory_space=pltpu.VMEM)


def smem_spec():
    return pl.BlockSpec(memory_space=pltpu.SMEM)


def standardise(full, own_ref, other_ref):
    share = own_ref.shape[1]
    core = lax.axis_index("tp")
    full[:, pl.ds(pl.multiple_of(core * share, 128), share)] = own_ref[...].astype(jnp.float32)
    full[:, pl.ds(pl.multiple_of((1 - core) * share, 128), share)] = other_ref[...].astype(jnp.float32)
    whole = full[...]
    centred = whole - jnp.mean(whole, axis=1, keepdims=True)
    variance = jnp.mean(centred * centred, axis=1, keepdims=True)
    return centred * lax.rsqrt(variance + 1e-06)


def project_part(packed, normed, weight, part):
    out = jnp.dot(normed[...], weight, preferred_element_type=jnp.float32)
    if part == 0:
        out = out * (math.log2(math.e) / math.sqrt(HEAD_DIM))
    for head in range(out.shape[1] // HEAD_DIM):
        packed[head, part] = out[:, head * HEAD_DIM:(head + 1) * HEAD_DIM].astype(jnp.bfloat16)


def load_weights(load, refs, weights, side):
    depth, columns = weights.shape[1:]
    for part, ref in enumerate(refs):
        for cut in range(2):
            here = pl.ds(cut * (depth // 2), depth // 2)
            load(ref.at[here, pl.ds(pl.multiple_of(side * columns, 128), columns)], weights.at[part, here])


def project_kernel(colours, act_ref, block_ref, own_ref, other_ref, time_ref, wq_ref, wk_ref, wv_ref, *rest):
    packed, mod_ref, gate_ref, weights, times, full, normed, sems = rest
    depth = full.shape[1]
    share = own_ref.shape[1]
    freq = times.shape[0]
    core = lax.axis_index("tp")
    loads = []

    def load(source, target):
        loads.append(pltpu.make_async_copy(source, target, sems.at[len(loads)]))
        loads[-1].start()

    for part in range(2):
        here = pl.ds(part * (freq // 2), freq // 2)
        load(time_ref.at[here, pl.ds(0, 2 * depth)], times.at[here, pl.ds(0, 2 * depth)])
    load_weights(load, (wq_ref, wk_ref, wv_ref), weights, place_of(colours)[1])
    load(
        time_ref.at[:, pl.ds(pl.multiple_of(2 * depth + core * share, 128), share)],
        times.at[:, pl.ds(2 * depth, share)],
    )
    full[...] = standardise(full, own_ref, other_ref)
    act = jnp.transpose(jnp.broadcast_to(act_ref[...], (8, freq)))[:, :1]
    act = jnp.broadcast_to(act, (freq, HEAD_DIM))

    def modulation(column):
        return jnp.sum(act * times[:, column:column + HEAD_DIM], axis=0, keepdims=True)

    loads[0].wait()
    loads[1].wait()
    for column in range(0, depth, HEAD_DIM):
        here = slice(column, column + HEAD_DIM)
        shift = modulation(column) + block_ref[0:1, here]
        scale = modulation(depth + column) + block_ref[1:2, here]
        mod_ref[0:1, here] = shift
        mod_ref[1:2, here] = scale
        normed[:, here] = (full[:, here] * (1.0 + scale) + shift).astype(jnp.bfloat16)
    for part in range(3):
        loads[2 + 2 * part].wait()
        loads[3 + 2 * part].wait()
        project_part(packed, normed, weights[part], part)
    loads[8].wait()
    for column in range(0, share, HEAD_DIM):
        here = pl.ds(pl.multiple_of(core * share + column, 128), HEAD_DIM)
        gate_ref[:, column:column + HEAD_DIM] = modulation(2 * depth + column) + block_ref[2:3, here]


def project(act, block_mod, own, other, time_weight, w_query, w_key, w_value, colours):
    rows, share = own.shape
    depth, columns = w_query.shape
    columns = columns // 2
    freq = time_weight.shape[0]
    heads = columns // HEAD_DIM
    return pl.pallas_call(
        functools.partial(project_kernel, colours),
        in_specs=[vmem_spec()] * 4 + [any_spec()] * 4,
        out_specs=[vmem_spec()] * 3,
        out_shape=[
            jax.ShapeDtypeStruct((heads, 3, rows, HEAD_DIM), jnp.bfloat16),
            jax.ShapeDtypeStruct((2, depth), jnp.float32),
            jax.ShapeDtypeStruct((1, share), jnp.float32),
        ],
        scratch_shapes=[
            pltpu.VMEM((3, depth, columns), jnp.bfloat16),
            pltpu.VMEM((freq, 2 * depth + share), jnp.float32),
            pltpu.VMEM((rows, depth), jnp.float32),
            pltpu.VMEM((rows, depth), jnp.bfloat16),
            pltpu.SemaphoreType.DMA((9,)),
        ],
        compiler_params=pltpu.CompilerParams(vmem_limit_bytes=STREAM_LIMIT),
        cost_estimate=pl.CostEstimate(flops=6 * rows * depth * columns, bytes_accessed=8 * 2**20, transcendentals=0),
    )(act, block_mod, own, other, time_weight, w_query, w_key, w_value)


def share_kernel(colours, near_ref, far_ref, mod_ref, mine, wq_ref, wk_ref, wv_ref, *rest):
    outs, (weights, full, normed, packed, load_sems, sems) = rest[:colours], rest[colours:]
    heads, _, rows, _ = mine.shape
    slot, side, _ = place_of(colours)
    loads = []

    def load(source, target):
        loads.append(pltpu.make_async_copy(source, target, load_sems.at[len(loads)]))
        loads[-1].start()

    load_weights(load, (wq_ref, wk_ref, wv_ref), weights, side)

    def each_copy(source, position, offset, act):
        for head in range(heads):
            for colour in range(colours):
                @pl.when((slot ^ colour) == head)
                def _():
                    here = pl.ds(pl.multiple_of(position * rows, 64), rows)
                    act(pltpu.make_async_copy(source.at[head], outs[colour].at[:, here], sems.at[offset + head]))

    each_copy(mine, side, 0, lambda copy: copy.start())
    scaled = standardise(full, near_ref, far_ref)
    normed[...] = (scaled * (1.0 + mod_ref[1:2, :]) + mod_ref[0:1, :]).astype(jnp.bfloat16)
    for part in range(3):
        loads[2 * part].wait()
        loads[2 * part + 1].wait()
        project_part(packed, normed, weights[part], part)
    each_copy(packed, 1 - side, heads, lambda copy: copy.start())
    each_copy(mine, side, 0, lambda copy: copy.wait())
    each_copy(packed, 1 - side, heads, lambda copy: copy.wait())


def project_shared(near, far, mod, mine, w_query, w_key, w_value, colours):
    heads, _, rows, _ = mine.shape
    depth = mod.shape[1]
    return pl.pallas_call(
        functools.partial(share_kernel, colours),
        in_specs=[vmem_spec()] * 3 + [any_spec()] * 4,
        out_specs=[any_spec()] * colours,
        out_shape=[jax.ShapeDtypeStruct((3, 2 * rows, HEAD_DIM), jnp.bfloat16)] * colours,
        scratch_shapes=[
            pltpu.VMEM((3, depth, heads * HEAD_DIM), jnp.bfloat16),
            pltpu.VMEM((rows, depth), jnp.float32),
            pltpu.VMEM((rows, depth), jnp.bfloat16),
            pltpu.VMEM(mine.shape, jnp.bfloat16),
            pltpu.SemaphoreType.DMA((6,)),
            pltpu.SemaphoreType.DMA((2 * heads,)),
        ],
        compiler_params=pltpu.CompilerParams(vmem_limit_bytes=STREAM_LIMIT),
    )(near, far, mod, mine, w_query, w_key, w_value)


def collect_kernel(colours, sent_ref, *refs):
    pieces, out, sems = refs[:colours], refs[colours], refs[colours + 1]
    own = place_of(colours)[2]

    def each_copy(act):
        for colour, piece in enumerate(pieces):
            copy = pltpu.make_async_copy(piece.at[pl.ds(1, 2)], out.at[colour], sems.at[colour])
            if colour:
                act(copy)
            else:
                pl.when(jnp.logical_not(own))(functools.partial(act, copy))
                local = pltpu.make_async_copy(sent_ref.at[pl.ds(1, 2)], out.at[colour], sems.at[colour])
                pl.when(own)(functools.partial(act, local))

    each_copy(lambda copy: copy.start())
    each_copy(lambda copy: copy.wait())


def collect(sent, pieces):
    _, rows, wide = sent.shape
    colours = len(pieces)
    return pl.pallas_call(
        functools.partial(collect_kernel, colours),
        in_specs=[any_spec()] * (colours + 1),
        out_specs=any_spec(),
        out_shape=jax.ShapeDtypeStruct((colours, 2, rows, wide), jnp.bfloat16),
        scratch_shapes=[pltpu.SemaphoreType.DMA((colours,))],
        compiler_params=pltpu.CompilerParams(vmem_limit_bytes=VMEM_LIMIT),
    )(sent, *pieces)


def attend_kernel(colours, heads, lengths_ref, sent_ref, *refs):
    pieces, swapped = refs[:colours], refs[colours]
    outs = refs[colours + 1:2 * colours + 1]
    query, keys, values, result, top, total, sems, out_sems = refs[2 * colours + 1:]
    rows = sent_ref.shape[1]
    own_rows, all_rows = query.shape[0], keys.shape[0]
    bit = lax.axis_index("tp")
    slot, _, own = place_of(colours)
    quarter = own_rows // 2
    rows = rows // 2
    front = pl.ds(0, HEAD_DIM)
    videos = lengths_ref.shape[0]

    def at(colour, side):
        return pl.ds(pl.multiple_of((slot ^ colour) * rows + side * quarter, 64), rows)

    def at_all(colour, which, side):
        return pl.ds(pl.multiple_of((slot ^ colour) * rows + (2 * side + which) * quarter, 64), rows)

    def each_copy(act):
        for colour in range(colours):
            def load(piece, colour=colour):
                for side in range(2):
                    here = pl.ds(side * rows, rows)
                    for part, target in enumerate((
                        query.at[at(colour, side), front],
                        keys.at[at_all(colour, bit, side), front],
                        values.at[at_all(colour, bit, side), front],
                    )):
                        sem = sems.at[10 * colour + 5 * side + part]
                        act(pltpu.make_async_copy(piece.at[part, here], target, sem))

            if colour:
                load(pieces[colour])
            else:
                pl.when(jnp.logical_not(own))(functools.partial(load, pieces[0]))
                pl.when(own)(functools.partial(load, sent_ref))
            for side in range(2):
                here = pl.ds(side * rows, rows)
                for part, target in enumerate((keys, values)):
                    target = target.at[at_all(colour, 1 - bit, side), front]
                    sem = sems.at[10 * colour + 5 * side + 3 + part]
                    act(pltpu.make_async_copy(swapped.at[colour, part, here], target, sem))

    @pl.when(slot < heads)
    def _():
        each_copy(lambda copy: copy.start())
        ends, end = [], jnp.int32(0)
        for video in range(videos):
            end = end + lengths_ref[video]
            ends.append(end)
        starts = [jnp.int32(0)] + ends[:-1]
        lane = lax.broadcasted_iota(jnp.int32, (1, HEAD_DIM), 1)
        lane_start = jnp.zeros((1, HEAD_DIM), jnp.int32)
        lane_stop = jnp.zeros((1, HEAD_DIM), jnp.int32)
        for video, (start, stop) in enumerate(zip(starts, ends)):
            lane_start = jnp.where(lane == video, start, lane_start)
            lane_stop = jnp.where(lane == video, stop, lane_stop)
        place = lax.broadcasted_iota(jnp.int32, (HEAD_DIM, HEAD_DIM), 0)

        def token_of(local):
            return local + jnp.where(local < quarter, bit, bit + 1) * quarter

        def inside(first):
            index = first + place
            return (index >= lane_start) & (index < lane_stop)

        def fill_query(block, carry):
            local = pl.multiple_of(block * HEAD_DIM, HEAD_DIM)
            member = inside(token_of(local))
            query[pl.ds(local, HEAD_DIM), HEAD_DIM:] = jnp.where(member, 1.0, 0.0).astype(jnp.bfloat16)
            return carry

        def fill_keys(block, carry):
            begin = pl.multiple_of(block * HEAD_DIM, HEAD_DIM)
            keys[pl.ds(begin, HEAD_DIM), HEAD_DIM:] = jnp.where(
                inside(begin) | (lane >= videos), 0.0, NEG
            ).astype(jnp.bfloat16)
            values[pl.ds(begin, HEAD_DIM), HEAD_DIM:] = jnp.ones((HEAD_DIM, HEAD_DIM), jnp.bfloat16)
            return carry

        lax.fori_loop(0, own_rows // HEAD_DIM, fill_query, 0)
        lax.fori_loop(0, all_rows // HEAD_DIM, fill_keys, 0)
        each_copy(lambda copy: copy.wait())

        def query_block(block, carry):
            local = pl.multiple_of(block * QUERY_BLOCK, QUERY_BLOCK)
            first = token_of(local)
            last = first + QUERY_BLOCK - 1
            low, high = jnp.int32(0), jnp.int32(0)
            for start, stop in zip(starts, ends):
                low = jnp.where(first >= start, start, low)
                high = jnp.where(last >= start, stop, high)
            low = low // HEAD_DIM * HEAD_DIM

            def scores(begin, count):
                score = lax.dot_general(
                    query[pl.ds(local, QUERY_BLOCK), :], keys[pl.ds(begin, count), :], (((1,), (1,)), ((), ())),
                    preferred_element_type=jnp.float32,
                )
                tiles = [score[:, j:j + HEAD_DIM] for j in range(0, count, HEAD_DIM)]
                most = jnp.max(functools.reduce(jnp.maximum, tiles), axis=1, keepdims=True)
                return tiles, jnp.broadcast_to(most, (QUERY_BLOCK, HEAD_DIM))

            def weigh(begin, count, tiles, now):
                probs = jnp.concatenate([jnp.exp2(tile - now).astype(jnp.bfloat16) for tile in tiles], axis=1)
                return jnp.dot(probs, values[pl.ds(begin, count), :], preferred_element_type=jnp.float32)

            def store(update):
                out = update[:, :HEAD_DIM] / update[:, HEAD_DIM:]
                result[pl.ds(local, QUERY_BLOCK), :] = out.astype(jnp.bfloat16)

            def window(count):
                begin = pl.multiple_of(jnp.minimum(low, all_rows - count), HEAD_DIM)
                tiles, now = scores(begin, count)
                store(weigh(begin, count, tiles, now))

            def long():
                top[...] = jnp.full(top.shape, 2 * NEG, jnp.float32)
                total[...] = jnp.zeros(total.shape, jnp.float32)

                def key_block(number, carry):
                    begin = pl.multiple_of(number * KEY_GROUP, KEY_GROUP)
                    tiles, most = scores(begin, KEY_GROUP)
                    before = top[...]
                    now = jnp.maximum(before, most)
                    update = weigh(begin, KEY_GROUP, tiles, now)
                    shrink = jnp.exp2(before - now)
                    total[:, :HEAD_DIM] = total[:, :HEAD_DIM] * shrink + update[:, :HEAD_DIM]
                    total[:, HEAD_DIM:] = total[:, HEAD_DIM:] * shrink + update[:, HEAD_DIM:]
                    top[...] = now
                    return carry

                lax.fori_loop(low // KEY_GROUP, (high + KEY_GROUP - 1) // KEY_GROUP, key_block, 0)
                store(total)

            need = high - low
            small, middle = WINDOWS
            pl.when(need <= small)(lambda: window(small))
            pl.when((need > small) & (need <= middle))(lambda: window(middle))
            if all_rows == KEY_GROUP:
                pl.when(need > middle)(lambda: window(KEY_GROUP))
            else:
                pl.when(need > middle)(long)
            return carry

        lax.fori_loop(0, own_rows // QUERY_BLOCK, query_block, 0)
        copies = [
            pltpu.make_async_copy(
                result.at[at(colour, side)], outs[colour].at[pl.ds(side * rows, rows)], out_sems.at[2 * colour + side]
            )
            for colour in range(colours) for side in range(2)
        ]
        for copy in copies:
            copy.start()
        for copy in copies:
            copy.wait()


def attend(lengths, sent, pieces, swapped, heads):
    rows = sent.shape[1]
    colours = len(pieces)
    own = colours * rows
    return pl.pallas_call(
        functools.partial(attend_kernel, colours, heads),
        in_specs=[smem_spec()] + [any_spec()] * (colours + 2),
        out_specs=[any_spec()] * colours,
        out_shape=[jax.ShapeDtypeStruct((rows, HEAD_DIM), jnp.bfloat16)] * colours,
        scratch_shapes=[
            pltpu.VMEM((own, 2 * HEAD_DIM), jnp.bfloat16),
            pltpu.VMEM((2 * own, 2 * HEAD_DIM), jnp.bfloat16),
            pltpu.VMEM((2 * own, 2 * HEAD_DIM), jnp.bfloat16),
            pltpu.VMEM((own, HEAD_DIM), jnp.bfloat16),
            pltpu.VMEM((QUERY_BLOCK, HEAD_DIM), jnp.float32),
            pltpu.VMEM((QUERY_BLOCK, 2 * HEAD_DIM), jnp.float32),
            pltpu.SemaphoreType.DMA((10 * colours,)),
            pltpu.SemaphoreType.DMA((2 * colours,)),
        ],
        compiler_params=pltpu.CompilerParams(vmem_limit_bytes=VMEM_LIMIT),
    )(lengths, sent, *pieces, swapped)


def part_kernel(colours, done_ref, *refs):
    pieces, (keep, give, sems) = refs[:colours], refs[colours:]
    heads, rows, _ = keep.shape
    slot, own_side, own = place_of(colours)

    def each_copy(act):
        for head in range(heads):
            for number, (target, position) in enumerate(((give, 1 - own_side), (keep, own_side))):
                here = pl.ds(pl.multiple_of(position * rows, 64), rows)

                def move(piece, head=head, number=number, target=target, here=here):
                    act(pltpu.make_async_copy(piece.at[here], target.at[head], sems.at[2 * head + number]))

                for colour in range(colours):
                    right = (slot ^ colour) == head
                    if colour:
                        pl.when(right)(functools.partial(move, pieces[colour]))
                    else:
                        pl.when(right & jnp.logical_not(own))(functools.partial(move, pieces[0]))
                        pl.when(right & own)(functools.partial(move, done_ref))

    each_copy(lambda copy: copy.start())
    each_copy(lambda copy: copy.wait())


def part(done, pieces, heads):
    rows = done.shape[0] // 2
    shape = jax.ShapeDtypeStruct((heads, rows, HEAD_DIM), jnp.bfloat16)
    return pl.pallas_call(
        functools.partial(part_kernel, len(pieces)),
        in_specs=[any_spec()] * (len(pieces) + 1),
        out_specs=[any_spec()] * 2,
        out_shape=[shape, shape],
        scratch_shapes=[pltpu.SemaphoreType.DMA((2 * heads,))],
        compiler_params=pltpu.CompilerParams(vmem_limit_bytes=VMEM_LIMIT),
    )(done, *pieces)


def combine_kernel(colours, keep_ref, got_ref, weight, mine, theirs, attended, sems):
    share = mine.shape[1]
    heads = keep_ref.shape[0]
    core = lax.axis_index("tp")
    side = place_of(colours)[1]
    copies = []
    for head in range(heads):
        for source, which in ((keep_ref, side), (got_ref, 1 - side)):
            columns = pl.ds(pl.multiple_of((which * heads + head) * HEAD_DIM, HEAD_DIM), HEAD_DIM)
            copies.append(pltpu.make_async_copy(source.at[head], attended.at[:, columns], sems.at[len(copies)]))
            copies[-1].start()
    for copy in copies:
        copy.wait()
    left = attended[...]
    for out, where in ((theirs, 1 - core), (mine, core)):
        columns = pl.ds(pl.multiple_of(where * share, 128), share)
        out[...] = jnp.dot(left, weight[:, columns], preferred_element_type=jnp.float32).astype(out.dtype)


def combine(keep, got, w_out, colours):
    heads, rows, _ = keep.shape
    depth, width = w_out.shape
    return pl.pallas_call(
        functools.partial(combine_kernel, colours),
        in_specs=[any_spec()] * 2 + [vmem_spec()],
        out_specs=[vmem_spec(), vmem_spec()],
        out_shape=[
            jax.ShapeDtypeStruct((rows, width // 2), jnp.float32),
            jax.ShapeDtypeStruct((rows, width // 2), jnp.bfloat16),
        ],
        scratch_shapes=[
            pltpu.VMEM((rows, depth), jnp.bfloat16),
            pltpu.SemaphoreType.DMA((2 * heads,)),
        ],
        compiler_params=pltpu.CompilerParams(vmem_limit_bytes=VMEM_LIMIT),
    )(keep, got, w_out)


def finish_kernel(timestep_ref, mine, theirs, tokens, gate_ref, velocity, stepped):
    step_value = jnp.full((1, 128), timestep_ref[0], jnp.int32).astype(jnp.float32)
    delta = (noise_level(step_value - 1.0) - noise_level(step_value))[:, :1]
    branch = gate_ref[...] * (mine[...] + theirs[...].astype(jnp.float32))
    velocity[...] = branch.astype(jnp.bfloat16)
    stepped[...] = (tokens[...].astype(jnp.float32) + delta * branch).astype(jnp.bfloat16)


def finish(timestep, mine, theirs, tokens, gate):
    shape = jax.ShapeDtypeStruct(tokens.shape, jnp.bfloat16)
    return pl.pallas_call(
        finish_kernel,
        in_specs=[smem_spec()] + [vmem_spec()] * 4,
        out_specs=[vmem_spec(), vmem_spec()],
        out_shape=[shape, shape],
        compiler_params=pltpu.CompilerParams(vmem_limit_bytes=VMEM_LIMIT),
    )(timestep, mine, theirs, tokens, gate)


def make(mesh):
    chips = mesh.shape["req"]
    colours = chips // 4
    swap = [(0, 1), (1, 0)]
    cross = [(chip, (chip + chips // 2) % chips) for chip in range(chips)]

    def on_device(tokens, video_lengths, timestep, time_weight, block_mod, w_query, w_key, w_value, w_out):
        heads = w_query.shape[1] // HEAD_DIM // 2
        routes = [pairs_out(chips, heads, colour) for colour in range(colours)]
        near = lax.ppermute(tokens, "req", cross)
        other = lax.ppermute(tokens, "tp", swap)
        half_freq = time_weight.shape[0] // 2
        time_value = jnp.broadcast_to(timestep, (half_freq,)).astype(jnp.float32)
        sigma = noise_level(time_value)
        frequency = jnp.exp(-math.log(10000.0) * jnp.arange(half_freq, dtype=jnp.float32) / half_freq)
        angle = 1000.0 * sigma * frequency
        act = jax.nn.silu(jnp.concatenate([jnp.cos(angle), jnp.sin(angle)]))[None, :]
        mine, mod, gate = project(act, block_mod, tokens, other, time_weight, w_query, w_key, w_value, colours)
        near, mine, mod, gate = lax.optimization_barrier((near, mine, mod, gate))
        far = lax.ppermute(near, "tp", swap)
        sent = project_shared(near, far, mod, mine, w_query, w_key, w_value, colours)
        got = [lax.ppermute(piece, ("req", "tp"), route) for piece, route in zip(sent, routes)]
        swapped = lax.ppermute(collect(sent[0], got), "tp", swap)
        done = attend(video_lengths, sent[0], got, swapped, heads)
        back = [
            lax.ppermute(piece, ("req", "tp"), [(b, a) for a, b in route]) for piece, route in zip(done, routes)
        ]
        keep, give = part(done[0], back, heads)
        mine, theirs = combine(keep, lax.ppermute(give, "req", cross), w_out, colours)
        theirs = lax.ppermute(theirs, "tp", swap)
        velocity, stepped = finish(timestep, mine, theirs, tokens, gate)
        return (velocity, stepped)

    return on_device


def solution(mesh):
    return jax.shard_map(
        make(mesh),
        mesh=mesh,
        in_specs=(
            P("req", "tp"), P(), P(), P(), P(), P(None, "tp"), P(None, "tp"), P(None, "tp"), P("tp", None),
        ),
        out_specs=(P("req", "tp"), P("req", "tp")),
        check_vma=False,
    )
```

```python
import functools
import math

import jax
import jax.numpy as jnp
from jax import lax
from jax.experimental import pallas as pl
from jax.experimental.pallas import tpu as pltpu
from jax.sharding import PartitionSpec as P

HEAD_DIM = 128
STEPS = 1000
QUERY_BLOCK = 384
KEY_GROUP = 3072
WINDOWS = (512, 1024, 1536, 2048, 2560)
NEG = -1e30
STREAM_LIMIT = 51 * 1024 * 1024
VMEM_LIMIT = 32 * 1024 * 1024


def noise_level(step_value):
    frac = step_value / STEPS
    return 5.0 * frac / (1.0 + 4.0 * frac)


def pairs_out(chips, heads, colour):
    half = chips // 2
    pairs = []
    for chip in range(chips):
        side, slot, x = chip // half, chip % half // 2, chip % 2
        for core in range(2):
            source, target = chip * 2 + core, (core * half + (slot ^ colour) * 2 + x) * 2 + side
            if (slot ^ colour) < heads:
                pairs.append((source, target))
    return pairs


def place_of(colours):
    chip = lax.axis_index("req")
    return lax.rem(chip // 2, colours), lax.rem(chip, 2)


def any_spec():
    return pl.BlockSpec(memory_space=pl.ANY)


def vmem_spec():
    return pl.BlockSpec(memory_space=pltpu.VMEM)


def smem_spec():
    return pl.BlockSpec(memory_space=pltpu.SMEM)


def standardise(full, own_ref, other_ref):
    share = own_ref.shape[1]
    core = lax.axis_index("tp")
    full[:, pl.ds(pl.multiple_of(core * share, 128), share)] = own_ref[...].astype(jnp.float32)
    full[:, pl.ds(pl.multiple_of((1 - core) * share, 128), share)] = other_ref[...].astype(jnp.float32)
    whole = full[...]
    centred = whole - jnp.mean(whole, axis=1, keepdims=True)
    variance = jnp.mean(centred * centred, axis=1, keepdims=True)
    return centred * lax.rsqrt(variance + 1e-06)


def project_part(packed, normed, weight, part):
    out = jnp.dot(normed[...], weight, preferred_element_type=jnp.float32)
    if part == 0:
        out = out * (math.log2(math.e) / math.sqrt(HEAD_DIM))
    for head in range(out.shape[1] // HEAD_DIM):
        packed[head, part] = out[:, head * HEAD_DIM:(head + 1) * HEAD_DIM].astype(jnp.bfloat16)


def load_weights(load, refs, weights):
    depth, columns = weights.shape[1:]
    x = lax.rem(lax.axis_index("req"), 2)
    for part, ref in enumerate(refs):
        for cut in range(2):
            here = pl.ds(cut * (depth // 2), depth // 2)
            load(ref.at[here, pl.ds(pl.multiple_of(x * columns, 128), columns)], weights.at[part, here])


def project_kernel(act_ref, block_ref, own_ref, other_ref, time_ref, wq_ref, wk_ref, wv_ref, *rest):
    packed, mod_ref, gate_ref, weights, times, full, normed, sems = rest
    depth = full.shape[1]
    share = own_ref.shape[1]
    freq = times.shape[0]
    core = lax.axis_index("tp")
    loads = []

    def load(source, target):
        loads.append(pltpu.make_async_copy(source, target, sems.at[len(loads)]))
        loads[-1].start()

    for part in range(2):
        here = pl.ds(part * (freq // 2), freq // 2)
        load(time_ref.at[here, pl.ds(0, 2 * depth)], times.at[here, pl.ds(0, 2 * depth)])
    load_weights(load, (wq_ref, wk_ref, wv_ref), weights)
    load(
        time_ref.at[:, pl.ds(pl.multiple_of(2 * depth + core * share, 128), share)],
        times.at[:, pl.ds(2 * depth, share)],
    )
    full[...] = standardise(full, own_ref, other_ref)
    act = jnp.transpose(jnp.broadcast_to(act_ref[...], (8, freq)))[:, :1]
    act = jnp.broadcast_to(act, (freq, HEAD_DIM))

    def modulation(column):
        return jnp.sum(act * times[:, column:column + HEAD_DIM], axis=0, keepdims=True)

    loads[0].wait()
    loads[1].wait()
    for column in range(0, depth, HEAD_DIM):
        here = slice(column, column + HEAD_DIM)
        shift = modulation(column) + block_ref[0:1, here]
        scale = modulation(depth + column) + block_ref[1:2, here]
        mod_ref[0:1, here] = shift
        mod_ref[1:2, here] = scale
        normed[:, here] = (full[:, here] * (1.0 + scale) + shift).astype(jnp.bfloat16)
    for part in range(3):
        loads[2 + 2 * part].wait()
        loads[3 + 2 * part].wait()
        project_part(packed, normed, weights[part], part)
    loads[8].wait()
    for column in range(0, share, HEAD_DIM):
        here = pl.ds(pl.multiple_of(core * share + column, 128), HEAD_DIM)
        gate_ref[:, column:column + HEAD_DIM] = modulation(2 * depth + column) + block_ref[2:3, here]


def project(act, block_mod, own, other, time_weight, w_query, w_key, w_value):
    rows, share = own.shape
    depth, columns = w_query.shape
    columns = columns // 2
    freq = time_weight.shape[0]
    heads = columns // HEAD_DIM
    return pl.pallas_call(
        project_kernel,
        in_specs=[vmem_spec()] * 4 + [any_spec()] * 4,
        out_specs=[vmem_spec()] * 3,
        out_shape=[
            jax.ShapeDtypeStruct((heads, 3, rows, HEAD_DIM), jnp.bfloat16),
            jax.ShapeDtypeStruct((2, depth), jnp.float32),
            jax.ShapeDtypeStruct((1, share), jnp.float32),
        ],
        scratch_shapes=[
            pltpu.VMEM((3, depth, columns), jnp.bfloat16),
            pltpu.VMEM((freq, 2 * depth + share), jnp.float32),
            pltpu.VMEM((rows, depth), jnp.float32),
            pltpu.VMEM((rows, depth), jnp.bfloat16),
            pltpu.SemaphoreType.DMA((9,)),
        ],
        compiler_params=pltpu.CompilerParams(vmem_limit_bytes=STREAM_LIMIT),
        cost_estimate=pl.CostEstimate(flops=6 * rows * depth * columns, bytes_accessed=8 * 2**20, transcendentals=0),
    )(act, block_mod, own, other, time_weight, w_query, w_key, w_value)


def share_kernel(colours, near_ref, far_ref, mod_ref, mine, wq_ref, wk_ref, wv_ref, *rest):
    outs, (weights, full, normed, packed, load_sems, sems) = rest[:colours], rest[colours:]
    heads, _, rows, _ = mine.shape
    loads = []

    def load(source, target):
        loads.append(pltpu.make_async_copy(source, target, load_sems.at[len(loads)]))
        loads[-1].start()

    load_weights(load, (wq_ref, wk_ref, wv_ref), weights)
    slot, x = place_of(colours)

    def each_copy(source, position, offset, act):
        for head in range(heads):
            for colour in range(colours):
                @pl.when((slot ^ colour) == head)
                def _():
                    here = pl.ds(pl.multiple_of(position * rows, 64), rows)
                    act(pltpu.make_async_copy(source.at[head], outs[colour].at[:, here], sems.at[offset + head]))

    each_copy(mine, x, 0, lambda copy: copy.start())
    scaled = standardise(full, near_ref, far_ref)
    normed[...] = (scaled * (1.0 + mod_ref[1:2, :]) + mod_ref[0:1, :]).astype(jnp.bfloat16)
    for part in range(3):
        loads[2 * part].wait()
        loads[2 * part + 1].wait()
        project_part(packed, normed, weights[part], part)
    each_copy(packed, 1 - x, heads, lambda copy: copy.start())
    each_copy(mine, x, 0, lambda copy: copy.wait())
    each_copy(packed, 1 - x, heads, lambda copy: copy.wait())


def project_shared(near, far, mod, mine, w_query, w_key, w_value, colours):
    heads, _, rows, _ = mine.shape
    depth = mod.shape[1]
    return pl.pallas_call(
        functools.partial(share_kernel, colours),
        in_specs=[vmem_spec()] * 3 + [any_spec()] * 4,
        out_specs=[any_spec()] * colours,
        out_shape=[jax.ShapeDtypeStruct((3, 2 * rows, HEAD_DIM), jnp.bfloat16)] * colours,
        scratch_shapes=[
            pltpu.VMEM((3, depth, heads * HEAD_DIM), jnp.bfloat16),
            pltpu.VMEM((rows, depth), jnp.float32),
            pltpu.VMEM((rows, depth), jnp.bfloat16),
            pltpu.VMEM(mine.shape, jnp.bfloat16),
            pltpu.SemaphoreType.DMA((6,)),
            pltpu.SemaphoreType.DMA((2 * heads,)),
        ],
        compiler_params=pltpu.CompilerParams(vmem_limit_bytes=STREAM_LIMIT),
    )(near, far, mod, mine, w_query, w_key, w_value)


def attend_kernel(colours, heads, lengths_ref, *refs):
    pieces, swapped, outs = refs[:colours], refs[colours:2 * colours], refs[2 * colours:3 * colours]
    query, keys, values, result, top, total, sems, out_sems = refs[3 * colours:]
    rows = pieces[0].shape[1]
    own_rows, all_rows = query.shape[0], keys.shape[0]
    side = lax.axis_index("tp")
    slot, _ = place_of(colours)
    front = pl.ds(0, HEAD_DIM)
    videos = lengths_ref.shape[0]

    def at(colour, which):
        return pl.ds(pl.multiple_of((slot ^ colour) * rows + which * own_rows, 128), rows)

    def each_copy(act):
        for colour in range(colours):
            near, far = pieces[colour], swapped[colour]
            for number, (source, target) in enumerate((
                (near.at[0], query.at[at(colour, 0), front]),
                (near.at[1], keys.at[at(colour, side), front]),
                (near.at[2], values.at[at(colour, side), front]),
                (far.at[1], keys.at[at(colour, 1 - side), front]),
                (far.at[2], values.at[at(colour, 1 - side), front]),
            )):
                act(pltpu.make_async_copy(source, target, sems.at[5 * colour + number]))

    @pl.when(slot < heads)
    def _():
        each_copy(lambda copy: copy.start())
        ends, end = [], jnp.int32(0)
        for video in range(videos):
            end = end + lengths_ref[video]
            ends.append(end)
        starts = [jnp.int32(0)] + ends[:-1]
        lane = lax.broadcasted_iota(jnp.int32, (1, HEAD_DIM), 1)
        lane_start = jnp.zeros((1, HEAD_DIM), jnp.int32)
        lane_stop = jnp.zeros((1, HEAD_DIM), jnp.int32)
        for video, (start, stop) in enumerate(zip(starts, ends)):
            lane_start = jnp.where(lane == video, start, lane_start)
            lane_stop = jnp.where(lane == video, stop, lane_stop)
        place = lax.broadcasted_iota(jnp.int32, (HEAD_DIM, HEAD_DIM), 0)

        def inside(first):
            index = first + place
            return (index >= lane_start) & (index < lane_stop)

        def fill_query(block, carry):
            local = pl.multiple_of(block * HEAD_DIM, HEAD_DIM)
            member = inside(side * own_rows + local)
            query[pl.ds(local, HEAD_DIM), HEAD_DIM:] = jnp.where(member, 1.0, 0.0).astype(jnp.bfloat16)
            return carry

        def fill_keys(block, carry):
            begin = pl.multiple_of(block * HEAD_DIM, HEAD_DIM)
            keys[pl.ds(begin, HEAD_DIM), HEAD_DIM:] = jnp.where(
                inside(begin) | (lane >= videos), 0.0, NEG
            ).astype(jnp.bfloat16)
            values[pl.ds(begin, HEAD_DIM), HEAD_DIM:] = jnp.ones((HEAD_DIM, HEAD_DIM), jnp.bfloat16)
            return carry

        lax.fori_loop(0, own_rows // HEAD_DIM, fill_query, 0)
        lax.fori_loop(0, all_rows // HEAD_DIM, fill_keys, 0)
        each_copy(lambda copy: copy.wait())

        sub = QUERY_BLOCK // 2

        def query_block(block, carry):
            local = pl.multiple_of(block * QUERY_BLOCK, QUERY_BLOCK)
            first = side * own_rows + local
            last = first + QUERY_BLOCK - 1
            low, high = jnp.int32(0), jnp.int32(0)
            for start, stop in zip(starts, ends):
                low = jnp.where(first >= start, start, low)
                high = jnp.where(last >= start, stop, high)
            low = low // HEAD_DIM * HEAD_DIM

            def scores(offset, begin, count):
                q = query[pl.ds(pl.multiple_of(local + offset, 64), sub), :]
                score = lax.dot_general(
                    q, keys[pl.ds(begin, count), :], (((1,), (1,)), ((), ())), preferred_element_type=jnp.float32
                )
                tiles = [score[:, j:j + HEAD_DIM] for j in range(0, count, HEAD_DIM)]
                most = jnp.max(functools.reduce(jnp.maximum, tiles), axis=1, keepdims=True)
                return tiles, jnp.broadcast_to(most, (sub, HEAD_DIM))

            def weigh(begin, count, tiles, now):
                probs = jnp.concatenate([jnp.exp2(tile - now).astype(jnp.bfloat16) for tile in tiles], axis=1)
                return jnp.dot(probs, values[pl.ds(begin, count), :], preferred_element_type=jnp.float32)

            def store(offset, update):
                out = update[:, :HEAD_DIM] / update[:, HEAD_DIM:]
                result[pl.ds(pl.multiple_of(local + offset, 64), sub), :] = out.astype(jnp.bfloat16)

            def window(count):
                begin = pl.multiple_of(jnp.minimum(low, all_rows - count), HEAD_DIM)
                tiles, now = scores(0, begin, count)
                for offset in range(0, QUERY_BLOCK, sub):
                    later = scores(offset + sub, begin, count) if offset + sub < QUERY_BLOCK else None
                    store(offset, weigh(begin, count, tiles, now))
                    if later is not None:
                        tiles, now = later

            def long(offset):
                top[...] = jnp.full(top.shape, 2 * NEG, jnp.float32)
                total[...] = jnp.zeros(total.shape, jnp.float32)

                def key_block(number, carry):
                    begin = pl.multiple_of(number * KEY_GROUP, KEY_GROUP)
                    tiles, most = scores(offset, begin, KEY_GROUP)
                    before = top[...]
                    now = jnp.maximum(before, most)
                    update = weigh(begin, KEY_GROUP, tiles, now)
                    shrink = jnp.exp2(before - now)
                    total[:, :HEAD_DIM] = total[:, :HEAD_DIM] * shrink + update[:, :HEAD_DIM]
                    total[:, HEAD_DIM:] = total[:, HEAD_DIM:] * shrink + update[:, HEAD_DIM:]
                    top[...] = now
                    return carry

                lax.fori_loop(low // KEY_GROUP, (high + KEY_GROUP - 1) // KEY_GROUP, key_block, 0)
                store(offset, total)

            need = high - low
            floor = 0
            for count in WINDOWS:
                pl.when((need > floor) & (need <= count))(functools.partial(window, count))
                floor = count

            @pl.when(need > floor)
            def _():
                if all_rows == KEY_GROUP:
                    window(KEY_GROUP)
                else:
                    for offset in range(0, QUERY_BLOCK, sub):
                        long(offset)

            return carry

        lax.fori_loop(0, own_rows // QUERY_BLOCK, query_block, 0)
        copies = [
            pltpu.make_async_copy(result.at[at(colour, 0)], outs[colour], out_sems.at[colour])
            for colour in range(colours)
        ]
        for copy in copies:
            copy.start()
        for copy in copies:
            copy.wait()


def attend(lengths, pieces, swapped, heads):
    rows = pieces[0].shape[1]
    colours = len(pieces)
    own = colours * rows
    return pl.pallas_call(
        functools.partial(attend_kernel, colours, heads),
        in_specs=[smem_spec()] + [any_spec()] * (2 * colours),
        out_specs=[any_spec()] * colours,
        out_shape=[jax.ShapeDtypeStruct((rows, HEAD_DIM), jnp.bfloat16)] * colours,
        scratch_shapes=[
            pltpu.VMEM((own, 2 * HEAD_DIM), jnp.bfloat16),
            pltpu.VMEM((2 * own, 2 * HEAD_DIM), jnp.bfloat16),
            pltpu.VMEM((2 * own, 2 * HEAD_DIM), jnp.bfloat16),
            pltpu.VMEM((own, HEAD_DIM), jnp.bfloat16),
            pltpu.VMEM((QUERY_BLOCK // 2, HEAD_DIM), jnp.float32),
            pltpu.VMEM((QUERY_BLOCK // 2, 2 * HEAD_DIM), jnp.float32),
            pltpu.SemaphoreType.DMA((5 * colours,)),
            pltpu.SemaphoreType.DMA((colours,)),
        ],
        compiler_params=pltpu.CompilerParams(vmem_limit_bytes=VMEM_LIMIT),
    )(lengths, *pieces, *swapped)


def part_kernel(colours, *refs):
    pieces, (keep, give, sems) = refs[:colours], refs[colours:]
    heads, rows, _ = keep.shape
    slot, x = place_of(colours)

    def each_copy(act):
        for head in range(heads):
            for number, (target, position) in enumerate(((give, 1 - x), (keep, x))):
                here = pl.ds(pl.multiple_of(position * rows, 64), rows)
                for colour in range(colours):
                    @pl.when((slot ^ colour) == head)
                    def _():
                        source = pieces[colour].at[here]
                        act(pltpu.make_async_copy(source, target.at[head], sems.at[2 * head + number]))

    each_copy(lambda copy: copy.start())
    each_copy(lambda copy: copy.wait())


def part(pieces, heads):
    rows = pieces[0].shape[0] // 2
    shape = jax.ShapeDtypeStruct((heads, rows, HEAD_DIM), jnp.bfloat16)
    return pl.pallas_call(
        functools.partial(part_kernel, len(pieces)),
        in_specs=[any_spec()] * len(pieces),
        out_specs=[any_spec()] * 2,
        out_shape=[shape, shape],
        scratch_shapes=[pltpu.SemaphoreType.DMA((2 * heads,))],
        compiler_params=pltpu.CompilerParams(vmem_limit_bytes=VMEM_LIMIT),
    )(*pieces)


def combine_kernel(keep_ref, got_ref, weight, mine, theirs, attended, sems):
    share = mine.shape[1]
    heads = keep_ref.shape[0]
    core = lax.axis_index("tp")
    x = lax.rem(lax.axis_index("req"), 2)
    copies = []
    for head in range(heads):
        for source, which in ((keep_ref, x), (got_ref, 1 - x)):
            columns = pl.ds(pl.multiple_of((which * heads + head) * HEAD_DIM, HEAD_DIM), HEAD_DIM)
            copies.append(pltpu.make_async_copy(source.at[head], attended.at[:, columns], sems.at[len(copies)]))
            copies[-1].start()
    for copy in copies:
        copy.wait()
    left = attended[...]
    for out, where in ((theirs, 1 - core), (mine, core)):
        columns = pl.ds(pl.multiple_of(where * share, 128), share)
        out[...] = jnp.dot(left, weight[:, columns], preferred_element_type=jnp.float32).astype(out.dtype)


def combine(keep, got, w_out):
    heads, rows, _ = keep.shape
    depth, width = w_out.shape
    return pl.pallas_call(
        combine_kernel,
        in_specs=[any_spec()] * 2 + [vmem_spec()],
        out_specs=[vmem_spec(), vmem_spec()],
        out_shape=[
            jax.ShapeDtypeStruct((rows, width // 2), jnp.float32),
            jax.ShapeDtypeStruct((rows, width // 2), jnp.bfloat16),
        ],
        scratch_shapes=[
            pltpu.VMEM((rows, depth), jnp.bfloat16),
            pltpu.SemaphoreType.DMA((2 * heads,)),
        ],
        compiler_params=pltpu.CompilerParams(vmem_limit_bytes=VMEM_LIMIT),
    )(keep, got, w_out)


def finish_kernel(timestep_ref, mine, theirs, tokens, gate_ref, velocity, stepped):
    step_value = jnp.full((1, 128), timestep_ref[0], jnp.int32).astype(jnp.float32)
    delta = (noise_level(step_value - 1.0) - noise_level(step_value))[:, :1]
    branch = gate_ref[...] * (mine[...] + theirs[...].astype(jnp.float32))
    velocity[...] = branch.astype(jnp.bfloat16)
    stepped[...] = (tokens[...].astype(jnp.float32) + delta * branch).astype(jnp.bfloat16)


def finish(timestep, mine, theirs, tokens, gate):
    shape = jax.ShapeDtypeStruct(tokens.shape, jnp.bfloat16)
    return pl.pallas_call(
        finish_kernel,
        in_specs=[smem_spec()] + [vmem_spec()] * 4,
        out_specs=[vmem_spec(), vmem_spec()],
        out_shape=[shape, shape],
        compiler_params=pltpu.CompilerParams(vmem_limit_bytes=VMEM_LIMIT),
    )(timestep, mine, theirs, tokens, gate)


def make(mesh):
    chips = mesh.shape["req"]
    colours = chips // 4
    swap = [(0, 1), (1, 0)]
    cross = [(chip, chip ^ 1) for chip in range(chips)]

    def on_device(tokens, video_lengths, timestep, time_weight, block_mod, w_query, w_key, w_value, w_out):
        heads = w_query.shape[1] // HEAD_DIM // 2
        routes = [pairs_out(chips, heads, colour) for colour in range(colours)]
        near = lax.ppermute(tokens, "req", cross)
        other = lax.ppermute(tokens, "tp", swap)
        half_freq = time_weight.shape[0] // 2
        time_value = jnp.broadcast_to(timestep, (half_freq,)).astype(jnp.float32)
        sigma = noise_level(time_value)
        frequency = jnp.exp(-math.log(10000.0) * jnp.arange(half_freq, dtype=jnp.float32) / half_freq)
        angle = 1000.0 * sigma * frequency
        act = jax.nn.silu(jnp.concatenate([jnp.cos(angle), jnp.sin(angle)]))[None, :]
        mine, mod, gate = project(act, block_mod, tokens, other, time_weight, w_query, w_key, w_value)
        near, mine, mod, gate = lax.optimization_barrier((near, mine, mod, gate))
        far = lax.ppermute(near, "tp", swap)
        sent = project_shared(near, far, mod, mine, w_query, w_key, w_value, colours)
        got = [lax.ppermute(piece, ("req", "tp"), route) for piece, route in zip(sent, routes)]
        swapped = [lax.ppermute(piece, "tp", swap) for piece in got]
        done = attend(video_lengths, got, swapped, heads)
        back = [
            lax.ppermute(piece, ("req", "tp"), [(b, a) for a, b in route]) for piece, route in zip(done, routes)
        ]
        keep, give = part(back, heads)
        mine, theirs = combine(keep, lax.ppermute(give, "req", cross), w_out)
        theirs = lax.ppermute(theirs, "tp", swap)
        velocity, stepped = finish(timestep, mine, theirs, tokens, gate)
        return (velocity, stepped)

    return on_device


def solution(mesh):
    return jax.shard_map(
        make(mesh),
        mesh=mesh,
        in_specs=(
            P("req", "tp"), P(), P(), P(), P(), P(None, "tp"), P(None, "tp"), P(None, "tp"), P("tp", None),
        ),
        out_specs=(P("req", "tp"), P("req", "tp")),
        check_vma=False,
    )
```

```python
import functools
import math

import jax
import jax.numpy as jnp
from jax import lax
from jax.experimental import pallas as pl
from jax.experimental.pallas import tpu as pltpu
from jax.sharding import PartitionSpec as P

HEAD_DIM = 128
STEPS = 1000
QUERY_BLOCK = 384
KEY_GROUP = 3072
WINDOWS = (512, 1024, 1536, 2048, 2560)
NEG = -1e30
STREAM_LIMIT = 51 * 1024 * 1024
VMEM_LIMIT = 32 * 1024 * 1024


def noise_level(step_value):
    frac = step_value / STEPS
    return 5.0 * frac / (1.0 + 4.0 * frac)


def turned(colours, side):
    return colours // 2 * (1 - side)


def pairs_out(chips, heads, colour):
    half = chips // 2
    colours = half // 2
    pairs = []
    for chip in range(chips):
        side, x = chip // half, chip % 2
        slot = chip % half // 2 ^ turned(colours, side)
        for core in range(2):
            place = slot ^ colour ^ turned(colours, core)
            if (slot ^ colour) < heads:
                pairs.append((chip * 2 + core, (core * half + place * 2 + x) * 2 + side))
    return pairs


def place_of(colours):
    chip = lax.axis_index("req")
    return lax.rem(chip // 2, colours) ^ turned(colours, chip // (2 * colours)), lax.rem(chip, 2)


def any_spec():
    return pl.BlockSpec(memory_space=pl.ANY)


def vmem_spec():
    return pl.BlockSpec(memory_space=pltpu.VMEM)


def smem_spec():
    return pl.BlockSpec(memory_space=pltpu.SMEM)


def standardise(full, own_ref, other_ref):
    share = own_ref.shape[1]
    core = lax.axis_index("tp")
    full[:, pl.ds(pl.multiple_of(core * share, 128), share)] = own_ref[...].astype(jnp.float32)
    full[:, pl.ds(pl.multiple_of((1 - core) * share, 128), share)] = other_ref[...].astype(jnp.float32)
    whole = full[...]
    centred = whole - jnp.mean(whole, axis=1, keepdims=True)
    variance = jnp.mean(centred * centred, axis=1, keepdims=True)
    return centred * lax.rsqrt(variance + 1e-06)


def project_part(packed, normed, weight, part):
    out = jnp.dot(normed[...], weight, preferred_element_type=jnp.float32)
    if part == 0:
        out = out * (math.log2(math.e) / math.sqrt(HEAD_DIM))
    for head in range(out.shape[1] // HEAD_DIM):
        packed[head, part] = out[:, head * HEAD_DIM:(head + 1) * HEAD_DIM].astype(jnp.bfloat16)


def load_weights(load, refs, weights):
    depth, columns = weights.shape[1:]
    x = lax.rem(lax.axis_index("req"), 2)
    for part, ref in enumerate(refs):
        for cut in range(2):
            here = pl.ds(cut * (depth // 2), depth // 2)
            load(ref.at[here, pl.ds(pl.multiple_of(x * columns, 128), columns)], weights.at[part, here])


def project_kernel(act_ref, block_ref, own_ref, other_ref, time_ref, wq_ref, wk_ref, wv_ref, *rest):
    packed, mod_ref, gate_ref, weights, times, full, normed, sems = rest
    depth = full.shape[1]
    share = own_ref.shape[1]
    freq = times.shape[0]
    core = lax.axis_index("tp")
    loads = []

    def load(source, target):
        loads.append(pltpu.make_async_copy(source, target, sems.at[len(loads)]))
        loads[-1].start()

    for part in range(2):
        here = pl.ds(part * (freq // 2), freq // 2)
        load(time_ref.at[here, pl.ds(0, 2 * depth)], times.at[here, pl.ds(0, 2 * depth)])
    load_weights(load, (wq_ref, wk_ref, wv_ref), weights)
    load(
        time_ref.at[:, pl.ds(pl.multiple_of(2 * depth + core * share, 128), share)],
        times.at[:, pl.ds(2 * depth, share)],
    )
    full[...] = standardise(full, own_ref, other_ref)
    act = jnp.transpose(jnp.broadcast_to(act_ref[...], (8, freq)))[:, :1]
    act = jnp.broadcast_to(act, (freq, HEAD_DIM))

    def modulation(column):
        return jnp.sum(act * times[:, column:column + HEAD_DIM], axis=0, keepdims=True)

    loads[0].wait()
    loads[1].wait()
    for column in range(0, depth, HEAD_DIM):
        here = slice(column, column + HEAD_DIM)
        shift = modulation(column) + block_ref[0:1, here]
        scale = modulation(depth + column) + block_ref[1:2, here]
        mod_ref[0:1, here] = shift
        mod_ref[1:2, here] = scale
        normed[:, here] = (full[:, here] * (1.0 + scale) + shift).astype(jnp.bfloat16)
    for part in range(3):
        loads[2 + 2 * part].wait()
        loads[3 + 2 * part].wait()
        project_part(packed, normed, weights[part], part)
    loads[8].wait()
    for column in range(0, share, HEAD_DIM):
        here = pl.ds(pl.multiple_of(core * share + column, 128), HEAD_DIM)
        gate_ref[:, column:column + HEAD_DIM] = modulation(2 * depth + column) + block_ref[2:3, here]


def project(act, block_mod, own, other, time_weight, w_query, w_key, w_value):
    rows, share = own.shape
    depth, columns = w_query.shape
    columns = columns // 2
    freq = time_weight.shape[0]
    heads = columns // HEAD_DIM
    return pl.pallas_call(
        project_kernel,
        in_specs=[vmem_spec()] * 4 + [any_spec()] * 4,
        out_specs=[vmem_spec()] * 3,
        out_shape=[
            jax.ShapeDtypeStruct((heads, 3, rows, HEAD_DIM), jnp.bfloat16),
            jax.ShapeDtypeStruct((2, depth), jnp.float32),
            jax.ShapeDtypeStruct((1, share), jnp.float32),
        ],
        scratch_shapes=[
            pltpu.VMEM((3, depth, columns), jnp.bfloat16),
            pltpu.VMEM((freq, 2 * depth + share), jnp.float32),
            pltpu.VMEM((rows, depth), jnp.float32),
            pltpu.VMEM((rows, depth), jnp.bfloat16),
            pltpu.SemaphoreType.DMA((9,)),
        ],
        compiler_params=pltpu.CompilerParams(vmem_limit_bytes=STREAM_LIMIT),
        cost_estimate=pl.CostEstimate(flops=6 * rows * depth * columns, bytes_accessed=8 * 2**20, transcendentals=0),
    )(act, block_mod, own, other, time_weight, w_query, w_key, w_value)


def share_kernel(colours, near_ref, far_ref, mod_ref, mine, wq_ref, wk_ref, wv_ref, *rest):
    outs, (weights, full, normed, packed, load_sems, sems) = rest[:colours], rest[colours:]
    heads, _, rows, _ = mine.shape
    loads = []

    def load(source, target):
        loads.append(pltpu.make_async_copy(source, target, load_sems.at[len(loads)]))
        loads[-1].start()

    load_weights(load, (wq_ref, wk_ref, wv_ref), weights)
    slot, x = place_of(colours)

    def each_copy(source, position, offset, act):
        for head in range(heads):
            for colour in range(colours):
                @pl.when((slot ^ colour) == head)
                def _():
                    here = pl.ds(pl.multiple_of(position * rows, 64), rows)
                    act(pltpu.make_async_copy(source.at[head], outs[colour].at[:, here], sems.at[offset + head]))

    each_copy(mine, x, 0, lambda copy: copy.start())
    scaled = standardise(full, near_ref, far_ref)
    normed[...] = (scaled * (1.0 + mod_ref[1:2, :]) + mod_ref[0:1, :]).astype(jnp.bfloat16)
    for part in range(3):
        loads[2 * part].wait()
        loads[2 * part + 1].wait()
        project_part(packed, normed, weights[part], part)
    each_copy(packed, 1 - x, heads, lambda copy: copy.start())
    each_copy(mine, x, 0, lambda copy: copy.wait())
    each_copy(packed, 1 - x, heads, lambda copy: copy.wait())


def project_shared(near, far, mod, mine, w_query, w_key, w_value, colours):
    heads, _, rows, _ = mine.shape
    depth = mod.shape[1]
    return pl.pallas_call(
        functools.partial(share_kernel, colours),
        in_specs=[vmem_spec()] * 3 + [any_spec()] * 4,
        out_specs=[any_spec()] * colours,
        out_shape=[jax.ShapeDtypeStruct((3, 2 * rows, HEAD_DIM), jnp.bfloat16)] * colours,
        scratch_shapes=[
            pltpu.VMEM((3, depth, heads * HEAD_DIM), jnp.bfloat16),
            pltpu.VMEM((rows, depth), jnp.float32),
            pltpu.VMEM((rows, depth), jnp.bfloat16),
            pltpu.VMEM(mine.shape, jnp.bfloat16),
            pltpu.SemaphoreType.DMA((6,)),
            pltpu.SemaphoreType.DMA((2 * heads,)),
        ],
        compiler_params=pltpu.CompilerParams(vmem_limit_bytes=STREAM_LIMIT),
    )(near, far, mod, mine, w_query, w_key, w_value)


def attend_kernel(colours, heads, lengths_ref, *refs):
    pieces, swapped, outs = refs[:colours], refs[colours:2 * colours], refs[2 * colours:3 * colours]
    query, keys, values, result, top, total, sems, out_sems = refs[3 * colours:]
    rows = pieces[0].shape[1]
    own_rows, all_rows = query.shape[0], keys.shape[0]
    side = lax.axis_index("tp")
    slot, _ = place_of(colours)
    front = pl.ds(0, HEAD_DIM)
    videos = lengths_ref.shape[0]

    def at(colour, which, whole):
        place = slot ^ colour ^ turned(colours, which)
        return pl.ds(pl.multiple_of(place * rows + (which * own_rows if whole else 0), 128), rows)

    def each_copy(act):
        for colour in range(colours):
            near, far = pieces[colour], swapped[colour]
            for number, (source, target) in enumerate((
                (near.at[0], query.at[at(colour, side, False), front]),
                (near.at[1], keys.at[at(colour, side, True), front]),
                (near.at[2], values.at[at(colour, side, True), front]),
                (far.at[1], keys.at[at(colour, 1 - side, True), front]),
                (far.at[2], values.at[at(colour, 1 - side, True), front]),
            )):
                act(pltpu.make_async_copy(source, target, sems.at[5 * colour + number]))

    @pl.when(slot < heads)
    def _():
        each_copy(lambda copy: copy.start())
        ends, end = [], jnp.int32(0)
        for video in range(videos):
            end = end + lengths_ref[video]
            ends.append(end)
        starts = [jnp.int32(0)] + ends[:-1]
        lane = lax.broadcasted_iota(jnp.int32, (1, HEAD_DIM), 1)
        lane_start = jnp.zeros((1, HEAD_DIM), jnp.int32)
        lane_stop = jnp.zeros((1, HEAD_DIM), jnp.int32)
        for video, (start, stop) in enumerate(zip(starts, ends)):
            lane_start = jnp.where(lane == video, start, lane_start)
            lane_stop = jnp.where(lane == video, stop, lane_stop)
        place = lax.broadcasted_iota(jnp.int32, (HEAD_DIM, HEAD_DIM), 0)

        def inside(first):
            index = first + place
            return (index >= lane_start) & (index < lane_stop)

        def fill_query(block, carry):
            local = pl.multiple_of(block * HEAD_DIM, HEAD_DIM)
            member = inside(side * own_rows + local)
            query[pl.ds(local, HEAD_DIM), HEAD_DIM:] = jnp.where(member, 1.0, 0.0).astype(jnp.bfloat16)
            return carry

        def fill_keys(block, carry):
            begin = pl.multiple_of(block * HEAD_DIM, HEAD_DIM)
            keys[pl.ds(begin, HEAD_DIM), HEAD_DIM:] = jnp.where(
                inside(begin) | (lane >= videos), 0.0, NEG
            ).astype(jnp.bfloat16)
            values[pl.ds(begin, HEAD_DIM), HEAD_DIM:] = jnp.ones((HEAD_DIM, HEAD_DIM), jnp.bfloat16)
            return carry

        lax.fori_loop(0, own_rows // HEAD_DIM, fill_query, 0)
        lax.fori_loop(0, all_rows // HEAD_DIM, fill_keys, 0)
        each_copy(lambda copy: copy.wait())

        sub = QUERY_BLOCK // 2

        def query_block(block, carry):
            local = pl.multiple_of(block * QUERY_BLOCK, QUERY_BLOCK)
            first = side * own_rows + local
            last = first + QUERY_BLOCK - 1
            low, high = jnp.int32(0), jnp.int32(0)
            for start, stop in zip(starts, ends):
                low = jnp.where(first >= start, start, low)
                high = jnp.where(last >= start, stop, high)
            low = low // HEAD_DIM * HEAD_DIM

            def scores(offset, begin, count):
                q = query[pl.ds(pl.multiple_of(local + offset, 64), sub), :]
                score = lax.dot_general(
                    q, keys[pl.ds(begin, count), :], (((1,), (1,)), ((), ())), preferred_element_type=jnp.float32
                )
                tiles = [score[:, j:j + HEAD_DIM] for j in range(0, count, HEAD_DIM)]
                most = jnp.max(functools.reduce(jnp.maximum, tiles), axis=1, keepdims=True)
                return tiles, jnp.broadcast_to(most, (sub, HEAD_DIM))

            def weigh(begin, count, tiles, now):
                probs = jnp.concatenate([jnp.exp2(tile - now).astype(jnp.bfloat16) for tile in tiles], axis=1)
                return jnp.dot(probs, values[pl.ds(begin, count), :], preferred_element_type=jnp.float32)

            def store(offset, update):
                out = update[:, :HEAD_DIM] / update[:, HEAD_DIM:]
                result[pl.ds(pl.multiple_of(local + offset, 64), sub), :] = out.astype(jnp.bfloat16)

            def window(count):
                begin = pl.multiple_of(jnp.minimum(low, all_rows - count), HEAD_DIM)
                tiles, now = scores(0, begin, count)
                for offset in range(0, QUERY_BLOCK, sub):
                    later = scores(offset + sub, begin, count) if offset + sub < QUERY_BLOCK else None
                    store(offset, weigh(begin, count, tiles, now))
                    if later is not None:
                        tiles, now = later

            def long(offset):
                top[...] = jnp.full(top.shape, 2 * NEG, jnp.float32)
                total[...] = jnp.zeros(total.shape, jnp.float32)

                def key_block(number, carry):
                    begin = pl.multiple_of(number * KEY_GROUP, KEY_GROUP)
                    tiles, most = scores(offset, begin, KEY_GROUP)
                    before = top[...]
                    now = jnp.maximum(before, most)
                    update = weigh(begin, KEY_GROUP, tiles, now)
                    shrink = jnp.exp2(before - now)
                    total[:, :HEAD_DIM] = total[:, :HEAD_DIM] * shrink + update[:, :HEAD_DIM]
                    total[:, HEAD_DIM:] = total[:, HEAD_DIM:] * shrink + update[:, HEAD_DIM:]
                    top[...] = now
                    return carry

                lax.fori_loop(low // KEY_GROUP, (high + KEY_GROUP - 1) // KEY_GROUP, key_block, 0)
                store(offset, total)

            need = high - low
            floor = 0
            for count in WINDOWS:
                pl.when((need > floor) & (need <= count))(functools.partial(window, count))
                floor = count

            @pl.when(need > floor)
            def _():
                if all_rows == KEY_GROUP:
                    window(KEY_GROUP)
                else:
                    for offset in range(0, QUERY_BLOCK, sub):
                        long(offset)

            return carry

        lax.fori_loop(0, own_rows // QUERY_BLOCK, query_block, 0)
        copies = [
            pltpu.make_async_copy(result.at[at(colour, side, False)], outs[colour], out_sems.at[colour])
            for colour in range(colours)
        ]
        for copy in copies:
            copy.start()
        for copy in copies:
            copy.wait()


def attend(lengths, pieces, swapped, heads):
    rows = pieces[0].shape[1]
    colours = len(pieces)
    own = colours * rows
    return pl.pallas_call(
        functools.partial(attend_kernel, colours, heads),
        in_specs=[smem_spec()] + [any_spec()] * (2 * colours),
        out_specs=[any_spec()] * colours,
        out_shape=[jax.ShapeDtypeStruct((rows, HEAD_DIM), jnp.bfloat16)] * colours,
        scratch_shapes=[
            pltpu.VMEM((own, 2 * HEAD_DIM), jnp.bfloat16),
            pltpu.VMEM((2 * own, 2 * HEAD_DIM), jnp.bfloat16),
            pltpu.VMEM((2 * own, 2 * HEAD_DIM), jnp.bfloat16),
            pltpu.VMEM((own, HEAD_DIM), jnp.bfloat16),
            pltpu.VMEM((QUERY_BLOCK // 2, HEAD_DIM), jnp.float32),
            pltpu.VMEM((QUERY_BLOCK // 2, 2 * HEAD_DIM), jnp.float32),
            pltpu.SemaphoreType.DMA((5 * colours,)),
            pltpu.SemaphoreType.DMA((colours,)),
        ],
        compiler_params=pltpu.CompilerParams(vmem_limit_bytes=VMEM_LIMIT),
    )(lengths, *pieces, *swapped)


def part_kernel(colours, *refs):
    pieces, (keep, give, sems) = refs[:colours], refs[colours:]
    heads, rows, _ = keep.shape
    slot, x = place_of(colours)

    def each_copy(act):
        for head in range(heads):
            for number, (target, position) in enumerate(((give, 1 - x), (keep, x))):
                here = pl.ds(pl.multiple_of(position * rows, 64), rows)
                for colour in range(colours):
                    @pl.when((slot ^ colour) == head)
                    def _():
                        source = pieces[colour].at[here]
                        act(pltpu.make_async_copy(source, target.at[head], sems.at[2 * head + number]))

    each_copy(lambda copy: copy.start())
    each_copy(lambda copy: copy.wait())


def part(pieces, heads):
    rows = pieces[0].shape[0] // 2
    shape = jax.ShapeDtypeStruct((heads, rows, HEAD_DIM), jnp.bfloat16)
    return pl.pallas_call(
        functools.partial(part_kernel, len(pieces)),
        in_specs=[any_spec()] * len(pieces),
        out_specs=[any_spec()] * 2,
        out_shape=[shape, shape],
        scratch_shapes=[pltpu.SemaphoreType.DMA((2 * heads,))],
        compiler_params=pltpu.CompilerParams(vmem_limit_bytes=VMEM_LIMIT),
    )(*pieces)


def combine_kernel(keep_ref, got_ref, weight, mine, theirs, attended, sems):
    share = mine.shape[1]
    heads = keep_ref.shape[0]
    core = lax.axis_index("tp")
    x = lax.rem(lax.axis_index("req"), 2)
    copies = []
    for head in range(heads):
        for source, which in ((keep_ref, x), (got_ref, 1 - x)):
            columns = pl.ds(pl.multiple_of((which * heads + head) * HEAD_DIM, HEAD_DIM), HEAD_DIM)
            copies.append(pltpu.make_async_copy(source.at[head], attended.at[:, columns], sems.at[len(copies)]))
            copies[-1].start()
    for copy in copies:
        copy.wait()
    left = attended[...]
    for out, where in ((theirs, 1 - core), (mine, core)):
        columns = pl.ds(pl.multiple_of(where * share, 128), share)
        out[...] = jnp.dot(left, weight[:, columns], preferred_element_type=jnp.float32).astype(out.dtype)


def combine(keep, got, w_out):
    heads, rows, _ = keep.shape
    depth, width = w_out.shape
    return pl.pallas_call(
        combine_kernel,
        in_specs=[any_spec()] * 2 + [vmem_spec()],
        out_specs=[vmem_spec(), vmem_spec()],
        out_shape=[
            jax.ShapeDtypeStruct((rows, width // 2), jnp.float32),
            jax.ShapeDtypeStruct((rows, width // 2), jnp.bfloat16),
        ],
        scratch_shapes=[
            pltpu.VMEM((rows, depth), jnp.bfloat16),
            pltpu.SemaphoreType.DMA((2 * heads,)),
        ],
        compiler_params=pltpu.CompilerParams(vmem_limit_bytes=VMEM_LIMIT),
    )(keep, got, w_out)


def finish_kernel(timestep_ref, mine, theirs, tokens, gate_ref, velocity, stepped):
    step_value = jnp.full((1, 128), timestep_ref[0], jnp.int32).astype(jnp.float32)
    delta = (noise_level(step_value - 1.0) - noise_level(step_value))[:, :1]
    branch = gate_ref[...] * (mine[...] + theirs[...].astype(jnp.float32))
    velocity[...] = branch.astype(jnp.bfloat16)
    stepped[...] = (tokens[...].astype(jnp.float32) + delta * branch).astype(jnp.bfloat16)


def finish(timestep, mine, theirs, tokens, gate):
    shape = jax.ShapeDtypeStruct(tokens.shape, jnp.bfloat16)
    return pl.pallas_call(
        finish_kernel,
        in_specs=[smem_spec()] + [vmem_spec()] * 4,
        out_specs=[vmem_spec(), vmem_spec()],
        out_shape=[shape, shape],
        compiler_params=pltpu.CompilerParams(vmem_limit_bytes=VMEM_LIMIT),
    )(timestep, mine, theirs, tokens, gate)


def make(mesh):
    chips = mesh.shape["req"]
    colours = chips // 4
    swap = [(0, 1), (1, 0)]
    cross = [(chip, chip ^ 1) for chip in range(chips)]

    def on_device(tokens, video_lengths, timestep, time_weight, block_mod, w_query, w_key, w_value, w_out):
        heads = w_query.shape[1] // HEAD_DIM // 2
        routes = [pairs_out(chips, heads, colour) for colour in range(colours)]
        near = lax.ppermute(tokens, "req", cross)
        other = lax.ppermute(tokens, "tp", swap)
        half_freq = time_weight.shape[0] // 2
        time_value = jnp.broadcast_to(timestep, (half_freq,)).astype(jnp.float32)
        sigma = noise_level(time_value)
        frequency = jnp.exp(-math.log(10000.0) * jnp.arange(half_freq, dtype=jnp.float32) / half_freq)
        angle = 1000.0 * sigma * frequency
        act = jax.nn.silu(jnp.concatenate([jnp.cos(angle), jnp.sin(angle)]))[None, :]
        mine, mod, gate = project(act, block_mod, tokens, other, time_weight, w_query, w_key, w_value)
        near, mine, mod, gate = lax.optimization_barrier((near, mine, mod, gate))
        far = lax.ppermute(near, "tp", swap)
        sent = project_shared(near, far, mod, mine, w_query, w_key, w_value, colours)
        got = [lax.ppermute(piece, ("req", "tp"), route) for piece, route in zip(sent, routes)]
        swapped = [lax.ppermute(piece, "tp", swap) for piece in got]
        done = attend(video_lengths, got, swapped, heads)
        back = [
            lax.ppermute(piece, ("req", "tp"), [(b, a) for a, b in route]) for piece, route in zip(done, routes)
        ]
        keep, give = part(back, heads)
        mine, theirs = combine(keep, lax.ppermute(give, "req", cross), w_out)
        theirs = lax.ppermute(theirs, "tp", swap)
        velocity, stepped = finish(timestep, mine, theirs, tokens, gate)
        return (velocity, stepped)

    return on_device


def solution(mesh):
    return jax.shard_map(
        make(mesh),
        mesh=mesh,
        in_specs=(
            P("req", "tp"), P(), P(), P(), P(), P(None, "tp"), P(None, "tp"), P(None, "tp"), P("tp", None),
        ),
        out_specs=(P("req", "tp"), P("req", "tp")),
        check_vma=False,
    )
```

```python
import functools
import math

import jax
import jax.numpy as jnp
from jax import lax
from jax.experimental import pallas as pl
from jax.experimental.pallas import tpu as pltpu
from jax.sharding import PartitionSpec as P

HEAD_DIM = 128
STEPS = 1000
QUERY_BLOCK = 384
KEY_GROUP = 3072
WINDOWS = (512, 1024, 1536, 2048, 2560)
NEG = -1e30
STREAM_LIMIT = 51 * 1024 * 1024
VMEM_LIMIT = 32 * 1024 * 1024


def noise_level(step_value):
    frac = step_value / STEPS
    return 5.0 * frac / (1.0 + 4.0 * frac)


def turned(colours, side):
    return colours // 2 * (1 - side)


def pairs_out(chips, heads, colour):
    half = chips // 2
    colours = half // 2
    pairs = []
    for chip in range(chips):
        side, x = chip // half, chip % 2
        slot = chip % half // 2 ^ turned(colours, side)
        for core in range(2):
            place = slot ^ colour ^ turned(colours, core)
            if (slot ^ colour) < heads:
                pairs.append((chip * 2 + core, (core * half + place * 2 + x) * 2 + side))
    return pairs


def place_of(colours):
    chip = lax.axis_index("req")
    return lax.rem(chip // 2, colours) ^ turned(colours, chip // (2 * colours)), lax.rem(chip, 2)


def any_spec():
    return pl.BlockSpec(memory_space=pl.ANY)


def vmem_spec():
    return pl.BlockSpec(memory_space=pltpu.VMEM)


def smem_spec():
    return pl.BlockSpec(memory_space=pltpu.SMEM)


def standardise(full, own_ref, other_ref):
    share = own_ref.shape[1]
    core = lax.axis_index("tp")
    full[:, pl.ds(pl.multiple_of(core * share, 128), share)] = own_ref[...].astype(jnp.float32)
    full[:, pl.ds(pl.multiple_of((1 - core) * share, 128), share)] = other_ref[...].astype(jnp.float32)
    whole = full[...]
    centred = whole - jnp.mean(whole, axis=1, keepdims=True)
    variance = jnp.mean(centred * centred, axis=1, keepdims=True)
    return centred * lax.rsqrt(variance + 1e-06)


def project_part(packed, normed, weight, part):
    out = jnp.dot(normed[...], weight, preferred_element_type=jnp.float32)
    if part == 0:
        out = out * (math.log2(math.e) / math.sqrt(HEAD_DIM))
    for head in range(out.shape[1] // HEAD_DIM):
        packed[head, part] = out[:, head * HEAD_DIM:(head + 1) * HEAD_DIM].astype(jnp.bfloat16)


def load_weights(load, refs, weights):
    depth, columns = weights.shape[1:]
    x = lax.rem(lax.axis_index("req"), 2)
    for part, ref in enumerate(refs):
        for cut in range(2):
            here = pl.ds(cut * (depth // 2), depth // 2)
            load(ref.at[here, pl.ds(pl.multiple_of(x * columns, 128), columns)], weights.at[part, here])


def project_kernel(act_ref, block_ref, own_ref, other_ref, time_ref, wq_ref, wk_ref, wv_ref, *rest):
    packed, mod_ref, gate_ref, weights, times, full, normed, sems = rest
    depth = full.shape[1]
    share = own_ref.shape[1]
    freq = times.shape[0]
    core = lax.axis_index("tp")
    loads = []

    def load(source, target):
        loads.append(pltpu.make_async_copy(source, target, sems.at[len(loads)]))
        loads[-1].start()

    for part in range(2):
        here = pl.ds(part * (freq // 2), freq // 2)
        load(time_ref.at[here, pl.ds(0, 2 * depth)], times.at[here, pl.ds(0, 2 * depth)])
    load_weights(load, (wq_ref, wk_ref, wv_ref), weights)
    load(
        time_ref.at[:, pl.ds(pl.multiple_of(2 * depth + core * share, 128), share)],
        times.at[:, pl.ds(2 * depth, share)],
    )
    full[...] = standardise(full, own_ref, other_ref)
    act = jnp.transpose(jnp.broadcast_to(act_ref[...], (8, freq)))[:, :1]
    act = jnp.broadcast_to(act, (freq, HEAD_DIM))

    def modulation(column):
        return jnp.sum(act * times[:, column:column + HEAD_DIM], axis=0, keepdims=True)

    loads[0].wait()
    loads[1].wait()
    for column in range(0, depth, HEAD_DIM):
        here = slice(column, column + HEAD_DIM)
        shift = modulation(column) + block_ref[0:1, here]
        scale = modulation(depth + column) + block_ref[1:2, here]
        mod_ref[0:1, here] = shift
        mod_ref[1:2, here] = scale
        normed[:, here] = (full[:, here] * (1.0 + scale) + shift).astype(jnp.bfloat16)
    for part in range(3):
        loads[2 + 2 * part].wait()
        loads[3 + 2 * part].wait()
        project_part(packed, normed, weights[part], part)
    loads[8].wait()
    for column in range(0, share, HEAD_DIM):
        here = pl.ds(pl.multiple_of(core * share + column, 128), HEAD_DIM)
        gate_ref[:, column:column + HEAD_DIM] = modulation(2 * depth + column) + block_ref[2:3, here]


def project(act, block_mod, own, other, time_weight, w_query, w_key, w_value):
    rows, share = own.shape
    depth, columns = w_query.shape
    columns = columns // 2
    freq = time_weight.shape[0]
    heads = columns // HEAD_DIM
    return pl.pallas_call(
        project_kernel,
        in_specs=[vmem_spec()] * 4 + [any_spec()] * 4,
        out_specs=[vmem_spec()] * 3,
        out_shape=[
            jax.ShapeDtypeStruct((heads, 3, rows, HEAD_DIM), jnp.bfloat16),
            jax.ShapeDtypeStruct((2, depth), jnp.float32),
            jax.ShapeDtypeStruct((1, share), jnp.float32),
        ],
        scratch_shapes=[
            pltpu.VMEM((3, depth, columns), jnp.bfloat16),
            pltpu.VMEM((freq, 2 * depth + share), jnp.float32),
            pltpu.VMEM((rows, depth), jnp.float32),
            pltpu.VMEM((rows, depth), jnp.bfloat16),
            pltpu.SemaphoreType.DMA((9,)),
        ],
        compiler_params=pltpu.CompilerParams(vmem_limit_bytes=STREAM_LIMIT),
        cost_estimate=pl.CostEstimate(flops=6 * rows * depth * columns, bytes_accessed=8 * 2**20, transcendentals=0),
    )(act, block_mod, own, other, time_weight, w_query, w_key, w_value)


def share_kernel(colours, near_ref, far_ref, mod_ref, mine, wq_ref, wk_ref, wv_ref, *rest):
    outs, (full, normed, packed, sems) = rest[:colours], rest[colours:]
    heads, _, rows, _ = mine.shape
    slot, x = place_of(colours)

    def each_copy(source, position, offset, act):
        for head in range(heads):
            for colour in range(colours):
                @pl.when((slot ^ colour) == head)
                def _():
                    here = pl.ds(pl.multiple_of(position * rows, 64), rows)
                    act(pltpu.make_async_copy(source.at[head], outs[colour].at[:, here], sems.at[offset + head]))

    each_copy(mine, x, 0, lambda copy: copy.start())
    scaled = standardise(full, near_ref, far_ref)
    normed[...] = (scaled * (1.0 + mod_ref[1:2, :]) + mod_ref[0:1, :]).astype(jnp.bfloat16)
    columns = pl.ds(pl.multiple_of(x * heads * HEAD_DIM, HEAD_DIM), heads * HEAD_DIM)
    for part, ref in enumerate((wq_ref, wk_ref, wv_ref)):
        project_part(packed, normed, ref[:, columns], part)
    each_copy(packed, 1 - x, heads, lambda copy: copy.start())
    each_copy(mine, x, 0, lambda copy: copy.wait())
    each_copy(packed, 1 - x, heads, lambda copy: copy.wait())


def project_shared(near, far, mod, mine, w_query, w_key, w_value, colours):
    heads, _, rows, _ = mine.shape
    depth = mod.shape[1]
    return pl.pallas_call(
        functools.partial(share_kernel, colours),
        in_specs=[vmem_spec()] * 3 + [any_spec()] + [vmem_spec()] * 3,
        out_specs=[any_spec()] * colours,
        out_shape=[jax.ShapeDtypeStruct((3, 2 * rows, HEAD_DIM), jnp.bfloat16)] * colours,
        scratch_shapes=[
            pltpu.VMEM((rows, depth), jnp.float32),
            pltpu.VMEM((rows, depth), jnp.bfloat16),
            pltpu.VMEM(mine.shape, jnp.bfloat16),
            pltpu.SemaphoreType.DMA((2 * heads,)),
        ],
        compiler_params=pltpu.CompilerParams(vmem_limit_bytes=VMEM_LIMIT),
    )(near, far, mod, mine, w_query, w_key, w_value)


def attend_kernel(colours, heads, lengths_ref, *refs):
    pieces, swapped, outs = refs[:colours], refs[colours:2 * colours], refs[2 * colours:3 * colours]
    query, keys, values, result, top, total, sems, out_sems = refs[3 * colours:]
    rows = pieces[0].shape[1]
    own_rows, all_rows = query.shape[0], keys.shape[0]
    side = lax.axis_index("tp")
    slot, _ = place_of(colours)
    front = pl.ds(0, HEAD_DIM)
    videos = lengths_ref.shape[0]

    def at(colour, which, whole):
        place = slot ^ colour ^ turned(colours, which)
        return pl.ds(pl.multiple_of(place * rows + (which * own_rows if whole else 0), 128), rows)

    def each_copy(act):
        for colour in range(colours):
            near, far = pieces[colour], swapped[colour]
            for number, (source, target) in enumerate((
                (near.at[0], query.at[at(colour, side, False), front]),
                (near.at[1], keys.at[at(colour, side, True), front]),
                (near.at[2], values.at[at(colour, side, True), front]),
                (far.at[1], keys.at[at(colour, 1 - side, True), front]),
                (far.at[2], values.at[at(colour, 1 - side, True), front]),
            )):
                act(pltpu.make_async_copy(source, target, sems.at[5 * colour + number]))

    @pl.when(slot < heads)
    def _():
        each_copy(lambda copy: copy.start())
        ends, end = [], jnp.int32(0)
        for video in range(videos):
            end = end + lengths_ref[video]
            ends.append(end)
        starts = [jnp.int32(0)] + ends[:-1]
        lane = lax.broadcasted_iota(jnp.int32, (1, HEAD_DIM), 1)
        lane_start = jnp.zeros((1, HEAD_DIM), jnp.int32)
        lane_stop = jnp.zeros((1, HEAD_DIM), jnp.int32)
        for video, (start, stop) in enumerate(zip(starts, ends)):
            lane_start = jnp.where(lane == video, start, lane_start)
            lane_stop = jnp.where(lane == video, stop, lane_stop)
        place = lax.broadcasted_iota(jnp.int32, (HEAD_DIM, HEAD_DIM), 0)

        def inside(first):
            index = first + place
            return (index >= lane_start) & (index < lane_stop)

        def fill_query(block, carry):
            local = pl.multiple_of(block * HEAD_DIM, HEAD_DIM)
            member = inside(side * own_rows + local)
            query[pl.ds(local, HEAD_DIM), HEAD_DIM:] = jnp.where(member, 1.0, 0.0).astype(jnp.bfloat16)
            return carry

        def fill_keys(block, carry):
            begin = pl.multiple_of(block * HEAD_DIM, HEAD_DIM)
            keys[pl.ds(begin, HEAD_DIM), HEAD_DIM:] = jnp.where(
                inside(begin) | (lane >= videos), 0.0, NEG
            ).astype(jnp.bfloat16)
            values[pl.ds(begin, HEAD_DIM), HEAD_DIM:] = jnp.ones((HEAD_DIM, HEAD_DIM), jnp.bfloat16)
            return carry

        lax.fori_loop(0, own_rows // HEAD_DIM, fill_query, 0)
        lax.fori_loop(0, all_rows // HEAD_DIM, fill_keys, 0)
        each_copy(lambda copy: copy.wait())

        sub = QUERY_BLOCK // 2

        def query_block(block, carry):
            local = pl.multiple_of(block * QUERY_BLOCK, QUERY_BLOCK)
            first = side * own_rows + local
            last = first + QUERY_BLOCK - 1
            low, high = jnp.int32(0), jnp.int32(0)
            for start, stop in zip(starts, ends):
                low = jnp.where(first >= start, start, low)
                high = jnp.where(last >= start, stop, high)
            low = low // HEAD_DIM * HEAD_DIM

            def scores(offset, begin, count):
                q = query[pl.ds(pl.multiple_of(local + offset, 64), sub), :]
                score = lax.dot_general(
                    q, keys[pl.ds(begin, count), :], (((1,), (1,)), ((), ())), preferred_element_type=jnp.float32
                )
                tiles = [score[:, j:j + HEAD_DIM] for j in range(0, count, HEAD_DIM)]
                most = jnp.max(functools.reduce(jnp.maximum, tiles), axis=1, keepdims=True)
                return tiles, jnp.broadcast_to(most, (sub, HEAD_DIM))

            def weigh(begin, count, tiles, now):
                probs = jnp.concatenate([jnp.exp2(tile - now).astype(jnp.bfloat16) for tile in tiles], axis=1)
                return jnp.dot(probs, values[pl.ds(begin, count), :], preferred_element_type=jnp.float32)

            def store(offset, update):
                out = update[:, :HEAD_DIM] / update[:, HEAD_DIM:]
                result[pl.ds(pl.multiple_of(local + offset, 64), sub), :] = out.astype(jnp.bfloat16)

            def window(count):
                begin = pl.multiple_of(jnp.minimum(low, all_rows - count), HEAD_DIM)
                tiles, now = scores(0, begin, count)
                for offset in range(0, QUERY_BLOCK, sub):
                    later = scores(offset + sub, begin, count) if offset + sub < QUERY_BLOCK else None
                    store(offset, weigh(begin, count, tiles, now))
                    if later is not None:
                        tiles, now = later

            def long(offset):
                top[...] = jnp.full(top.shape, 2 * NEG, jnp.float32)
                total[...] = jnp.zeros(total.shape, jnp.float32)

                def key_block(number, carry):
                    begin = pl.multiple_of(number * KEY_GROUP, KEY_GROUP)
                    tiles, most = scores(offset, begin, KEY_GROUP)
                    before = top[...]
                    now = jnp.maximum(before, most)
                    update = weigh(begin, KEY_GROUP, tiles, now)
                    shrink = jnp.exp2(before - now)
                    total[:, :HEAD_DIM] = total[:, :HEAD_DIM] * shrink + update[:, :HEAD_DIM]
                    total[:, HEAD_DIM:] = total[:, HEAD_DIM:] * shrink + update[:, HEAD_DIM:]
                    top[...] = now
                    return carry

                lax.fori_loop(low // KEY_GROUP, (high + KEY_GROUP - 1) // KEY_GROUP, key_block, 0)
                store(offset, total)

            need = high - low
            floor = 0
            for count in WINDOWS:
                pl.when((need > floor) & (need <= count))(functools.partial(window, count))
                floor = count

            @pl.when(need > floor)
            def _():
                if all_rows == KEY_GROUP:
                    window(KEY_GROUP)
                else:
                    for offset in range(0, QUERY_BLOCK, sub):
                        long(offset)

            return carry

        lax.fori_loop(0, own_rows // QUERY_BLOCK, query_block, 0)
        copies = [
            pltpu.make_async_copy(result.at[at(colour, side, False)], outs[colour], out_sems.at[colour])
            for colour in range(colours)
        ]
        for copy in copies:
            copy.start()
        for copy in copies:
            copy.wait()


def attend(lengths, pieces, swapped, heads):
    rows = pieces[0].shape[1]
    colours = len(pieces)
    own = colours * rows
    return pl.pallas_call(
        functools.partial(attend_kernel, colours, heads),
        in_specs=[smem_spec()] + [any_spec()] * (2 * colours),
        out_specs=[any_spec()] * colours,
        out_shape=[jax.ShapeDtypeStruct((rows, HEAD_DIM), jnp.bfloat16)] * colours,
        scratch_shapes=[
            pltpu.VMEM((own, 2 * HEAD_DIM), jnp.bfloat16),
            pltpu.VMEM((2 * own, 2 * HEAD_DIM), jnp.bfloat16),
            pltpu.VMEM((2 * own, 2 * HEAD_DIM), jnp.bfloat16),
            pltpu.VMEM((own, HEAD_DIM), jnp.bfloat16),
            pltpu.VMEM((QUERY_BLOCK // 2, HEAD_DIM), jnp.float32),
            pltpu.VMEM((QUERY_BLOCK // 2, 2 * HEAD_DIM), jnp.float32),
            pltpu.SemaphoreType.DMA((5 * colours,)),
            pltpu.SemaphoreType.DMA((colours,)),
        ],
        compiler_params=pltpu.CompilerParams(vmem_limit_bytes=VMEM_LIMIT),
    )(lengths, *pieces, *swapped)


def part_kernel(colours, *refs):
    pieces, (keep, give, sems) = refs[:colours], refs[colours:]
    heads, rows, _ = keep.shape
    slot, x = place_of(colours)

    def each_copy(act):
        for head in range(heads):
            for number, (target, position) in enumerate(((give, 1 - x), (keep, x))):
                here = pl.ds(pl.multiple_of(position * rows, 64), rows)
                for colour in range(colours):
                    @pl.when((slot ^ colour) == head)
                    def _():
                        source = pieces[colour].at[here]
                        act(pltpu.make_async_copy(source, target.at[head], sems.at[2 * head + number]))

    each_copy(lambda copy: copy.start())
    each_copy(lambda copy: copy.wait())


def part(pieces, heads):
    rows = pieces[0].shape[0] // 2
    shape = jax.ShapeDtypeStruct((heads, rows, HEAD_DIM), jnp.bfloat16)
    return pl.pallas_call(
        functools.partial(part_kernel, len(pieces)),
        in_specs=[any_spec()] * len(pieces),
        out_specs=[any_spec()] * 2,
        out_shape=[shape, shape],
        scratch_shapes=[pltpu.SemaphoreType.DMA((2 * heads,))],
        compiler_params=pltpu.CompilerParams(vmem_limit_bytes=VMEM_LIMIT),
    )(*pieces)


def combine_kernel(keep_ref, got_ref, weight, mine, theirs, attended, sems):
    share = mine.shape[1]
    heads = keep_ref.shape[0]
    core = lax.axis_index("tp")
    x = lax.rem(lax.axis_index("req"), 2)
    copies = []
    for head in range(heads):
        for source, which in ((keep_ref, x), (got_ref, 1 - x)):
            columns = pl.ds(pl.multiple_of((which * heads + head) * HEAD_DIM, HEAD_DIM), HEAD_DIM)
            copies.append(pltpu.make_async_copy(source.at[head], attended.at[:, columns], sems.at[len(copies)]))
            copies[-1].start()
    for copy in copies:
        copy.wait()
    left = attended[...]
    for out, where in ((theirs, 1 - core), (mine, core)):
        columns = pl.ds(pl.multiple_of(where * share, 128), share)
        out[...] = jnp.dot(left, weight[:, columns], preferred_element_type=jnp.float32).astype(out.dtype)


def combine(keep, got, w_out):
    heads, rows, _ = keep.shape
    depth, width = w_out.shape
    return pl.pallas_call(
        combine_kernel,
        in_specs=[any_spec()] * 2 + [vmem_spec()],
        out_specs=[vmem_spec(), vmem_spec()],
        out_shape=[
            jax.ShapeDtypeStruct((rows, width // 2), jnp.float32),
            jax.ShapeDtypeStruct((rows, width // 2), jnp.bfloat16),
        ],
        scratch_shapes=[
            pltpu.VMEM((rows, depth), jnp.bfloat16),
            pltpu.SemaphoreType.DMA((2 * heads,)),
        ],
        compiler_params=pltpu.CompilerParams(vmem_limit_bytes=VMEM_LIMIT),
    )(keep, got, w_out)


def finish_kernel(timestep_ref, mine, theirs, tokens, gate_ref, velocity, stepped):
    step_value = jnp.full((1, 128), timestep_ref[0], jnp.int32).astype(jnp.float32)
    delta = (noise_level(step_value - 1.0) - noise_level(step_value))[:, :1]
    branch = gate_ref[...] * (mine[...] + theirs[...].astype(jnp.float32))
    velocity[...] = branch.astype(jnp.bfloat16)
    stepped[...] = (tokens[...].astype(jnp.float32) + delta * branch).astype(jnp.bfloat16)


def finish(timestep, mine, theirs, tokens, gate):
    shape = jax.ShapeDtypeStruct(tokens.shape, jnp.bfloat16)
    return pl.pallas_call(
        finish_kernel,
        in_specs=[smem_spec()] + [vmem_spec()] * 4,
        out_specs=[vmem_spec(), vmem_spec()],
        out_shape=[shape, shape],
        compiler_params=pltpu.CompilerParams(vmem_limit_bytes=VMEM_LIMIT),
    )(timestep, mine, theirs, tokens, gate)


def make(mesh):
    chips = mesh.shape["req"]
    colours = chips // 4
    swap = [(0, 1), (1, 0)]
    cross = [(chip, chip ^ 1) for chip in range(chips)]

    def on_device(tokens, video_lengths, timestep, time_weight, block_mod, w_query, w_key, w_value, w_out):
        heads = w_query.shape[1] // HEAD_DIM // 2
        routes = [pairs_out(chips, heads, colour) for colour in range(colours)]
        near = lax.ppermute(tokens, "req", cross)
        other = lax.ppermute(tokens, "tp", swap)
        half_freq = time_weight.shape[0] // 2
        time_value = jnp.broadcast_to(timestep, (half_freq,)).astype(jnp.float32)
        sigma = noise_level(time_value)
        frequency = jnp.exp(-math.log(10000.0) * jnp.arange(half_freq, dtype=jnp.float32) / half_freq)
        angle = 1000.0 * sigma * frequency
        act = jax.nn.silu(jnp.concatenate([jnp.cos(angle), jnp.sin(angle)]))[None, :]
        mine, mod, gate = project(act, block_mod, tokens, other, time_weight, w_query, w_key, w_value)
        near, mine, mod, gate = lax.optimization_barrier((near, mine, mod, gate))
        far = lax.ppermute(near, "tp", swap)
        sent = project_shared(near, far, mod, mine, w_query, w_key, w_value, colours)
        got = [lax.ppermute(piece, ("req", "tp"), route) for piece, route in zip(sent, routes)]
        swapped = [lax.ppermute(piece, "tp", swap) for piece in got]
        done = attend(video_lengths, got, swapped, heads)
        back = [
            lax.ppermute(piece, ("req", "tp"), [(b, a) for a, b in route]) for piece, route in zip(done, routes)
        ]
        keep, give = part(back, heads)
        mine, theirs = combine(keep, lax.ppermute(give, "req", cross), w_out)
        theirs = lax.ppermute(theirs, "tp", swap)
        velocity, stepped = finish(timestep, mine, theirs, tokens, gate)
        return (velocity, stepped)

    return on_device


def solution(mesh):
    return jax.shard_map(
        make(mesh),
        mesh=mesh,
        in_specs=(
            P("req", "tp"), P(), P(), P(), P(), P(None, "tp"), P(None, "tp"), P(None, "tp"), P("tp", None),
        ),
        out_specs=(P("req", "tp"), P("req", "tp")),
        check_vma=False,
    )
```

```python
import functools
import math

import jax
import jax.numpy as jnp
from jax import lax
from jax.experimental import pallas as pl
from jax.experimental.pallas import tpu as pltpu
from jax.sharding import PartitionSpec as P

HEAD_DIM = 128
STEPS = 1000
QUERY_BLOCK = 384
KEY_GROUP = 3072
WINDOWS = (1280, 2048, 2560)
PARTS = 3
NEG = -1e30
STREAM_LIMIT = 51 * 1024 * 1024
VMEM_LIMIT = 32 * 1024 * 1024


def noise_level(step_value):
    frac = step_value / STEPS
    return 5.0 * frac / (1.0 + 4.0 * frac)


def turned(colours, side):
    return colours // 2 * (1 - side)


def pairs_out(chips, heads, colour):
    half = chips // 2
    colours = half // 2
    pairs = []
    for chip in range(chips):
        side, x = chip // half, chip % 2
        slot = chip % half // 2 ^ turned(colours, side)
        for core in range(2):
            place = slot ^ colour ^ turned(colours, core)
            if (slot ^ colour) < heads:
                pairs.append((chip * 2 + core, (core * half + place * 2 + x) * 2 + side))
    return pairs


def place_of(colours):
    chip = lax.axis_index("req")
    return lax.rem(chip // 2, colours) ^ turned(colours, chip // (2 * colours)), lax.rem(chip, 2)


def any_spec():
    return pl.BlockSpec(memory_space=pl.ANY)


def vmem_spec():
    return pl.BlockSpec(memory_space=pltpu.VMEM)


def smem_spec():
    return pl.BlockSpec(memory_space=pltpu.SMEM)


def standardise(full, own_ref, other_ref):
    share = own_ref.shape[1]
    core = lax.axis_index("tp")
    full[:, pl.ds(pl.multiple_of(core * share, 128), share)] = own_ref[...].astype(jnp.float32)
    full[:, pl.ds(pl.multiple_of((1 - core) * share, 128), share)] = other_ref[...].astype(jnp.float32)
    whole = full[...]
    centred = whole - jnp.mean(whole, axis=1, keepdims=True)
    variance = jnp.mean(centred * centred, axis=1, keepdims=True)
    return centred * lax.rsqrt(variance + 1e-06)


def project_part(packed, normed, weight, part):
    out = jnp.dot(normed[...], weight, preferred_element_type=jnp.float32)
    if part == 0:
        out = out * (math.log2(math.e) / math.sqrt(HEAD_DIM))
    for head in range(out.shape[1] // HEAD_DIM):
        packed[head, part] = out[:, head * HEAD_DIM:(head + 1) * HEAD_DIM].astype(jnp.bfloat16)


def load_weights(load, refs, weights):
    depth, columns = weights.shape[1:]
    x = lax.rem(lax.axis_index("req"), 2)
    for part, ref in enumerate(refs):
        for cut in range(2):
            here = pl.ds(cut * (depth // 2), depth // 2)
            load(ref.at[here, pl.ds(pl.multiple_of(x * columns, 128), columns)], weights.at[part, here])


def project_kernel(act_ref, block_ref, own_ref, other_ref, time_ref, wq_ref, wk_ref, wv_ref, *rest):
    packed, mod_ref, gate_ref, weights, times, full, normed, sems = rest
    depth = full.shape[1]
    share = own_ref.shape[1]
    freq = times.shape[0]
    core = lax.axis_index("tp")
    loads = []

    def load(source, target):
        loads.append(pltpu.make_async_copy(source, target, sems.at[len(loads)]))
        loads[-1].start()

    for part in range(2):
        here = pl.ds(part * (freq // 2), freq // 2)
        load(time_ref.at[here, pl.ds(0, 2 * depth)], times.at[here, pl.ds(0, 2 * depth)])
    load_weights(load, (wq_ref, wk_ref, wv_ref), weights)
    load(
        time_ref.at[:, pl.ds(pl.multiple_of(2 * depth + core * share, 128), share)],
        times.at[:, pl.ds(2 * depth, share)],
    )
    full[...] = standardise(full, own_ref, other_ref)
    act = jnp.transpose(jnp.broadcast_to(act_ref[...], (8, freq)))[:, :1]
    act = jnp.broadcast_to(act, (freq, HEAD_DIM))

    def modulation(column):
        return jnp.sum(act * times[:, column:column + HEAD_DIM], axis=0, keepdims=True)

    loads[0].wait()
    loads[1].wait()
    for column in range(0, depth, HEAD_DIM):
        here = slice(column, column + HEAD_DIM)
        shift = modulation(column) + block_ref[0:1, here]
        scale = modulation(depth + column) + block_ref[1:2, here]
        mod_ref[0:1, here] = shift
        mod_ref[1:2, here] = scale
        normed[:, here] = (full[:, here] * (1.0 + scale) + shift).astype(jnp.bfloat16)
    for part in range(3):
        loads[2 + 2 * part].wait()
        loads[3 + 2 * part].wait()
        project_part(packed, normed, weights[part], part)
    loads[8].wait()
    for column in range(0, share, HEAD_DIM):
        here = pl.ds(pl.multiple_of(core * share + column, 128), HEAD_DIM)
        gate_ref[:, column:column + HEAD_DIM] = modulation(2 * depth + column) + block_ref[2:3, here]


def project(act, block_mod, own, other, time_weight, w_query, w_key, w_value):
    rows, share = own.shape
    depth, columns = w_query.shape
    columns = columns // 2
    freq = time_weight.shape[0]
    heads = columns // HEAD_DIM
    return pl.pallas_call(
        project_kernel,
        in_specs=[vmem_spec()] * 4 + [any_spec()] * 4,
        out_specs=[vmem_spec()] * 3,
        out_shape=[
            jax.ShapeDtypeStruct((heads, 3, rows, HEAD_DIM), jnp.bfloat16),
            jax.ShapeDtypeStruct((2, depth), jnp.float32),
            jax.ShapeDtypeStruct((1, share), jnp.float32),
        ],
        scratch_shapes=[
            pltpu.VMEM((3, depth, columns), jnp.bfloat16),
            pltpu.VMEM((freq, 2 * depth + share), jnp.float32),
            pltpu.VMEM((rows, depth), jnp.float32),
            pltpu.VMEM((rows, depth), jnp.bfloat16),
            pltpu.SemaphoreType.DMA((9,)),
        ],
        compiler_params=pltpu.CompilerParams(vmem_limit_bytes=STREAM_LIMIT),
        cost_estimate=pl.CostEstimate(flops=6 * rows * depth * columns, bytes_accessed=8 * 2**20, transcendentals=0),
    )(act, block_mod, own, other, time_weight, w_query, w_key, w_value)


def share_kernel(colours, near_ref, far_ref, mod_ref, mine, wq_ref, wk_ref, wv_ref, *rest):
    outs, (full, normed, packed, sems) = rest[:colours], rest[colours:]
    heads, _, rows, _ = mine.shape
    slot, x = place_of(colours)

    def each_copy(source, position, offset, act):
        for head in range(heads):
            for colour in range(colours):
                @pl.when((slot ^ colour) == head)
                def _():
                    here = pl.ds(pl.multiple_of(position * rows, 64), rows)
                    act(pltpu.make_async_copy(source.at[head], outs[colour].at[:, here], sems.at[offset + head]))

    each_copy(mine, x, 0, lambda copy: copy.start())
    scaled = standardise(full, near_ref, far_ref)
    normed[...] = (scaled * (1.0 + mod_ref[1:2, :]) + mod_ref[0:1, :]).astype(jnp.bfloat16)
    columns = pl.ds(pl.multiple_of(x * heads * HEAD_DIM, HEAD_DIM), heads * HEAD_DIM)
    for part, ref in enumerate((wq_ref, wk_ref, wv_ref)):
        project_part(packed, normed, ref[:, columns], part)
    each_copy(packed, 1 - x, heads, lambda copy: copy.start())
    each_copy(mine, x, 0, lambda copy: copy.wait())
    each_copy(packed, 1 - x, heads, lambda copy: copy.wait())


def project_shared(near, far, mod, mine, w_query, w_key, w_value, colours):
    heads, _, rows, _ = mine.shape
    depth = mod.shape[1]
    return pl.pallas_call(
        functools.partial(share_kernel, colours),
        in_specs=[vmem_spec()] * 3 + [any_spec()] + [vmem_spec()] * 3,
        out_specs=[any_spec()] * colours,
        out_shape=[jax.ShapeDtypeStruct((3, 2 * rows, HEAD_DIM), jnp.bfloat16)] * colours,
        scratch_shapes=[
            pltpu.VMEM((rows, depth), jnp.float32),
            pltpu.VMEM((rows, depth), jnp.bfloat16),
            pltpu.VMEM(mine.shape, jnp.bfloat16),
            pltpu.SemaphoreType.DMA((2 * heads,)),
        ],
        compiler_params=pltpu.CompilerParams(vmem_limit_bytes=VMEM_LIMIT),
    )(near, far, mod, mine, w_query, w_key, w_value)


def attend_kernel(colours, heads, lengths_ref, *refs):
    pieces, swapped, outs = refs[:colours], refs[colours:2 * colours], refs[2 * colours:3 * colours]
    query, keys, values, result, top, total, sems, out_sems = refs[3 * colours:]
    rows = pieces[0].shape[1]
    own_rows, all_rows = query.shape[0], keys.shape[0]
    side = lax.axis_index("tp")
    slot, _ = place_of(colours)
    front = pl.ds(0, HEAD_DIM)
    videos = lengths_ref.shape[0]

    def at(colour, which, whole):
        place = slot ^ colour ^ turned(colours, which)
        return pl.ds(pl.multiple_of(place * rows + (which * own_rows if whole else 0), 128), rows)

    def each_copy(act):
        for colour in range(colours):
            near, far = pieces[colour], swapped[colour]
            for number, (source, target) in enumerate((
                (near.at[0], query.at[at(colour, side, False), front]),
                (near.at[1], keys.at[at(colour, side, True), front]),
                (near.at[2], values.at[at(colour, side, True), front]),
                (far.at[1], keys.at[at(colour, 1 - side, True), front]),
                (far.at[2], values.at[at(colour, 1 - side, True), front]),
            )):
                act(pltpu.make_async_copy(source, target, sems.at[5 * colour + number]))

    @pl.when(slot < heads)
    def _():
        each_copy(lambda copy: copy.start())
        ends, end = [], jnp.int32(0)
        for video in range(videos):
            end = end + lengths_ref[video]
            ends.append(end)
        starts = [jnp.int32(0)] + ends[:-1]
        lane = lax.broadcasted_iota(jnp.int32, (1, HEAD_DIM), 1)
        lane_start = jnp.zeros((1, HEAD_DIM), jnp.int32)
        lane_stop = jnp.zeros((1, HEAD_DIM), jnp.int32)
        for video, (start, stop) in enumerate(zip(starts, ends)):
            lane_start = jnp.where(lane == video, start, lane_start)
            lane_stop = jnp.where(lane == video, stop, lane_stop)
        place = lax.broadcasted_iota(jnp.int32, (HEAD_DIM, HEAD_DIM), 0)

        def inside(first):
            index = first + place
            return (index >= lane_start) & (index < lane_stop)

        def fill_query(block, carry):
            local = pl.multiple_of(block * HEAD_DIM, HEAD_DIM)
            member = inside(side * own_rows + local)
            query[pl.ds(local, HEAD_DIM), HEAD_DIM:] = jnp.where(member, 1.0, 0.0).astype(jnp.bfloat16)
            return carry

        def fill_keys(block, carry):
            begin = pl.multiple_of(block * HEAD_DIM, HEAD_DIM)
            keys[pl.ds(begin, HEAD_DIM), HEAD_DIM:] = jnp.where(
                inside(begin) | (lane >= videos), 0.0, NEG
            ).astype(jnp.bfloat16)
            values[pl.ds(begin, HEAD_DIM), HEAD_DIM:] = jnp.ones((HEAD_DIM, HEAD_DIM), jnp.bfloat16)
            return carry

        lax.fori_loop(0, own_rows // HEAD_DIM, fill_query, 0)
        lax.fori_loop(0, all_rows // HEAD_DIM, fill_keys, 0)
        each_copy(lambda copy: copy.wait())

        sub = QUERY_BLOCK // PARTS

        def query_block(block, carry):
            local = pl.multiple_of(block * QUERY_BLOCK, QUERY_BLOCK)
            first = side * own_rows + local
            last = first + QUERY_BLOCK - 1
            low, high = jnp.int32(0), jnp.int32(0)
            for start, stop in zip(starts, ends):
                low = jnp.where(first >= start, start, low)
                high = jnp.where(last >= start, stop, high)
            low = low // HEAD_DIM * HEAD_DIM

            def scores(offset, begin, count):
                q = query[pl.ds(pl.multiple_of(local + offset, 64), sub), :]
                score = lax.dot_general(
                    q, keys[pl.ds(begin, count), :], (((1,), (1,)), ((), ())), preferred_element_type=jnp.float32
                )
                tiles = [score[:, j:j + HEAD_DIM] for j in range(0, count, HEAD_DIM)]
                most = jnp.max(functools.reduce(jnp.maximum, tiles), axis=1, keepdims=True)
                return tiles, jnp.broadcast_to(most, (sub, HEAD_DIM))

            def weigh(begin, count, tiles, now):
                probs = jnp.concatenate([jnp.exp2(tile - now).astype(jnp.bfloat16) for tile in tiles], axis=1)
                return jnp.dot(probs, values[pl.ds(begin, count), :], preferred_element_type=jnp.float32)

            def store(offset, update):
                out = update[:, :HEAD_DIM] / update[:, HEAD_DIM:]
                result[pl.ds(pl.multiple_of(local + offset, 64), sub), :] = out.astype(jnp.bfloat16)

            def window(count):
                begin = pl.multiple_of(jnp.minimum(low, all_rows - count), HEAD_DIM)
                tiles, now = scores(0, begin, count)
                for offset in range(0, QUERY_BLOCK, sub):
                    later = scores(offset + sub, begin, count) if offset + sub < QUERY_BLOCK else None
                    store(offset, weigh(begin, count, tiles, now))
                    if later is not None:
                        tiles, now = later

            def long(offset):
                top[...] = jnp.full(top.shape, 2 * NEG, jnp.float32)
                total[...] = jnp.zeros(total.shape, jnp.float32)

                def key_block(number, carry):
                    begin = pl.multiple_of(number * KEY_GROUP, KEY_GROUP)
                    tiles, most = scores(offset, begin, KEY_GROUP)
                    before = top[...]
                    now = jnp.maximum(before, most)
                    update = weigh(begin, KEY_GROUP, tiles, now)
                    shrink = jnp.exp2(before - now)
                    total[:, :HEAD_DIM] = total[:, :HEAD_DIM] * shrink + update[:, :HEAD_DIM]
                    total[:, HEAD_DIM:] = total[:, HEAD_DIM:] * shrink + update[:, HEAD_DIM:]
                    top[...] = now
                    return carry

                lax.fori_loop(low // KEY_GROUP, (high + KEY_GROUP - 1) // KEY_GROUP, key_block, 0)
                store(offset, total)

            need = high - low
            floor = 0
            for count in WINDOWS:
                pl.when((need > floor) & (need <= count))(functools.partial(window, count))
                floor = count

            @pl.when(need > floor)
            def _():
                if all_rows == KEY_GROUP:
                    window(KEY_GROUP)
                else:
                    for offset in range(0, QUERY_BLOCK, sub):
                        long(offset)

            return carry

        lax.fori_loop(0, own_rows // QUERY_BLOCK, query_block, 0)
        copies = [
            pltpu.make_async_copy(result.at[at(colour, side, False)], outs[colour], out_sems.at[colour])
            for colour in range(colours)
        ]
        for copy in copies:
            copy.start()
        for copy in copies:
            copy.wait()


def attend(lengths, pieces, swapped, heads):
    rows = pieces[0].shape[1]
    colours = len(pieces)
    own = colours * rows
    return pl.pallas_call(
        functools.partial(attend_kernel, colours, heads),
        in_specs=[smem_spec()] + [any_spec()] * (2 * colours),
        out_specs=[any_spec()] * colours,
        out_shape=[jax.ShapeDtypeStruct((rows, HEAD_DIM), jnp.bfloat16)] * colours,
        scratch_shapes=[
            pltpu.VMEM((own, 2 * HEAD_DIM), jnp.bfloat16),
            pltpu.VMEM((2 * own, 2 * HEAD_DIM), jnp.bfloat16),
            pltpu.VMEM((2 * own, 2 * HEAD_DIM), jnp.bfloat16),
            pltpu.VMEM((own, HEAD_DIM), jnp.bfloat16),
            pltpu.VMEM((QUERY_BLOCK // PARTS, HEAD_DIM), jnp.float32),
            pltpu.VMEM((QUERY_BLOCK // PARTS, 2 * HEAD_DIM), jnp.float32),
            pltpu.SemaphoreType.DMA((5 * colours,)),
            pltpu.SemaphoreType.DMA((colours,)),
        ],
        compiler_params=pltpu.CompilerParams(vmem_limit_bytes=VMEM_LIMIT),
    )(lengths, *pieces, *swapped)


def part_kernel(colours, *refs):
    pieces, (keep, give, sems) = refs[:colours], refs[colours:]
    heads, rows, _ = keep.shape
    slot, x = place_of(colours)

    def each_copy(act):
        for head in range(heads):
            for number, (target, position) in enumerate(((give, 1 - x), (keep, x))):
                here = pl.ds(pl.multiple_of(position * rows, 64), rows)
                for colour in range(colours):
                    @pl.when((slot ^ colour) == head)
                    def _():
                        source = pieces[colour].at[here]
                        act(pltpu.make_async_copy(source, target.at[head], sems.at[2 * head + number]))

    each_copy(lambda copy: copy.start())
    each_copy(lambda copy: copy.wait())


def part(pieces, heads):
    rows = pieces[0].shape[0] // 2
    shape = jax.ShapeDtypeStruct((heads, rows, HEAD_DIM), jnp.bfloat16)
    return pl.pallas_call(
        functools.partial(part_kernel, len(pieces)),
        in_specs=[any_spec()] * len(pieces),
        out_specs=[any_spec()] * 2,
        out_shape=[shape, shape],
        scratch_shapes=[pltpu.SemaphoreType.DMA((2 * heads,))],
        compiler_params=pltpu.CompilerParams(vmem_limit_bytes=VMEM_LIMIT),
    )(*pieces)


def combine_kernel(keep_ref, got_ref, weight, mine, theirs, attended, sems):
    share = mine.shape[1]
    heads = keep_ref.shape[0]
    core = lax.axis_index("tp")
    x = lax.rem(lax.axis_index("req"), 2)
    copies = []
    for head in range(heads):
        for source, which in ((keep_ref, x), (got_ref, 1 - x)):
            columns = pl.ds(pl.multiple_of((which * heads + head) * HEAD_DIM, HEAD_DIM), HEAD_DIM)
            copies.append(pltpu.make_async_copy(source.at[head], attended.at[:, columns], sems.at[len(copies)]))
            copies[-1].start()
    for copy in copies:
        copy.wait()
    left = attended[...]
    for out, where in ((theirs, 1 - core), (mine, core)):
        columns = pl.ds(pl.multiple_of(where * share, 128), share)
        out[...] = jnp.dot(left, weight[:, columns], preferred_element_type=jnp.float32).astype(out.dtype)


def combine(keep, got, w_out):
    heads, rows, _ = keep.shape
    depth, width = w_out.shape
    return pl.pallas_call(
        combine_kernel,
        in_specs=[any_spec()] * 2 + [vmem_spec()],
        out_specs=[vmem_spec(), vmem_spec()],
        out_shape=[
            jax.ShapeDtypeStruct((rows, width // 2), jnp.float32),
            jax.ShapeDtypeStruct((rows, width // 2), jnp.bfloat16),
        ],
        scratch_shapes=[
            pltpu.VMEM((rows, depth), jnp.bfloat16),
            pltpu.SemaphoreType.DMA((2 * heads,)),
        ],
        compiler_params=pltpu.CompilerParams(vmem_limit_bytes=VMEM_LIMIT),
    )(keep, got, w_out)


def finish_kernel(timestep_ref, mine, theirs, tokens, gate_ref, velocity, stepped):
    step_value = jnp.full((1, 128), timestep_ref[0], jnp.int32).astype(jnp.float32)
    delta = (noise_level(step_value - 1.0) - noise_level(step_value))[:, :1]
    branch = gate_ref[...] * (mine[...] + theirs[...].astype(jnp.float32))
    velocity[...] = branch.astype(jnp.bfloat16)
    stepped[...] = (tokens[...].astype(jnp.float32) + delta * branch).astype(jnp.bfloat16)


def finish(timestep, mine, theirs, tokens, gate):
    shape = jax.ShapeDtypeStruct(tokens.shape, jnp.bfloat16)
    return pl.pallas_call(
        finish_kernel,
        in_specs=[smem_spec()] + [vmem_spec()] * 4,
        out_specs=[vmem_spec(), vmem_spec()],
        out_shape=[shape, shape],
        compiler_params=pltpu.CompilerParams(vmem_limit_bytes=VMEM_LIMIT),
    )(timestep, mine, theirs, tokens, gate)


def make(mesh):
    chips = mesh.shape["req"]
    colours = chips // 4
    swap = [(0, 1), (1, 0)]
    cross = [(chip, chip ^ 1) for chip in range(chips)]

    def on_device(tokens, video_lengths, timestep, time_weight, block_mod, w_query, w_key, w_value, w_out):
        heads = w_query.shape[1] // HEAD_DIM // 2
        routes = [pairs_out(chips, heads, colour) for colour in range(colours)]
        near = lax.ppermute(tokens, "req", cross)
        other = lax.ppermute(tokens, "tp", swap)
        half_freq = time_weight.shape[0] // 2
        time_value = jnp.broadcast_to(timestep, (half_freq,)).astype(jnp.float32)
        sigma = noise_level(time_value)
        frequency = jnp.exp(-math.log(10000.0) * jnp.arange(half_freq, dtype=jnp.float32) / half_freq)
        angle = 1000.0 * sigma * frequency
        act = jax.nn.silu(jnp.concatenate([jnp.cos(angle), jnp.sin(angle)]))[None, :]
        mine, mod, gate = project(act, block_mod, tokens, other, time_weight, w_query, w_key, w_value)
        near, mine, mod, gate = lax.optimization_barrier((near, mine, mod, gate))
        far = lax.ppermute(near, "tp", swap)
        sent = project_shared(near, far, mod, mine, w_query, w_key, w_value, colours)
        got = [lax.ppermute(piece, ("req", "tp"), route) for piece, route in zip(sent, routes)]
        swapped = [lax.ppermute(piece, "tp", swap) for piece in got]
        done = attend(video_lengths, got, swapped, heads)
        back = [
            lax.ppermute(piece, ("req", "tp"), [(b, a) for a, b in route]) for piece, route in zip(done, routes)
        ]
        keep, give = part(back, heads)
        mine, theirs = combine(keep, lax.ppermute(give, "req", cross), w_out)
        theirs = lax.ppermute(theirs, "tp", swap)
        velocity, stepped = finish(timestep, mine, theirs, tokens, gate)
        return (velocity, stepped)

    return on_device


def solution(mesh):
    return jax.shard_map(
        make(mesh),
        mesh=mesh,
        in_specs=(
            P("req", "tp"), P(), P(), P(), P(), P(None, "tp"), P(None, "tp"), P(None, "tp"), P("tp", None),
        ),
        out_specs=(P("req", "tp"), P("req", "tp")),
        check_vma=False,
    )
```

```python
import functools
import math

import jax
import jax.numpy as jnp
from jax import lax
from jax.experimental import pallas as pl
from jax.experimental.pallas import tpu as pltpu
from jax.sharding import PartitionSpec as P

HEAD_DIM = 128
STEPS = 1000
QUERY_BLOCK = 384
KEY_GROUP = 3072
WINDOWS = (1280, 2048, 2560)
PARTS = 3
NEG = -1e30
STREAM_LIMIT = 51 * 1024 * 1024
VMEM_LIMIT = 32 * 1024 * 1024


def noise_level(step_value):
    frac = step_value / STEPS
    return 5.0 * frac / (1.0 + 4.0 * frac)


def turned(colours, side):
    return colours // 2 * (1 - side)


def pairs_out(chips, heads, colour):
    half = chips // 2
    colours = half // 2
    pairs = []
    for chip in range(chips):
        side, x = chip // half, chip % 2
        slot = chip % half // 2 ^ turned(colours, side)
        for core in range(2):
            place = slot ^ colour ^ turned(colours, core)
            if (slot ^ colour) < heads:
                pairs.append((chip * 2 + core, (core * half + place * 2 + x) * 2 + side))
    return pairs


def place_of(colours):
    chip = lax.axis_index("req")
    return lax.rem(chip // 2, colours) ^ turned(colours, chip // (2 * colours)), lax.rem(chip, 2)


def any_spec():
    return pl.BlockSpec(memory_space=pl.ANY)


def vmem_spec():
    return pl.BlockSpec(memory_space=pltpu.VMEM)


def smem_spec():
    return pl.BlockSpec(memory_space=pltpu.SMEM)


def standardise(full, own_ref, other_ref):
    share = own_ref.shape[1]
    core = lax.axis_index("tp")
    full[:, pl.ds(pl.multiple_of(core * share, 128), share)] = own_ref[...].astype(jnp.float32)
    full[:, pl.ds(pl.multiple_of((1 - core) * share, 128), share)] = other_ref[...].astype(jnp.float32)
    whole = full[...]
    centred = whole - jnp.mean(whole, axis=1, keepdims=True)
    variance = jnp.mean(centred * centred, axis=1, keepdims=True)
    return centred * lax.rsqrt(variance + 1e-06)


def project_part(packed, normed, weight, part):
    out = jnp.dot(normed[...], weight, preferred_element_type=jnp.float32)
    if part == 0:
        out = out * (math.log2(math.e) / math.sqrt(HEAD_DIM))
    for head in range(out.shape[1] // HEAD_DIM):
        packed[head, part] = out[:, head * HEAD_DIM:(head + 1) * HEAD_DIM].astype(jnp.bfloat16)


def load_weights(load, refs, weights):
    depth, columns = weights.shape[1:]
    x = lax.rem(lax.axis_index("req"), 2)
    for part, ref in enumerate(refs):
        for cut in range(2):
            here = pl.ds(cut * (depth // 2), depth // 2)
            load(ref.at[here, pl.ds(pl.multiple_of(x * columns, 128), columns)], weights.at[part, here])


def project_kernel(act_ref, block_ref, own_ref, other_ref, time_ref, wq_ref, wk_ref, wv_ref, *rest):
    packed, mod_ref, gate_ref, weights, times, full, normed, sems = rest
    depth = full.shape[1]
    share = own_ref.shape[1]
    freq = times.shape[0]
    core = lax.axis_index("tp")
    loads = []

    def load(source, target):
        loads.append(pltpu.make_async_copy(source, target, sems.at[len(loads)]))
        loads[-1].start()

    for part in range(2):
        here = pl.ds(part * (freq // 2), freq // 2)
        load(time_ref.at[here, pl.ds(0, 2 * depth)], times.at[here, pl.ds(0, 2 * depth)])
    load_weights(load, (wq_ref, wk_ref, wv_ref), weights)
    load(
        time_ref.at[:, pl.ds(pl.multiple_of(2 * depth + core * share, 128), share)],
        times.at[:, pl.ds(2 * depth, share)],
    )
    full[...] = standardise(full, own_ref, other_ref)
    act = jnp.transpose(jnp.broadcast_to(act_ref[...], (8, freq)))[:, :1]
    act = jnp.broadcast_to(act, (freq, HEAD_DIM))

    def modulation(column):
        return jnp.sum(act * times[:, column:column + HEAD_DIM], axis=0, keepdims=True)

    loads[0].wait()
    loads[1].wait()
    for column in range(0, depth, HEAD_DIM):
        here = slice(column, column + HEAD_DIM)
        shift = modulation(column) + block_ref[0:1, here]
        scale = modulation(depth + column) + block_ref[1:2, here]
        mod_ref[0:1, here] = shift
        mod_ref[1:2, here] = scale
        normed[:, here] = (full[:, here] * (1.0 + scale) + shift).astype(jnp.bfloat16)
    for part in range(3):
        loads[2 + 2 * part].wait()
        loads[3 + 2 * part].wait()
        project_part(packed, normed, weights[part], part)
    loads[8].wait()
    for column in range(0, share, HEAD_DIM):
        here = pl.ds(pl.multiple_of(core * share + column, 128), HEAD_DIM)
        gate_ref[:, column:column + HEAD_DIM] = modulation(2 * depth + column) + block_ref[2:3, here]


def project(act, block_mod, own, other, time_weight, w_query, w_key, w_value):
    rows, share = own.shape
    depth, columns = w_query.shape
    columns = columns // 2
    freq = time_weight.shape[0]
    heads = columns // HEAD_DIM
    return pl.pallas_call(
        project_kernel,
        in_specs=[vmem_spec()] * 4 + [any_spec()] * 4,
        out_specs=[vmem_spec()] * 3,
        out_shape=[
            jax.ShapeDtypeStruct((heads, 3, rows, HEAD_DIM), jnp.bfloat16),
            jax.ShapeDtypeStruct((2, depth), jnp.float32),
            jax.ShapeDtypeStruct((1, share), jnp.float32),
        ],
        scratch_shapes=[
            pltpu.VMEM((3, depth, columns), jnp.bfloat16),
            pltpu.VMEM((freq, 2 * depth + share), jnp.float32),
            pltpu.VMEM((rows, depth), jnp.float32),
            pltpu.VMEM((rows, depth), jnp.bfloat16),
            pltpu.SemaphoreType.DMA((9,)),
        ],
        compiler_params=pltpu.CompilerParams(vmem_limit_bytes=STREAM_LIMIT),
        cost_estimate=pl.CostEstimate(flops=6 * rows * depth * columns, bytes_accessed=8 * 2**20, transcendentals=0),
    )(act, block_mod, own, other, time_weight, w_query, w_key, w_value)


def share_kernel(colours, near_ref, far_ref, mod_ref, mine, wq_ref, wk_ref, wv_ref, *rest):
    outs, (full, normed, packed, sems) = rest[:colours], rest[colours:]
    heads, _, rows, _ = mine.shape
    slot, x = place_of(colours)

    def each_copy(source, position, offset, act):
        for head in range(heads):
            for colour in range(colours):
                @pl.when((slot ^ colour) == head)
                def _():
                    here = pl.ds(pl.multiple_of(position * rows, 64), rows)
                    act(pltpu.make_async_copy(source.at[head], outs[colour].at[:, here], sems.at[offset + head]))

    each_copy(mine, x, 0, lambda copy: copy.start())
    scaled = standardise(full, near_ref, far_ref)
    normed[...] = (scaled * (1.0 + mod_ref[1:2, :]) + mod_ref[0:1, :]).astype(jnp.bfloat16)
    columns = pl.ds(pl.multiple_of(x * heads * HEAD_DIM, HEAD_DIM), heads * HEAD_DIM)
    for part, ref in enumerate((wq_ref, wk_ref, wv_ref)):
        project_part(packed, normed, ref[:, columns], part)
    each_copy(packed, 1 - x, heads, lambda copy: copy.start())
    each_copy(mine, x, 0, lambda copy: copy.wait())
    each_copy(packed, 1 - x, heads, lambda copy: copy.wait())


def project_shared(near, far, mod, mine, w_query, w_key, w_value, colours):
    heads, _, rows, _ = mine.shape
    depth = mod.shape[1]
    return pl.pallas_call(
        functools.partial(share_kernel, colours),
        in_specs=[vmem_spec()] * 3 + [any_spec()] + [vmem_spec()] * 3,
        out_specs=[any_spec()] * colours,
        out_shape=[jax.ShapeDtypeStruct((3, 2 * rows, HEAD_DIM), jnp.bfloat16)] * colours,
        scratch_shapes=[
            pltpu.VMEM((rows, depth), jnp.float32),
            pltpu.VMEM((rows, depth), jnp.bfloat16),
            pltpu.VMEM(mine.shape, jnp.bfloat16),
            pltpu.SemaphoreType.DMA((2 * heads,)),
        ],
        compiler_params=pltpu.CompilerParams(vmem_limit_bytes=VMEM_LIMIT),
    )(near, far, mod, mine, w_query, w_key, w_value)


def attend_kernel(colours, heads, lengths_ref, *refs):
    pieces, swapped, outs = refs[:colours], refs[colours:2 * colours], refs[2 * colours:3 * colours]
    query, keys, values, result, top, total, sems, out_sems = refs[3 * colours:]
    rows = pieces[0].shape[1]
    own_rows, all_rows = query.shape[0], keys.shape[0]
    side = lax.axis_index("tp")
    slot, _ = place_of(colours)
    front = pl.ds(0, HEAD_DIM)
    videos = lengths_ref.shape[0]

    def at(colour, which, whole):
        place = slot ^ colour ^ turned(colours, which)
        return pl.ds(pl.multiple_of(place * rows + (which * own_rows if whole else 0), 128), rows)

    def each_copy(act):
        for colour in range(colours):
            near, far = pieces[colour], swapped[colour]
            for number, (source, target) in enumerate((
                (near.at[0], query.at[at(colour, side, False), front]),
                (near.at[1], keys.at[at(colour, side, True), front]),
                (near.at[2], values.at[at(colour, side, True), front]),
                (far.at[1], keys.at[at(colour, 1 - side, True), front]),
                (far.at[2], values.at[at(colour, 1 - side, True), front]),
            )):
                act(pltpu.make_async_copy(source, target, sems.at[5 * colour + number]))

    @pl.when(slot < heads)
    def _():
        each_copy(lambda copy: copy.start())
        ends, end = [], jnp.int32(0)
        for video in range(videos):
            end = end + lengths_ref[video]
            ends.append(end)
        starts = [jnp.int32(0)] + ends[:-1]
        lane = lax.broadcasted_iota(jnp.int32, (1, HEAD_DIM), 1)
        lane_start = jnp.zeros((1, HEAD_DIM), jnp.int32)
        lane_stop = jnp.zeros((1, HEAD_DIM), jnp.int32)
        for video, (start, stop) in enumerate(zip(starts, ends)):
            lane_start = jnp.where(lane == video, start, lane_start)
            lane_stop = jnp.where(lane == video, stop, lane_stop)
        place = lax.broadcasted_iota(jnp.int32, (HEAD_DIM, HEAD_DIM), 0)

        def inside(first):
            index = first + place
            return (index >= lane_start) & (index < lane_stop)

        def fill_query(block, carry):
            local = pl.multiple_of(block * HEAD_DIM, HEAD_DIM)
            member = inside(side * own_rows + local)
            query[pl.ds(local, HEAD_DIM), HEAD_DIM:] = jnp.where(member, 1.0, 0.0).astype(jnp.bfloat16)
            return carry

        def fill_keys(block, carry):
            begin = pl.multiple_of(block * HEAD_DIM, HEAD_DIM)
            keys[pl.ds(begin, HEAD_DIM), HEAD_DIM:] = jnp.where(
                inside(begin) | (lane >= videos), 0.0, NEG
            ).astype(jnp.bfloat16)
            values[pl.ds(begin, HEAD_DIM), HEAD_DIM:] = jnp.ones((HEAD_DIM, HEAD_DIM), jnp.bfloat16)
            return carry

        lax.fori_loop(0, own_rows // HEAD_DIM, fill_query, 0)
        lax.fori_loop(0, all_rows // HEAD_DIM, fill_keys, 0)
        each_copy(lambda copy: copy.wait())

        sub = QUERY_BLOCK // PARTS

        def query_block(block, carry):
            local = pl.multiple_of(block * QUERY_BLOCK, QUERY_BLOCK)
            first = side * own_rows + local
            last = first + QUERY_BLOCK - 1
            low, high = jnp.int32(0), jnp.int32(0)
            for start, stop in zip(starts, ends):
                low = jnp.where(first >= start, start, low)
                high = jnp.where(last >= start, stop, high)
            low = low // HEAD_DIM * HEAD_DIM

            def scores(offset, begin, count):
                q = query[pl.ds(pl.multiple_of(local + offset, 64), sub), :]
                score = lax.dot_general(
                    q, keys[pl.ds(begin, count), :], (((1,), (1,)), ((), ())), preferred_element_type=jnp.float32
                )
                tiles = [score[:, j:j + HEAD_DIM] for j in range(0, count, HEAD_DIM)]
                most = jnp.max(functools.reduce(jnp.maximum, tiles), axis=1, keepdims=True)
                return tiles, jnp.broadcast_to(most, (sub, HEAD_DIM))

            def weigh(begin, count, tiles, now):
                probs = jnp.concatenate([jnp.exp2(tile - now).astype(jnp.bfloat16) for tile in tiles], axis=1)
                return jnp.dot(probs, values[pl.ds(begin, count), :], preferred_element_type=jnp.float32)

            def store(offset, update):
                out = update[:, :HEAD_DIM] / update[:, HEAD_DIM:]
                result[pl.ds(pl.multiple_of(local + offset, 64), sub), :] = out.astype(jnp.bfloat16)

            def window(count):
                begin = pl.multiple_of(jnp.minimum(low, all_rows - count), HEAD_DIM)
                tiles, now = scores(0, begin, count)
                for offset in range(0, QUERY_BLOCK, sub):
                    later = scores(offset + sub, begin, count) if offset + sub < QUERY_BLOCK else None
                    store(offset, weigh(begin, count, tiles, now))
                    if later is not None:
                        tiles, now = later

            def long(offset):
                top[...] = jnp.full(top.shape, 2 * NEG, jnp.float32)
                total[...] = jnp.zeros(total.shape, jnp.float32)

                def key_block(number, carry):
                    begin = pl.multiple_of(number * KEY_GROUP, KEY_GROUP)
                    tiles, most = scores(offset, begin, KEY_GROUP)
                    before = top[...]
                    now = jnp.maximum(before, most)
                    update = weigh(begin, KEY_GROUP, tiles, now)
                    shrink = jnp.exp2(before - now)
                    total[:, :HEAD_DIM] = total[:, :HEAD_DIM] * shrink + update[:, :HEAD_DIM]
                    total[:, HEAD_DIM:] = total[:, HEAD_DIM:] * shrink + update[:, HEAD_DIM:]
                    top[...] = now
                    return carry

                lax.fori_loop(low // KEY_GROUP, (high + KEY_GROUP - 1) // KEY_GROUP, key_block, 0)
                store(offset, total)

            need = high - low
            floor = 0
            for count in WINDOWS:
                pl.when((need > floor) & (need <= count))(functools.partial(window, count))
                floor = count

            @pl.when(need > floor)
            def _():
                if all_rows == KEY_GROUP:
                    window(KEY_GROUP)
                else:
                    for offset in range(0, QUERY_BLOCK, sub):
                        long(offset)

            return carry

        lax.fori_loop(0, own_rows // QUERY_BLOCK, query_block, 0)
        copies = [
            pltpu.make_async_copy(result.at[at(colour, side, False)], outs[colour], out_sems.at[colour])
            for colour in range(colours)
        ]
        for copy in copies:
            copy.start()
        for copy in copies:
            copy.wait()


def attend(lengths, pieces, swapped, heads):
    rows = pieces[0].shape[1]
    colours = len(pieces)
    own = colours * rows
    return pl.pallas_call(
        functools.partial(attend_kernel, colours, heads),
        in_specs=[smem_spec()] + [any_spec()] * (2 * colours),
        out_specs=[any_spec()] * colours,
        out_shape=[jax.ShapeDtypeStruct((rows, HEAD_DIM), jnp.bfloat16)] * colours,
        scratch_shapes=[
            pltpu.VMEM((own, 2 * HEAD_DIM), jnp.bfloat16),
            pltpu.VMEM((2 * own, 2 * HEAD_DIM), jnp.bfloat16),
            pltpu.VMEM((2 * own, 2 * HEAD_DIM), jnp.bfloat16),
            pltpu.VMEM((own, HEAD_DIM), jnp.bfloat16),
            pltpu.VMEM((QUERY_BLOCK // PARTS, HEAD_DIM), jnp.float32),
            pltpu.VMEM((QUERY_BLOCK // PARTS, 2 * HEAD_DIM), jnp.float32),
            pltpu.SemaphoreType.DMA((5 * colours,)),
            pltpu.SemaphoreType.DMA((colours,)),
        ],
        compiler_params=pltpu.CompilerParams(vmem_limit_bytes=VMEM_LIMIT),
    )(lengths, *pieces, *swapped)


def part_kernel(colours, *refs):
    pieces, (keep, give, sems) = refs[:colours], refs[colours:]
    heads, rows, _ = keep.shape
    slot, x = place_of(colours)

    def each_copy(act):
        for head in range(heads):
            for number, (target, position) in enumerate(((give, 1 - x), (keep, x))):
                here = pl.ds(pl.multiple_of(position * rows, 64), rows)
                for colour in range(colours):
                    @pl.when((slot ^ colour) == head)
                    def _():
                        source = pieces[colour].at[here]
                        act(pltpu.make_async_copy(source, target.at[head], sems.at[2 * head + number]))

    each_copy(lambda copy: copy.start())
    each_copy(lambda copy: copy.wait())


def part(pieces, heads):
    rows = pieces[0].shape[0] // 2
    shape = jax.ShapeDtypeStruct((heads, rows, HEAD_DIM), jnp.bfloat16)
    return pl.pallas_call(
        functools.partial(part_kernel, len(pieces)),
        in_specs=[any_spec()] * len(pieces),
        out_specs=[any_spec()] * 2,
        out_shape=[shape, shape],
        scratch_shapes=[pltpu.SemaphoreType.DMA((2 * heads,))],
        compiler_params=pltpu.CompilerParams(vmem_limit_bytes=VMEM_LIMIT),
    )(*pieces)


def multiply(attended, weight, out, where):
    share = out.shape[1]
    columns = pl.ds(pl.multiple_of(where * share, 128), share)
    out[...] = jnp.dot(attended[...], weight[:, columns], preferred_element_type=jnp.float32).astype(out.dtype)


def own_kernel(attended, weight, mine):
    multiply(attended, weight, mine, lax.axis_index("tp"))


def own_part(attended, w_out):
    rows, width = attended.shape[0], w_out.shape[1]
    return pl.pallas_call(
        own_kernel,
        in_specs=[vmem_spec()] * 2,
        out_specs=vmem_spec(),
        out_shape=jax.ShapeDtypeStruct((rows, width // 2), jnp.float32),
        compiler_params=pltpu.CompilerParams(vmem_limit_bytes=VMEM_LIMIT),
        cost_estimate=pl.CostEstimate(flops=rows * width * w_out.shape[0], bytes_accessed=2**20, transcendentals=0),
    )(attended, w_out)


def combine_kernel(keep_ref, got_ref, weight, theirs, attended, sems):
    heads = keep_ref.shape[0]
    core = lax.axis_index("tp")
    x = lax.rem(lax.axis_index("req"), 2)
    copies = []
    for head in range(heads):
        for source, which in ((keep_ref, x), (got_ref, 1 - x)):
            columns = pl.ds(pl.multiple_of((which * heads + head) * HEAD_DIM, HEAD_DIM), HEAD_DIM)
            copies.append(pltpu.make_async_copy(source.at[head], attended.at[:, columns], sems.at[len(copies)]))
            copies[-1].start()
    for copy in copies:
        copy.wait()
    multiply(attended, weight, theirs, 1 - core)


def combine(keep, got, w_out):
    heads, rows, _ = keep.shape
    depth, width = w_out.shape
    return pl.pallas_call(
        combine_kernel,
        in_specs=[any_spec()] * 2 + [vmem_spec()],
        out_specs=[vmem_spec(), vmem_spec()],
        out_shape=[
            jax.ShapeDtypeStruct((rows, width // 2), jnp.bfloat16),
            jax.ShapeDtypeStruct((rows, depth), jnp.bfloat16),
        ],
        scratch_shapes=[
            pltpu.SemaphoreType.DMA((2 * heads,)),
        ],
        compiler_params=pltpu.CompilerParams(vmem_limit_bytes=VMEM_LIMIT),
    )(keep, got, w_out)


def finish_kernel(timestep_ref, mine, theirs, tokens, gate_ref, velocity, stepped):
    step_value = jnp.full((1, 128), timestep_ref[0], jnp.int32).astype(jnp.float32)
    delta = (noise_level(step_value - 1.0) - noise_level(step_value))[:, :1]
    branch = gate_ref[...] * (mine[...] + theirs[...].astype(jnp.float32))
    velocity[...] = branch.astype(jnp.bfloat16)
    stepped[...] = (tokens[...].astype(jnp.float32) + delta * branch).astype(jnp.bfloat16)


def finish(timestep, mine, theirs, tokens, gate):
    shape = jax.ShapeDtypeStruct(tokens.shape, jnp.bfloat16)
    return pl.pallas_call(
        finish_kernel,
        in_specs=[smem_spec()] + [vmem_spec()] * 4,
        out_specs=[vmem_spec(), vmem_spec()],
        out_shape=[shape, shape],
        compiler_params=pltpu.CompilerParams(vmem_limit_bytes=VMEM_LIMIT),
    )(timestep, mine, theirs, tokens, gate)


def make(mesh):
    chips = mesh.shape["req"]
    colours = chips // 4
    swap = [(0, 1), (1, 0)]
    cross = [(chip, chip ^ 1) for chip in range(chips)]

    def on_device(tokens, video_lengths, timestep, time_weight, block_mod, w_query, w_key, w_value, w_out):
        heads = w_query.shape[1] // HEAD_DIM // 2
        routes = [pairs_out(chips, heads, colour) for colour in range(colours)]
        near = lax.ppermute(tokens, "req", cross)
        other = lax.ppermute(tokens, "tp", swap)
        half_freq = time_weight.shape[0] // 2
        time_value = jnp.broadcast_to(timestep, (half_freq,)).astype(jnp.float32)
        sigma = noise_level(time_value)
        frequency = jnp.exp(-math.log(10000.0) * jnp.arange(half_freq, dtype=jnp.float32) / half_freq)
        angle = 1000.0 * sigma * frequency
        act = jax.nn.silu(jnp.concatenate([jnp.cos(angle), jnp.sin(angle)]))[None, :]
        mine, mod, gate = project(act, block_mod, tokens, other, time_weight, w_query, w_key, w_value)
        near, mine, mod, gate = lax.optimization_barrier((near, mine, mod, gate))
        far = lax.ppermute(near, "tp", swap)
        sent = project_shared(near, far, mod, mine, w_query, w_key, w_value, colours)
        got = [lax.ppermute(piece, ("req", "tp"), route) for piece, route in zip(sent, routes)]
        swapped = [lax.ppermute(piece, "tp", swap) for piece in got]
        done = attend(video_lengths, got, swapped, heads)
        back = [
            lax.ppermute(piece, ("req", "tp"), [(b, a) for a, b in route]) for piece, route in zip(done, routes)
        ]
        keep, give = part(back, heads)
        theirs, attended = combine(keep, lax.ppermute(give, "req", cross), w_out)
        theirs = lax.ppermute(theirs, "tp", swap)
        mine = own_part(attended, w_out)
        velocity, stepped = finish(timestep, mine, theirs, tokens, gate)
        return (velocity, stepped)

    return on_device


def solution(mesh):
    return jax.shard_map(
        make(mesh),
        mesh=mesh,
        in_specs=(
            P("req", "tp"), P(), P(), P(), P(), P(None, "tp"), P(None, "tp"), P(None, "tp"), P("tp", None),
        ),
        out_specs=(P("req", "tp"), P("req", "tp")),
        check_vma=False,
    )
```
